32 devices in a mesh: half: 2 (over core), dp: 4 (over z), row: 4 (over y, x).
Axes of the slice: x: 2, y: 2, z: 4, core: 2. Of those that a mesh axis runs over, the one named last changes fastest.
Arguments:
- features: bfloat16 [128, 4, 4, 1536], P(('half', 'dp'), None, None, 'row'), may hold values from -20 to 20
- noise: float32 [128, 20], P(('half', 'dp')), may hold values from -3 to 3
- labels: int32 [128], P(('half', 'dp')), may hold values from 0 to 999
- counted: int32 [128], P(('half', 'dp')), may hold values from 0 to 1, as said below
- disc_first: bfloat16 [27, 96], replicated, may hold values from -1.25 to 1.25
- disc_second: bfloat16 [864, 96], replicated, may hold values from -0.21875 to 0.21875
- disc_skip: bfloat16 [3, 96], replicated, may hold values from -3.5 to 3.5
- disc_head: float32 [96], replicated, may hold values from -0.15625 to 0.15625
- disc_table: float32 [1000, 96], replicated, may hold values from -0.15625 to 0.15625
- conv_first: float32 [13824, 768], P(('half', 'dp'), 'row'), may hold values from -0.0546875 to 0.0546875
- conv_second: float32 [6912, 768], P(('half', 'dp'), 'row'), may hold values from -0.078125 to 0.078125
- conv_skip: float32 [1536, 768], P(('half', 'dp'), 'row'), may hold values from -0.15625 to 0.15625
- momentum_first: float32 [13824, 768], P(('half', 'dp'), 'row')
- momentum_second: float32 [6912, 768], P(('half', 'dp'), 'row')
- momentum_skip: float32 [1536, 768], P(('half', 'dp'), 'row')
- class_table: float32 [1000, 128], replicated, may hold values from -1.2 to 1.2
- table_mean: float32 [1000, 128], replicated
- table_square: float32 [1000, 128], replicated
- norm_first: float32 [148, 2, 1536], P(None, None, 'row'), may hold values from -0.5 to 0.5
- first_mean: float32 [148, 2, 1536], P(None, None, 'row')
- first_square: float32 [148, 2, 1536], P(None, None, 'row')
- norm_second: float32 [148, 2, 768], P(None, None, 'row'), may hold values from -0.5 to 0.5
- second_mean: float32 [148, 2, 768], P(None, None, 'row')
- second_square: float32 [148, 2, 768], P(None, None, 'row')
- colour_conv: float32 [9, 768, 3], P(None, 'row'), may hold values from -0.078125 to 0.078125
- colour_mean: float32 [9, 768, 3], P(None, 'row')
- colour_square: float32 [9, 768, 3], P(None, 'row')
Outputs:
- loss_sum: float32 [], replicated
- fake_count: float32 [], replicated
- conv_first_new: float32 [13824, 768], P(('half', 'dp'), 'row')
- conv_second_new: float32 [6912, 768], P(('half', 'dp'), 'row')
- conv_skip_new: float32 [1536, 768], P(('half', 'dp'), 'row')
- momentum_first_new: float32 [13824, 768], P(('half', 'dp'), 'row')
- momentum_second_new: float32 [6912, 768], P(('half', 'dp'), 'row')
- momentum_skip_new: float32 [1536, 768], P(('half', 'dp'), 'row')
- class_table_new: float32 [1000, 128], replicated
- table_mean_new: float32 [1000, 128], replicated
- table_square_new: float32 [1000, 128], replicated
- norm_first_new: float32 [148, 2, 1536], P(None, None, 'row')
- first_mean_new: float32 [148, 2, 1536], P(None, None, 'row')
- first_square_new: float32 [148, 2, 1536], P(None, None, 'row')
- norm_second_new: float32 [148, 2, 768], P(None, None, 'row')
- second_mean_new: float32 [148, 2, 768], P(None, None, 'row')
- second_square_new: float32 [148, 2, 768], P(None, None, 'row')
- colour_conv_new: float32 [9, 768, 3], P(None, 'row')
- colour_mean_new: float32 [9, 768, 3], P(None, 'row')
- colour_square_new: float32 [9, 768, 3], P(None, 'row')
The draws below stay inside these ranges and needn't reach their ends.
Inputs may be any that keep to these rules, and one draw needn't show every extreme that they name: `counted`: every image whose index is a multiple of 16 counts.
All inputs are finite; a program needn't handle non-finite values.
Results may differ from the reference program's by a relative error of at most 0.0085.
Values may be sent and summed in bfloat16 or wider, within the bound.
No kernel may reach another device: no remote copies, remote signals or barrier semaphores. Data moves between devices by JAX's collectives and lax.ppermute only.
A program may use at most 256 MiB of HBM per device.

```python
import math
import jax
import jax.numpy as jnp
from jax import lax

C1 = 1536
C2 = 768
EMB = 128
ZDIM = 20
NCLS = 1000
DCH = 96
IMG_DEV = 16
MICRO = 2
NS_ITERS = 5
STEP = 10
BATCH = 128
IMG_MB = 8
COND = 148
N_HALF = 2
N_DP = 4


def scaled_normal(key, extent, size_scale):
    return size_scale * jax.random.normal(key, extent, jnp.float32)


def scaled_square(key, extent, size_scale):
    spread = jnp.exp(jax.random.uniform(key, extent, jnp.float32, 0.0, 1.386))
    return 0.0526 * size_scale * size_scale * spread


def draw_features(key, part):
    key = jax.random.fold_in(key, 11)
    devices = BATCH // IMG_DEV
    position = (jnp.arange(BATCH) // IMG_DEV).astype(jnp.float32) / max(devices - 1, 1)
    subkeys = jax.random.split(key, 1)
    normal_part = jax.random.normal(subkeys[0], (BATCH, 4, 4, C1), jnp.float32)
    values = normal_part * (1.0 + 2.0 * position)[:, None, None, None]
    return jnp.clip(values, -20.0, 20.0).astype(jnp.bfloat16)


def draw_counted(key, part):
    key = jax.random.fold_in(key, 12)
    devices = BATCH // IMG_DEV
    device = jnp.arange(BATCH) // IMG_DEV
    threshold = 25 + 50 * device // max(devices - 1, 1)
    lottery = jax.random.randint(key, (BATCH,), 0, 100)
    chosen = (lottery < threshold) | (jnp.arange(BATCH) % IMG_DEV == 0)
    return jnp.where(chosen, 1, 0).astype(jnp.int32)


def draw_momentum_first(key, part):
    key = jax.random.fold_in(key, 21)
    return scaled_normal(key, (9 * C1, C2), 0.07 / math.sqrt(BATCH))


def draw_momentum_second(key, part):
    key = jax.random.fold_in(key, 22)
    return scaled_normal(key, (9 * C2, C2), 0.07 / math.sqrt(BATCH))


def draw_momentum_skip(key, part):
    key = jax.random.fold_in(key, 23)
    return scaled_normal(key, (C1, C2), 0.07 / math.sqrt(BATCH))


def draw_table_mean(key, part):
    key = jax.random.fold_in(key, 31)
    return scaled_normal(key, (NCLS, EMB), 0.11 * 0.2 / BATCH)


def draw_table_square(key, part):
    key = jax.random.fold_in(key, 32)
    return scaled_square(key, (NCLS, EMB), 0.2 / BATCH)


def draw_first_mean(key, part):
    key = jax.random.fold_in(key, 33)
    return scaled_normal(key, (COND, 2, C1), 0.11 * 0.02 / math.sqrt(BATCH))


def draw_first_square(key, part):
    key = jax.random.fold_in(key, 34)
    return scaled_square(key, (COND, 2, C1), 0.005 / math.sqrt(BATCH))


def draw_second_mean(key, part):
    key = jax.random.fold_in(key, 35)
    return scaled_normal(key, (COND, 2, C2), 0.11 * 0.02 / math.sqrt(BATCH))


def draw_second_square(key, part):
    key = jax.random.fold_in(key, 36)
    return scaled_square(key, (COND, 2, C2), 0.02 / math.sqrt(BATCH))


def draw_colour_mean(key, part):
    key = jax.random.fold_in(key, 37)
    return scaled_normal(key, (9, C2, 3), 0.11 * 0.8 / math.sqrt(BATCH))


def draw_colour_square(key, part):
    key = jax.random.fold_in(key, 38)
    return scaled_square(key, (9, C2, 3), 0.8 / math.sqrt(BATCH))


def touch_ends(drawn, stream_key, low, high):
    dims = drawn.shape
    spot = [jax.random.randint(jax.random.fold_in(stream_key, axis), (), 0, dims[axis]) for axis in range(len(dims))]
    drawn = drawn.at[tuple(spot)].set(low)
    longest = dims.index(max(dims))
    spot[longest] = (spot[longest] + 1) % dims[longest]
    return drawn.at[tuple(spot)].set(high)


def steps_of(key, shape, cuts, least, top_value):
    def one(dim, blocks):
        heights = jax.random.uniform(jax.random.fold_in(jax.random.fold_in(key, 6), dim), (blocks,), jnp.float32, least / len(cuts), top_value / len(cuts))
        return jnp.repeat(jnp.exp(heights), shape[dim] // blocks).reshape((-1,) + (1,) * (len(shape) - dim - 1))

    level = one(*cuts[0])
    for cut in cuts[1:]:
        level = level * one(*cut)
    return level


def centred(stream_key, shape, deviation, most, cuts=(), kind=jnp.bfloat16):
    array = jax.random.normal(stream_key, shape, jnp.float32) * deviation
    if len(cuts) > 0:
        array = steps_of(stream_key, shape, cuts, -0.22, 0.18) * array
    return jnp.clip(array, min=-most, max=most).astype(kind)


def setup_inputs(seed: int = 0) -> dict:
    key_of = jax.random.split(jax.random.key(seed), 28)
    return {
        "features": draw_features(jax.random.fold_in(key_of[27], 71), 0),
        "noise": centred(key_of[1], (BATCH, ZDIM), 0.5, 3.0, ((0, 8),), jnp.float32),
        "labels": touch_ends(jax.random.randint(key_of[2], (BATCH,), 0, NCLS), jax.random.fold_in(key_of[2], 1), 0, NCLS - 1).astype(jnp.int32),
        "counted": draw_counted(jax.random.fold_in(key_of[27], 71), 0),
        "disc_first": centred(key_of[4], (27, DCH), 27 ** -0.5, 1.25),
        "disc_second": centred(key_of[5], (9 * DCH, DCH), (9 * DCH) ** -0.5, 0.21875),
        "disc_skip": centred(key_of[6], (3, DCH), 3 ** -0.5, 3.5),
        "disc_head": centred(key_of[7], (DCH,), (16 * DCH) ** -0.5, 0.15625, (), jnp.float32),
        "disc_table": centred(key_of[8], (NCLS, DCH), (16 * DCH) ** -0.5, 0.15625, (), jnp.float32),
        "conv_first": centred(key_of[9], (9 * C1, C2), (9 * C1) ** -0.5, 0.0546875, ((0, 8), (1, 4)), jnp.float32),
        "conv_second": centred(key_of[10], (9 * C2, C2), (9 * C2) ** -0.5, 0.078125, ((0, 8), (1, 4)), jnp.float32),
        "conv_skip": centred(key_of[11], (C1, C2), C1 ** -0.5, 0.15625, ((0, 8), (1, 4)), jnp.float32),
        "momentum_first": draw_momentum_first(jax.random.fold_in(key_of[27], 71), 0),
        "momentum_second": draw_momentum_second(jax.random.fold_in(key_of[27], 71), 0),
        "momentum_skip": draw_momentum_skip(jax.random.fold_in(key_of[27], 71), 0),
        "class_table": centred(key_of[15], (NCLS, EMB), 0.2, 1.2, (), jnp.float32),
        "table_mean": draw_table_mean(jax.random.fold_in(key_of[27], 71), 0),
        "table_square": draw_table_square(jax.random.fold_in(key_of[27], 71), 0),
        "norm_first": centred(key_of[18], (COND, 2, C1), COND ** -0.5, 0.5, ((2, 4),), jnp.float32),
        "first_mean": draw_first_mean(jax.random.fold_in(key_of[27], 71), 0),
        "first_square": draw_first_square(jax.random.fold_in(key_of[27], 71), 0),
        "norm_second": centred(key_of[21], (COND, 2, C2), COND ** -0.5, 0.5, ((2, 4),), jnp.float32),
        "second_mean": draw_second_mean(jax.random.fold_in(key_of[27], 71), 0),
        "second_square": draw_second_square(jax.random.fold_in(key_of[27], 71), 0),
        "colour_conv": centred(key_of[24], (9, C2, 3), (9 * C2) ** -0.5, 0.078125, ((1, 4),), jnp.float32),
        "colour_mean": draw_colour_mean(jax.random.fold_in(key_of[27], 71), 0),
        "colour_square": draw_colour_square(jax.random.fold_in(key_of[27], 71), 0),
    }


@jax.custom_vjp
def low(v):
    return lax.optimization_barrier(v.astype(jnp.bfloat16)).astype(jnp.float32)

@jax.custom_vjp
def low_back(v):
    return v

def low_keep(v):
    return (low(v), None)

def low_pass(kept, grad):
    return (grad,)

def back_keep(v):
    return (v, None)

def back_low(kept, grad):
    return (low(grad),)
low.defvjp(low_keep, low_pass)
low_back.defvjp(back_keep, back_low)
highest = lax.Precision.HIGHEST
BN_EPS = 1e-05
NEWTON_EPSILON = 1e-07
NS_COEF = (3.4445, -4.775, 2.0315)
MOMENTUM = 0.9
MUON_RATE = 0.03
DECAY = 0.01
BETA_ONE = 0.9
BETA_TWO = 0.95
ADAM_EPS = 1e-08
ADAM_RATE = 0.05
COLOUR_RATE = 0.01

def patches_of(values):
    padded = jnp.pad(values, ((0, 0), (1, 1), (1, 1), (0, 0)))
    rows_in, cols_in = (values.shape[1], values.shape[2])
    return jnp.concatenate([padded[:, row_shift:row_shift + rows_in, col_shift:col_shift + cols_in, :] for row_shift in range(3) for col_shift in range(3)], axis=-1)

def conv_three(values, weight):
    return jnp.einsum('bhwk,ko->bhwo', patches_of(values), weight, precision=highest)

def upsample(values):
    return jnp.repeat(jnp.repeat(values, 2, axis=1), 2, axis=2)

def pooled(values):
    shaped = values.reshape(values.shape[0], values.shape[1] // 2, 2, values.shape[2] // 2, 2, values.shape[3])
    return lax.optimization_barrier(jnp.mean(shaped, axis=(2, 4)))

def normalize(values):
    centre = lax.optimization_barrier(jnp.mean(values, axis=(0, 1, 2)))
    square = lax.optimization_barrier(jnp.mean(values * values, axis=(0, 1, 2)))
    return (values - centre) * lax.rsqrt(square - centre * centre + BN_EPS)

def modulate(normed, mods):
    return normed * (1.0 + mods[:, 0])[:, None, None, :] + mods[:, 1][:, None, None, :]

def micro_loss(inputs, noise, labels, counted, weight_one, weight_two, weight_skip, colour_flat, class_table, norm_first, norm_second, disc):
    disc_first, disc_second, disc_skip, disc_head, disc_table = disc
    onehot = (labels[:, None] == jnp.arange(NCLS)[None, :]).astype(jnp.float32)
    cond = jnp.concatenate([jnp.dot(onehot, class_table, precision=highest), noise], axis=1)
    mods_one = jnp.einsum('bk,kgc->bgc', cond, norm_first, precision=highest)
    mods_two = jnp.einsum('bk,kgc->bgc', cond, norm_second, precision=highest)
    first = low(jax.nn.silu(modulate(normalize(inputs), mods_one)))
    hidden = low_back(conv_three(upsample(first), weight_one))
    second = low(jax.nn.silu(modulate(normalize(hidden), mods_two)))
    skipped = jnp.einsum('bhwc,co->bhwo', upsample(inputs), weight_skip, precision=highest)
    summed = low_back(conv_three(second, weight_two) + skipped)
    active = low(jax.nn.silu(summed))
    shade = jnp.tanh(low_back(conv_three(active, colour_flat)))
    picture = low(shade)
    front = low(jax.nn.silu(low_back(conv_three(picture, disc_first))))
    merged = pooled(conv_three(front, disc_second))
    merged = low_back(merged + jnp.einsum('bhwc,co->bhwo', pooled(picture), disc_skip, precision=highest))
    feature = lax.optimization_barrier(jnp.sum(jax.nn.silu(merged), axis=(1, 2)))
    score = jnp.dot(feature, disc_head, precision=highest)
    score = score + lax.optimization_barrier(jnp.sum(feature * jnp.dot(onehot, disc_table, precision=highest), axis=1))
    return -jnp.sum(counted.astype(jnp.float32) * score)

def micro_part(values, micro_index):
    groups = N_HALF * N_DP
    shaped = values.reshape((groups, MICRO, IMG_MB) + values.shape[1:])
    return shaped[:, micro_index].reshape((groups * IMG_MB,) + values.shape[1:])

def orthogonal(update_matrix):
    gram_product = jnp.dot(update_matrix.T, update_matrix, precision=highest)
    norm_scale = lax.rsqrt(jnp.trace(gram_product) + NEWTON_EPSILON)
    current = update_matrix * norm_scale
    gram_product = gram_product * norm_scale * norm_scale
    identity = jnp.eye(update_matrix.shape[1], dtype=jnp.float32)
    for iteration in range(NS_ITERS):
        if iteration > 0:
            gram_product = jnp.dot(current.T, current, precision=highest)
        mapping = NS_COEF[0] * identity + NS_COEF[1] * gram_product + NS_COEF[2] * jnp.dot(gram_product, gram_product, precision=highest)
        current = jnp.dot(current, mapping, precision=highest)
    return current

def adam_update(weight, gradient, mean_old, square_old, rate):
    mean_new = BETA_ONE * mean_old + (1.0 - BETA_ONE) * gradient
    square_new = BETA_TWO * square_old + (1.0 - BETA_TWO) * gradient * gradient
    ratio = mean_new / (1.0 - BETA_ONE ** STEP) / (jnp.sqrt(square_new / (1.0 - BETA_TWO ** STEP)) + ADAM_EPS)
    return (weight - rate * (ratio + DECAY * weight), mean_new, square_new)

def reference(features, noise, labels, counted, disc_first, disc_second, disc_skip, disc_head, disc_table, conv_first, conv_second, conv_skip, momentum_first, momentum_second, momentum_skip, class_table, table_mean, table_square, norm_first, first_mean, first_square, norm_second, second_mean, second_square, colour_conv, colour_mean, colour_square):
    inputs_all = features.astype(jnp.float32)
    disc = (disc_first.astype(jnp.float32), disc_second.astype(jnp.float32), disc_skip.astype(jnp.float32), disc_head, disc_table)

    def whole_loss(conv_one, conv_two, conv_sk, table, norm_one, norm_two, colour):
        weight_one = low(conv_one)
        weight_two = low(conv_two)
        weight_skip = low(conv_sk)
        colour_flat = low(colour.reshape(-1, 3))
        running = jnp.zeros((), jnp.float32)
        for micro_index in range(MICRO):
            running = running + micro_loss(micro_part(inputs_all, micro_index), micro_part(noise, micro_index), micro_part(labels, micro_index), micro_part(counted, micro_index), weight_one, weight_two, weight_skip, colour_flat, table, norm_one, norm_two, disc)
        return running
    loss_sum, pullback = jax.vjp(whole_loss, conv_first, conv_second, conv_skip, class_table, norm_first, norm_second, colour_conv)
    gradients = pullback(jnp.ones((), jnp.float32))
    fake_count = jnp.sum(counted).astype(jnp.float32)
    gradients = tuple((gradient / fake_count for gradient in gradients))
    outs_muon = []
    for weight, moment, gradient in ((conv_first, momentum_first, gradients[0]), (conv_second, momentum_second, gradients[1]), (conv_skip, momentum_skip, gradients[2])):
        moment_new = MOMENTUM * moment + gradient
        factor = 0.2 * math.sqrt(max(weight.shape[0], weight.shape[1]))
        weight_new = weight - MUON_RATE * (factor * orthogonal(moment_new) + DECAY * weight)
        outs_muon.append((weight_new, moment_new))
    table_new = adam_update(class_table, gradients[3], table_mean, table_square, ADAM_RATE)
    first_new = adam_update(norm_first, gradients[4], first_mean, first_square, ADAM_RATE)
    second_new = adam_update(norm_second, gradients[5], second_mean, second_square, ADAM_RATE)
    colour_new = adam_update(colour_conv, gradients[6], colour_mean, colour_square, COLOUR_RATE)
    return (loss_sum, fake_count, outs_muon[0][0], outs_muon[1][0], outs_muon[2][0], outs_muon[0][1], outs_muon[1][1], outs_muon[2][1], table_new[0], table_new[1], table_new[2], first_new[0], first_new[1], first_new[2], second_new[0], second_new[1], second_new[2], colour_new[0], colour_new[1], colour_new[2])
```

```python
import functools
import math

import jax
import jax.numpy as jnp
from jax import lax
from jax.experimental import pallas as pl
from jax.experimental.pallas import tpu as pltpu
from jax.sharding import PartitionSpec as P

EMB = 128
NCLS = 1000
MICRO = 2
NS_ITERS = 5
STEP = 10

highest = lax.Precision.HIGHEST
high = lax.Precision.HIGH
bf16 = jnp.bfloat16
f32 = jnp.float32
BN_EPS = 1e-05
NEWTON_EPSILON = 1e-07
NS_COEF = (3.4445, -4.775, 2.0315)
MOMENTUM = 0.9
MUON_RATE = 0.03
DECAY = 0.01
BETA_ONE = 0.9
BETA_TWO = 0.95
ADAM_EPS = 1e-08
ADAM_RATE = 0.05
COLOUR_RATE = 0.01
PAD = 8
VMEM_BYTES = 48 * 1024 * 1024


def kernel_params():
    return pltpu.CompilerParams(vmem_limit_bytes=VMEM_BYTES)


def whole(shape):
    return pl.BlockSpec(shape, lambda t, r: (0,) * len(shape))


def silu_slope(values):
    sigmoid_value = jax.nn.sigmoid(values)
    return sigmoid_value * (1.0 + values * (1.0 - sigmoid_value))


def contract_last(left, right):
    return lax.dot_general(left, right, (((1,), (1,)), ((), ())), preferred_element_type=f32)


def times(left, right):
    return jnp.dot(left, right, preferred_element_type=f32)


def axis_swap(value, axis, k):
    n = lax.axis_size(axis)
    return lax.ppermute(value, axis, [(i, i ^ k) for i in range(n)])


def axis_shift(value, axis, k):
    n = lax.axis_size(axis)
    return lax.ppermute(value, axis, [(i, (i + k) % n) for i in range(n)])


def row_gather(value):
    return [value] + [axis_swap(value, "row", k) for k in range(1, lax.axis_size("row"))]


def row_sum(value):
    return sum(row_gather(value))


def row_scatter(pieces):
    arrived = [axis_swap(pieces[k], "row", k) for k in range(1, len(pieces))]
    total = pieces[0].astype(f32)
    for piece in arrived:
        total = total + piece.astype(f32)
    return total


def group_sum(value):
    value = value + axis_swap(value, "half", 1)
    return sum([value] + [axis_shift(value, "dp", k) for k in range(1, lax.axis_size("dp"))])


def group_pile(value):
    parts = [value] + [axis_shift(value, "dp", k) for k in range(1, lax.axis_size("dp"))]
    return jnp.concatenate(parts + [axis_swap(part, "half", 1) for part in parts], axis=0)


def group_gather(value):
    n = lax.axis_size("dp")
    h, z = lax.axis_index("half"), lax.axis_index("dp")
    rows = value.shape[0]
    full = jnp.zeros((2 * n * rows,) + value.shape[1:], value.dtype)
    for k in range(n):
        part = value if k == 0 else axis_shift(value, "dp", k)
        other = axis_swap(part, "half", 1)
        place = lax.rem(z + n - k, n)
        full = lax.dynamic_update_slice_in_dim(full, part, (h * n + place) * rows, 0)
        full = lax.dynamic_update_slice_in_dim(full, other, ((1 - h) * n + place) * rows, 0)
    return full


def group_scatter(value):
    n = lax.axis_size("dp")
    h, z = lax.axis_index("half"), lax.axis_index("dp")
    halves = value.reshape((2, n, value.shape[0] // (2 * n)) + value.shape[1:])
    kept = lax.dynamic_index_in_dim(halves, h, 0, keepdims=False)
    sent = lax.dynamic_index_in_dim(halves, 1 - h, 0, keepdims=False)
    kept = kept.astype(f32) + axis_swap(sent, "half", 1).astype(f32)
    wire = kept.astype(value.dtype)
    total = lax.dynamic_index_in_dim(kept, z, 0, keepdims=False)
    for k in range(1, n):
        block = lax.dynamic_index_in_dim(wire, lax.rem(z + k, n), 0, keepdims=False)
        total = total + axis_shift(block, "dp", k).astype(f32)
    return total


def raise_two(values):
    h, w, n, c = values.shape
    wide = jnp.stack([values, values], axis=2).reshape(h, 2 * w, n, c)
    return jnp.stack([wide, wide], axis=1).reshape(2 * h, 2 * w, n, c)


def sum_two(values):
    h, w, n, c = values.shape
    shaped = values.reshape(h // 2, 2, w // 2, 2, n, c)
    return (shaped[:, 0, :, 0] + shaped[:, 0, :, 1]) + (shaped[:, 1, :, 0] + shaped[:, 1, :, 1])


def owned_rows(row_ref, k, size):
    return pl.ds(pl.multiple_of(lax.bitwise_xor(row_ref[0], k) * size, size), size)


def flat(values):
    return values.reshape(-1, values.shape[-1])


def conv_one_kernel(row_ref, *refs):
    blocks, (w_ref, out_ref, sums_ref, acc_ref) = refs[:-4], refs[-4:]
    h2, w2, n, c = out_ref.shape
    t = pl.program_id(0)
    dy, dx = lax.div(t, 3), lax.rem(t, 3)

    @pl.when(t == 0)
    def _():
        acc_ref[...] = jnp.zeros_like(acc_ref)

    product = sum(
        times(x_ref[...], w_ref[0, owned_rows(row_ref, k, x_ref.shape[1]), :])
        for k, x_ref in enumerate(blocks)
    )
    raised = raise_two(product.reshape(h2 // 2, w2 // 2, n, c))
    acc_ref[pl.ds(2 - dy, h2), pl.ds(2 - dx, w2)] += raised

    @pl.when(t == 8)
    def _():
        hidden = acc_ref[1 : h2 + 1, 1 : w2 + 1]
        out_ref[...] = hidden
        shaped = hidden.reshape(h2 * w2, n, c)
        first, second = jnp.sum(shaped, axis=0), jnp.sum(shaped * shaped, axis=0)
        m = n // MICRO
        for i in range(MICRO):
            sums_ref[i : i + 1, :] = jnp.sum(first[i * m : (i + 1) * m], axis=0, keepdims=True)
            sums_ref[MICRO + i : MICRO + i + 1, :] = jnp.sum(
                second[i * m : (i + 1) * m], axis=0, keepdims=True
            )


def conv_one(row, blocks, weight, pixels):
    h, w, n = pixels
    c = weight.shape[-1]
    return pl.pallas_call(
        conv_one_kernel,
        out_shape=(
            jax.ShapeDtypeStruct((2 * h, 2 * w, n, c), f32),
            jax.ShapeDtypeStruct((2 * MICRO, c), f32),
        ),
        grid_spec=pltpu.PrefetchScalarGridSpec(
            num_scalar_prefetch=1,
            grid=(9,),
            in_specs=[whole(b.shape) for b in blocks]
            + [pl.BlockSpec((1,) + weight.shape[1:], lambda t, r: (t, 0, 0))],
            out_specs=(whole((2 * h, 2 * w, n, c)), whole((2 * MICRO, c))),
            scratch_shapes=[pltpu.VMEM((2 * h + 2, 2 * w + 2, n, c), f32)],
        ),
        compiler_params=kernel_params(),
        name="conv_one",
    )(row, *blocks, weight)


def conv_two_kernel(count, row_ref, *refs):
    blocks, raws = refs[:count], refs[count : 2 * count]
    w_ref, skip_ref, colour_ref, sum_ref, act_ref, pic_ref, pad_ref, apad_ref = refs[2 * count :]
    h2, w2, n, c = sum_ref.shape
    t = pl.program_id(0)
    dy, dx = lax.div(t, 3), lax.rem(t, 3)

    @pl.when(t == 0)
    def _():
        pad_ref[...] = jnp.zeros_like(pad_ref)
        for k in range(count):
            pad_ref[k, 1 : h2 + 1, 1 : w2 + 1] = blocks[k][...]
        skipped = sum(
            times(x_ref[...], skip_ref[owned_rows(row_ref, k, x_ref.shape[1]), :])
            for k, x_ref in enumerate(raws)
        )
        sum_ref[...] = raise_two(skipped.reshape(h2 // 2, w2 // 2, n, c))

    product = sum(
        times(
            flat(pad_ref[k, pl.ds(dy, h2), pl.ds(dx, w2)]), w_ref[0, owned_rows(row_ref, k, c), :]
        )
        for k in range(count)
    )
    sum_ref[...] += product.reshape(sum_ref.shape)

    @pl.when(t == 8)
    def _():
        active = jax.nn.silu(sum_ref[...]).astype(bf16)
        act_ref[...] = active
        apad_ref[...] = jnp.zeros_like(apad_ref)
        apad_ref[1 : h2 + 1, 1 : w2 + 1] = active
        picture = jnp.zeros(pic_ref.shape, f32)
        for tap in range(9):
            y, x = divmod(tap, 3)
            picture = picture + contract_last(
                colour_ref[tap], flat(apad_ref[y : y + h2, x : x + w2])
            )
        pic_ref[...] = picture


def conv_two(row, blocks, raws, weight, skip, colour):
    h2, w2, n, c = blocks[0].shape
    return pl.pallas_call(
        functools.partial(conv_two_kernel, len(blocks)),
        out_shape=(
            jax.ShapeDtypeStruct((h2, w2, n, c), f32),
            jax.ShapeDtypeStruct((h2, w2, n, c), bf16),
            jax.ShapeDtypeStruct((PAD, h2 * w2 * n), f32),
        ),
        grid_spec=pltpu.PrefetchScalarGridSpec(
            num_scalar_prefetch=1,
            grid=(9,),
            in_specs=[whole(b.shape) for b in blocks + raws]
            + [
                pl.BlockSpec((1,) + weight.shape[1:], lambda t, r: (t, 0, 0)),
                whole(skip.shape),
                whole(colour.shape),
            ],
            out_specs=(whole((h2, w2, n, c)), whole((h2, w2, n, c)), whole((PAD, h2 * w2 * n))),
            scratch_shapes=[
                pltpu.VMEM((len(blocks), h2 + 2, w2 + 2, n, c), bf16),
                pltpu.VMEM((h2 + 2, w2 + 2, n, c), bf16),
            ],
        ),
        compiler_params=kernel_params(),
        name="conv_two",
    )(row, *blocks, *raws, weight, skip, colour)


def critic_kernel(
    dims, pic_ref, first_ref, second_ref, skip_ref, head_ref, count_ref, out_ref, loss_ref, small_ref, pad_ref
):
    h2, w2, n = dims
    h, w = h2 // 2, w2 // 2
    c = second_ref.shape[-1]
    taps = [divmod(tap, 3) for tap in range(9)]
    shade = jnp.tanh(jnp.transpose(pic_ref[...]))
    picture = shade.astype(bf16).reshape(h2, w2, n, PAD)
    small_ref[...] = jnp.zeros_like(small_ref)
    small_ref[1 : h2 + 1, 1 : w2 + 1] = picture
    pad_ref[...] = jnp.zeros_like(pad_ref)
    front_pre = sum(
        times(flat(small_ref[y : y + h2, x : x + w2]), first_ref[3 * y + x]) for y, x in taps
    )
    pad_ref[1 : h2 + 1, 1 : w2 + 1] = jax.nn.silu(front_pre).astype(bf16).reshape(h2, w2, n, c)
    merged = sum(times(flat(pad_ref[y : y + h2, x : x + w2]), second_ref[3 * y + x]) for y, x in taps)
    merged = 0.25 * flat(sum_two(merged.reshape(h2, w2, n, c)))
    small = 0.25 * flat(sum_two(picture.astype(f32)))
    skip = skip_ref[...].astype(f32)
    for i in range(3):
        merged = merged + small[:, i : i + 1] * skip[i : i + 1, :]
    feature = jnp.sum(jax.nn.silu(merged).reshape(h * w, n, c), axis=0)
    weights = head_ref[...] * count_ref[...]
    loss_ref[...] = jnp.broadcast_to(-jnp.sum(feature * weights, keepdims=True), loss_ref.shape)
    grad_merged = (silu_slope(merged).reshape(h * w, n, c) * -weights[None]).astype(bf16)
    grad_merged = grad_merged.reshape(h, w, n, c)
    grad_pool = raise_two(grad_merged) * jnp.bfloat16(0.25)
    pad_ref[1 : h2 + 1, 1 : w2 + 1] = grad_pool
    grad_front = sum(
        contract_last(flat(pad_ref[2 - y : 2 - y + h2, 2 - x : 2 - x + w2]), second_ref[3 * y + x])
        for y, x in taps
    )
    grad_front_pre = (grad_front * silu_slope(front_pre)).astype(bf16)
    pad_ref[1 : h2 + 1, 1 : w2 + 1] = grad_front_pre.reshape(h2, w2, n, c)
    grad_picture = sum(
        contract_last(flat(pad_ref[2 - y : 2 - y + h2, 2 - x : 2 - x + w2]), first_ref[3 * y + x])
        for y, x in taps
    )
    grad_skip = contract_last(flat(grad_merged), skip_ref[...]).reshape(h, w, n, PAD)
    grad_picture = grad_picture + 0.25 * flat(raise_two(grad_skip))
    grad_pre = (grad_picture * (1.0 - shade * shade)).astype(bf16)
    small_ref[1 : h2 + 1, 1 : w2 + 1] = grad_pre.reshape(h2, w2, n, PAD)
    out_ref[...] = jnp.concatenate(
        [flat(small_ref[2 - y : 2 - y + h2, 2 - x : 2 - x + w2]) for y, x in taps]
        + [jnp.zeros((h2 * w2 * n, 128 - 9 * PAD), bf16)],
        axis=1,
    )


def critic(picture, disc_first, disc_second, disc_skip, head, counted, dims):
    h2, w2, n = dims
    c = disc_second.shape[-1]
    return pl.pallas_call(
        functools.partial(critic_kernel, dims),
        out_shape=(
            jax.ShapeDtypeStruct((h2 * w2 * n, 128), bf16),
            jax.ShapeDtypeStruct((8, 128), f32),
        ),
        scratch_shapes=[
            pltpu.VMEM((h2 + 2, w2 + 2, n, PAD), bf16),
            pltpu.VMEM((h2 + 2, w2 + 2, n, c), bf16),
        ],
        compiler_params=kernel_params(),
        name="critic",
    )(picture, disc_first, disc_second, disc_skip, head, counted)


def back_two_kernel(count, row_ref, g_ref, sum_ref, act_ref, colour_ref, w_ref, *refs):
    gpad_ref, gcol_ref = refs[0], refs[1]
    outs, acc_ref = refs[2:-1], refs[-1]
    h2, w2, n, c = sum_ref.shape
    t = pl.program_id(0)
    dy, dx = lax.div(t, 3), lax.rem(t, 3)

    @pl.when(t == 0)
    def _():
        grad_active = times(g_ref[...], colour_ref[...]).reshape(h2, w2, n, c)
        gpad_ref[...] = jnp.zeros_like(gpad_ref)
        gpad_ref[1 : h2 + 1, 1 : w2 + 1] = (grad_active * silu_slope(sum_ref[...])).astype(bf16)
        gcol_ref[...] = lax.dot_general(
            g_ref[...], flat(act_ref[...]), (((0,), (0,)), ((), ())), preferred_element_type=f32
        )
        acc_ref[...] = jnp.zeros_like(acc_ref)

    shifted = flat(gpad_ref[pl.ds(2 - dy, h2), pl.ds(2 - dx, w2)])
    for k in range(count):
        acc_ref[k] += contract_last(shifted, w_ref[0, owned_rows(row_ref, k, c), :])

    @pl.when(t == 8)
    def _():
        for k in range(count):
            outs[k][...] = acc_ref[k].astype(bf16)


def back_two(row, grads, summed, active, colour, weight, count):
    h2, w2, n, c = summed.shape
    rows = h2 * w2 * n
    return pl.pallas_call(
        functools.partial(back_two_kernel, count),
        out_shape=(
            jax.ShapeDtypeStruct((h2 + 2, w2 + 2, n, c), bf16),
            jax.ShapeDtypeStruct((128, c), f32),
        )
        + tuple(jax.ShapeDtypeStruct((rows, c), bf16) for _ in range(count)),
        grid_spec=pltpu.PrefetchScalarGridSpec(
            num_scalar_prefetch=1,
            grid=(9,),
            in_specs=[
                whole(grads.shape),
                whole(summed.shape),
                whole(active.shape),
                whole(colour.shape),
                pl.BlockSpec((1,) + weight.shape[1:], lambda t, r: (t, 0, 0)),
            ],
            out_specs=(whole((h2 + 2, w2 + 2, n, c)), whole((128, c)))
            + tuple(whole((rows, c)) for _ in range(count)),
            scratch_shapes=[pltpu.VMEM((count, rows, c), f32)],
        ),
        compiler_params=kernel_params(),
        name="back_two",
    )(row, grads, summed, active, colour, weight)


def weight_two_kernel(count, row_ref, gpad_ref, *refs):
    blocks, raws, (out_ref, skip_ref) = refs[:count], refs[count : 2 * count], refs[2 * count :]
    h2, w2, n, c = (gpad_ref.shape[0] - 2, gpad_ref.shape[1] - 2) + gpad_ref.shape[2:]
    t = pl.program_id(0)
    dy, dx = lax.div(t, 3), lax.rem(t, 3)
    shifted = flat(gpad_ref[pl.ds(2 - dy, h2), pl.ds(2 - dx, w2)])
    for k in range(count):
        out_ref[0, owned_rows(row_ref, k, c), :] = times(blocks[k][...], shifted).astype(bf16)

    @pl.when(t == 8)
    def _():
        phases = gpad_ref[1 : h2 + 1, 1 : w2 + 1].reshape(h2 // 2, 2, w2 // 2, 2, n, c)
        for k in range(count):
            size = raws[k].shape[0]
            skip_ref[owned_rows(row_ref, k, size), :] = sum(
                times(raws[k][...], flat(phases[:, a, :, b])) for a in range(2) for b in range(2)
            ).astype(bf16)


def weight_two(row, gpad, blocks, raws):
    c = gpad.shape[-1]
    count = len(blocks)
    tall, wide = count * blocks[0].shape[0], count * raws[0].shape[0]
    return pl.pallas_call(
        functools.partial(weight_two_kernel, count),
        out_shape=(
            jax.ShapeDtypeStruct((9, tall, c), bf16),
            jax.ShapeDtypeStruct((wide, c), bf16),
        ),
        grid_spec=pltpu.PrefetchScalarGridSpec(
            num_scalar_prefetch=1,
            grid=(9,),
            in_specs=[whole(gpad.shape)] + [whole(b.shape) for b in blocks + raws],
            out_specs=(pl.BlockSpec((1, tall, c), lambda t, r: (t, 0, 0)), whole((wide, c))),
        ),
        compiler_params=kernel_params(),
        name="weight_two",
    )(row, gpad, *blocks, *raws)


def back_one_kernel(count, row_ref, g_ref, w_ref, *refs):
    blocks, out_ref, outs = refs[:count], refs[count], refs[count + 1 : 2 * count + 1]
    pad_ref, acc_ref = refs[2 * count + 1 :]
    h2, w2, n, c = g_ref.shape
    size = blocks[0].shape[0]
    t = pl.program_id(0)
    dy, dx = lax.div(t, 3), lax.rem(t, 3)

    @pl.when(t == 0)
    def _():
        pad_ref[...] = jnp.zeros_like(pad_ref)
        pad_ref[1 : h2 + 1, 1 : w2 + 1] = g_ref[...]
        acc_ref[...] = jnp.zeros_like(acc_ref)

    shifted = pad_ref[pl.ds(2 - dy, h2), pl.ds(2 - dx, w2)].astype(f32)
    pooled = flat(sum_two(shifted)).astype(bf16)
    for k in range(count):
        rows = owned_rows(row_ref, k, size)
        acc_ref[k] += contract_last(pooled, w_ref[0, rows, :])
        out_ref[0, rows, :] = times(blocks[k][...], pooled).astype(bf16)

    @pl.when(t == 8)
    def _():
        for k in range(count):
            outs[k][...] = acc_ref[k].astype(bf16)


def back_one(row, grads, weight, blocks):
    h2, w2, n, c = grads.shape
    count = len(blocks)
    size, rows = blocks[0].shape
    return pl.pallas_call(
        functools.partial(back_one_kernel, count),
        out_shape=(jax.ShapeDtypeStruct((9, count * size, c), bf16),)
        + tuple(jax.ShapeDtypeStruct((rows, size), bf16) for _ in range(count)),
        grid_spec=pltpu.PrefetchScalarGridSpec(
            num_scalar_prefetch=1,
            grid=(9,),
            in_specs=[
                whole(grads.shape),
                pl.BlockSpec((1,) + weight.shape[1:], lambda t, r: (t, 0, 0)),
            ]
            + [whole(b.shape) for b in blocks],
            out_specs=(pl.BlockSpec((1, count * size, c), lambda t, r: (t, 0, 0)),)
            + tuple(whole((rows, size)) for _ in range(count)),
            scratch_shapes=[
                pltpu.VMEM((h2 + 2, w2 + 2, n, c), bf16),
                pltpu.VMEM((count, rows, size), f32),
            ],
        ),
        compiler_params=kernel_params(),
        name="back_one",
    )(row, grads, weight, *blocks)


def in_order(pieces, axis_name):
    piled = jnp.stack(pieces, axis=0)
    r = lax.axis_index(axis_name)
    return jnp.concatenate(
        [
            lax.dynamic_index_in_dim(piled, lax.bitwise_xor(r, j), 0, keepdims=False)
            for j in range(len(pieces))
        ],
        axis=0,
    )


def gram_share(owned, pieces):
    blocks = [
        lax.dot_general(piece, owned, (((0,), (0,)), ((), ())), preferred_element_type=f32)
        for piece in pieces
    ]
    return in_order(blocks, "row")


def gram_whole(panel):
    n = lax.axis_size("dp")
    h, z = lax.axis_index("half"), lax.axis_index("dp")
    total = group_sum_wide(panel)
    pieces = row_gather(total)
    piled = jnp.stack(pieces, axis=0)
    r = lax.axis_index("row")
    return jnp.concatenate(
        [
            lax.dynamic_index_in_dim(piled, lax.bitwise_xor(r, j), 0, keepdims=False)
            for j in range(len(pieces))
        ],
        axis=1,
    )


def group_sum_wide(value):
    return group_gather(group_scatter(value))


def mul(left, right):
    return jnp.dot(left, right, precision=high, preferred_element_type=f32)


def newton_columns(gram, own):
    scale = lax.rsqrt(jnp.trace(gram) + NEWTON_EPSILON)
    current = gram * (scale * scale)
    identity = jnp.eye(gram.shape[0], dtype=f32)
    maps = []
    for iteration in range(NS_ITERS):
        square = mul(current, current)
        mapping = NS_COEF[0] * identity + NS_COEF[1] * current + NS_COEF[2] * square
        maps.append(mapping)
        if iteration < NS_ITERS - 1:
            current = mul(mapping, mul(current, mapping))
    start = lax.axis_index("row") * own
    columns = lax.dynamic_slice_in_dim(maps[-1], start, own, 1)
    for mapping in maps[-2::-1]:
        columns = mul(mapping, columns)
    return columns * scale


def muon(master, moment, gradient, groups):
    moment_new = MOMENTUM * moment + gradient
    owned = moment_new.astype(bf16)
    pieces = row_gather(owned)
    own = owned.shape[1]
    gram = gram_whole(gram_share(owned, pieces))
    columns = newton_columns(gram, own).astype(bf16)
    r = lax.axis_index("row")
    direction = sum(
        times(
            piece,
            lax.dynamic_slice_in_dim(columns, lax.bitwise_xor(r, k) * own, own, 0),
        )
        for k, piece in enumerate(pieces)
    )
    factor = 0.2 * math.sqrt(max(master.shape[0] * groups, own * len(pieces)))
    return master - MUON_RATE * (factor * direction + DECAY * master), moment_new


def adam_update(weight, gradient, mean_old, square_old, rate):
    mean_new = BETA_ONE * mean_old + (1.0 - BETA_ONE) * gradient
    square_new = BETA_TWO * square_old + (1.0 - BETA_TWO) * gradient * gradient
    ratio = (
        mean_new
        / (1.0 - BETA_ONE**STEP)
        / (jnp.sqrt(square_new / (1.0 - BETA_TWO**STEP)) + ADAM_EPS)
    )
    return (weight - rate * (ratio + DECAY * weight), mean_new, square_new)


def moments_of(totals, count):
    centre = totals[:MICRO] / count
    return centre, lax.rsqrt(totals[MICRO:] / count - centre * centre + BN_EPS)


def per_image(values, n):
    return jnp.repeat(values, n // MICRO, axis=0)


def per_micro(values):
    return jnp.sum(values.reshape(MICRO, -1, values.shape[-1]), axis=1)


def per_device(
    features,
    noise,
    labels,
    counted,
    disc_first,
    disc_second,
    disc_skip,
    disc_head,
    disc_table,
    conv_first,
    conv_second,
    conv_skip,
    momentum_first,
    momentum_second,
    momentum_skip,
    class_table,
    table_mean,
    table_square,
    norm_first,
    first_mean,
    first_square,
    norm_second,
    second_mean,
    second_square,
    colour_conv,
    colour_mean,
    colour_square,
):
    groups = lax.axis_size("half") * lax.axis_size("dp")
    ranks = lax.axis_size("row")
    row = lax.axis_index("row").astype(jnp.int32).reshape(1)
    n, h, w, c_in = features.shape
    c_out = conv_first.shape[1]
    count_low = float(n // MICRO * h * w * groups)
    count_high = 4.0 * count_low

    inputs = jnp.transpose(features, (1, 2, 0, 3))
    raw = inputs.astype(f32)
    sums_low = jnp.concatenate(
        [per_micro(jnp.sum(raw, axis=(0, 1))), per_micro(jnp.sum(raw * raw, axis=(0, 1)))], axis=0
    )
    totals_low = group_sum(sums_low)
    weight_one = group_gather(conv_first.astype(bf16)).reshape(9, ranks * c_in, c_out)

    onehot = (labels[:, None] == jnp.arange(NCLS)[None, :]).astype(f32)
    conds = jnp.concatenate([jnp.dot(onehot, class_table, precision=highest), noise], axis=1)
    class_disc = jnp.dot(onehot, disc_table, precision=highest)
    mods_one = jnp.einsum("bk,kgc->bgc", conds, norm_first, precision=highest)
    mods_two = jnp.einsum("bk,kgc->bgc", conds, norm_second, precision=highest)

    centre_one, spread_one = moments_of(totals_low, count_low)
    centre_one, spread_one = per_image(centre_one, n), per_image(spread_one, n)
    gain_one, gain_two = 1.0 + mods_one[:, 0], 1.0 + mods_two[:, 0]
    normed_one = (raw - centre_one) * spread_one
    pre_one = normed_one * gain_one + mods_one[:, 1]
    acted_one = flat(jax.nn.silu(pre_one).astype(bf16))
    ones = row_gather(acted_one)
    raws = row_gather(flat(inputs))

    hidden, sums_high = conv_one(row, ones, weight_one, (h, w, n))
    held_second, held_skip, _ = lax.optimization_barrier(
        (conv_second.astype(bf16), conv_skip.astype(bf16), weight_one[0, 0, 0])
    )
    weight_skip = group_gather(held_skip)
    weight_two = group_gather(held_second).reshape(9, ranks * c_out, c_out)
    totals_high = group_sum(sums_high)
    centre_two, spread_two = moments_of(totals_high, count_high)
    centre_two, spread_two = per_image(centre_two, n), per_image(spread_two, n)
    normed_two = (hidden - centre_two) * spread_two
    pre_two = normed_two * gain_two + mods_two[:, 1]
    acted_two = jax.nn.silu(pre_two).astype(bf16)
    twos = row_gather(acted_two)

    colour = jnp.pad(
        jnp.transpose(colour_conv, (0, 2, 1)).astype(bf16), ((0, 0), (0, PAD - 3), (0, 0))
    )
    summed, active, picture = conv_two(row, twos, raws, weight_two, weight_skip, colour)
    picture = row_sum(picture)

    first_taps = jnp.pad(disc_first.reshape(9, 3, -1), ((0, 0), (0, PAD - 3), (0, 0)))
    second_taps = disc_second.reshape(9, -1, disc_second.shape[-1])
    skip_taps = jnp.pad(disc_skip, ((0, PAD - 3), (0, 0)))
    mark = counted.astype(f32)[:, None]
    grads, loss_part = critic(
        picture,
        first_taps,
        second_taps,
        skip_taps,
        disc_head[None, :] + class_disc,
        mark,
        (2 * h, 2 * w, n),
    )
    colour_rows = jnp.pad(colour.reshape(9 * PAD, c_out), ((0, 128 - 9 * PAD), (0, 0)))
    backs = back_two(row, grads, summed, active, colour_rows, weight_two, ranks)
    gpad, grad_colour, pieces = backs[0], backs[1], backs[2:]
    grad_two, grad_skip = weight_two_grads(row, gpad, twos, raws)
    grad_acted_two = row_scatter(list(pieces)).reshape(hidden.shape)

    grad_pre_two = grad_acted_two * silu_slope(pre_two)
    gains_two = jnp.sum(grad_pre_two * normed_two, axis=(0, 1))
    shifts_two = jnp.sum(grad_pre_two, axis=(0, 1))
    back_sums = group_sum(
        jnp.concatenate([per_micro(gain_two * shifts_two), per_micro(gain_two * gains_two)], axis=0)
    )
    mean_g = per_image(back_sums[:MICRO] / count_high, n)
    mean_gy = per_image(back_sums[MICRO:] / count_high, n)
    grad_hidden = (spread_two * (grad_pre_two * gain_two - mean_g - normed_two * mean_gy)).astype(
        bf16
    )
    ones_turned = [jnp.transpose(one) for one in ones]
    backs = back_one(row, grad_hidden, weight_one, ones_turned)
    grad_one, pieces = flat(backs[0]), backs[1:]
    grad_acted_one = row_scatter(list(pieces)).reshape(raw.shape)
    grad_pre_one = grad_acted_one * silu_slope(pre_one)
    gains_one = jnp.sum(grad_pre_one * normed_one, axis=(0, 1))
    shifts_one = jnp.sum(grad_pre_one, axis=(0, 1))
    grad_mods_one = jnp.stack([gains_one, shifts_one], axis=1)
    grad_mods_two = jnp.stack([gains_two, shifts_two], axis=1)

    grad_cond = jnp.einsum("bgc,kgc->bk", grad_mods_one, norm_first[:EMB], precision=highest)
    grad_cond = grad_cond + jnp.einsum(
        "bgc,kgc->bk", grad_mods_two, norm_second[:EMB], precision=highest
    )
    grad_cond = row_sum(grad_cond)

    count_part = jnp.sum(counted).astype(f32)
    small = jnp.concatenate(
        [
            grad_colour[: 9 * PAD],
            jnp.broadcast_to(loss_part[:1, :1], (1, c_out)),
            jnp.broadcast_to(count_part, (1, c_out)),
        ],
        axis=0,
    )
    small = group_sum(small)
    loss_sum, fake_count = small[9 * PAD, 0], small[9 * PAD + 1, 0]
    inverse = 1.0 / fake_count
    g_colour = jnp.transpose(small[: 9 * PAD].reshape(9, PAD, c_out)[:, :3], (0, 2, 1))

    known = group_pile(jnp.concatenate([conds, labels.astype(f32)[:, None]], axis=1))
    found = group_pile(
        jnp.concatenate(
            [grad_mods_one.reshape(n, -1), grad_mods_two.reshape(n, -1), grad_cond], axis=1
        )
    )
    conds_all, labels_all = known[:, :-1], known[:, -1].astype(jnp.int32)
    onehot_all = (labels_all[:, None] == jnp.arange(NCLS)[None, :]).astype(f32)
    cut_one, cut_two = 2 * c_in, 2 * c_in + 2 * c_out
    g_norm = lax.dot_general(
        conds_all,
        found[:, :cut_two],
        (((0,), (0,)), ((), ())),
        precision=highest,
        preferred_element_type=f32,
    )
    g_norm_one = g_norm[:, :cut_one].reshape(norm_first.shape)
    g_norm_two = g_norm[:, cut_one:].reshape(norm_second.shape)
    g_table = lax.dot_general(
        onehot_all,
        found[:, cut_two:],
        (((0,), (0,)), ((), ())),
        precision=highest,
        preferred_element_type=f32,
    )

    shares = [group_scatter(flat(g)) for g in (grad_one, grad_two, grad_skip)]
    muons = [
        muon(master, moment, share * inverse, groups)
        for master, moment, share in zip(
            (conv_first, conv_second, conv_skip),
            (momentum_first, momentum_second, momentum_skip),
            shares,
        )
    ]
    table_new = adam_update(class_table, g_table * inverse, table_mean, table_square, ADAM_RATE)
    first_new = adam_update(norm_first, g_norm_one * inverse, first_mean, first_square, ADAM_RATE)
    second_new = adam_update(
        norm_second, g_norm_two * inverse, second_mean, second_square, ADAM_RATE
    )
    colour_new = adam_update(
        colour_conv, g_colour * inverse, colour_mean, colour_square, COLOUR_RATE
    )
    return (
        (loss_sum, fake_count)
        + tuple(m[0] for m in muons)
        + tuple(m[1] for m in muons)
        + table_new
        + first_new
        + second_new
        + colour_new
    )


def weight_two_grads(row, gpad, twos, raws):
    turned = [jnp.transpose(flat(two)) for two in twos]
    return weight_two(row, gpad, turned, [jnp.transpose(one) for one in raws])


def solution(mesh):
    group = ("half", "dp")
    placed = (
        (P(group, None, None, "row"), P(group, None), P(group), P(group))
        + (P(),) * 5
        + (P(group, "row"),) * 6
        + (P(),) * 3
        + (P(None, None, "row"),) * 6
        + (P(None, "row", None),) * 3
    )
    return jax.shard_map(
        per_device,
        mesh=mesh,
        in_specs=placed,
        out_specs=(P(), P())
        + (P(group, "row"),) * 6
        + (P(),) * 3
        + (P(None, None, "row"),) * 6
        + (P(None, "row", None),) * 3,
        check_vma=False,
    )
```

```python
import functools
import math

import jax
import jax.numpy as jnp
from jax import lax
from jax.experimental import pallas as pl
from jax.experimental.pallas import tpu as pltpu
from jax.sharding import PartitionSpec as P

EMB = 128
NCLS = 1000
MICRO = 2
NS_ITERS = 5
STEP = 10

highest = lax.Precision.HIGHEST
high = lax.Precision.HIGH
bf16 = jnp.bfloat16
f32 = jnp.float32
BN_EPS = 1e-05
NEWTON_EPSILON = 1e-07
NS_COEF = (3.4445, -4.775, 2.0315)
MOMENTUM = 0.9
MUON_RATE = 0.03
DECAY = 0.01
BETA_ONE = 0.9
BETA_TWO = 0.95
ADAM_EPS = 1e-08
ADAM_RATE = 0.05
COLOUR_RATE = 0.01
PAD = 8
MIB = 1024 * 1024


def kernel_params(size=20):
    return pltpu.CompilerParams(vmem_limit_bytes=size * MIB)


def whole(shape):
    return pl.BlockSpec(shape, lambda t, r: (0,) * len(shape))


def silu_slope(values):
    sigmoid_value = jax.nn.sigmoid(values)
    return sigmoid_value * (1.0 + values * (1.0 - sigmoid_value))


def contract_last(left, right):
    return lax.dot_general(left, right, (((1,), (1,)), ((), ())), preferred_element_type=f32)


def times(left, right):
    return jnp.dot(left, right, preferred_element_type=f32)


def axis_swap(value, axis, k):
    n = lax.axis_size(axis)
    return lax.ppermute(value, axis, [(i, i ^ k) for i in range(n)])


def axis_shift(value, axis, k):
    n = lax.axis_size(axis)
    return lax.ppermute(value, axis, [(i, (i + k) % n) for i in range(n)])


def row_gather(value):
    return [value] + [axis_swap(value, "row", k) for k in range(1, lax.axis_size("row"))]


def row_sum(value):
    return sum(row_gather(value))


def row_exchange(pieces):
    return [pieces[0]] + [axis_swap(pieces[k], "row", k) for k in range(1, len(pieces))]


def row_scatter(pieces):
    return sum(piece.astype(f32) for piece in row_exchange(pieces))


GROUP = ("half", "dp")


def group_sum(value):
    return lax.psum(value, GROUP)


def group_pile(value):
    return lax.all_gather(value, GROUP, axis=0, tiled=True)


def group_gather(value):
    return lax.all_gather(value, GROUP, axis=0, tiled=True)


def group_scatter(value):
    return lax.psum_scatter(value, GROUP, scatter_dimension=0, tiled=True).astype(f32)


def spread(value, axis):
    n = math.prod(lax.axis_size(name) for name in axis)
    return lax.all_to_all(jnp.broadcast_to(value[None], (n,) + value.shape), axis, 0, 0)


def near_sum(value):
    return jnp.sum(spread(value, GROUP), axis=0)


def after(value, *others):
    return lax.optimization_barrier((value,) + others)[0]


def step_below(value, s):
    n = lax.axis_size("dp")
    return lax.ppermute(value, "dp", [(i, i + 1) for i in range(s - 1, n - 1)])


def step_above(value, s):
    n = lax.axis_size("dp")
    return lax.ppermute(value, "dp", [(i, i - 1) for i in range(1, n - s + 1)])


def straight(value):
    return [value] + [axis_shift(value, "dp", k) for k in range(1, lax.axis_size("dp"))]


def both_cores(pieces):
    return pieces + [axis_swap(piece, "half", 1) for piece in pieces]


def placed_in_order(pieces):
    n = len(pieces)
    turned = [pieces[0]] + pieces[:0:-1]
    piled = jnp.stack(turned + turned[:-1], axis=0)
    start = lax.rem(n - lax.axis_index("dp"), n)
    return lax.dynamic_slice_in_dim(piled, start, n, 0)


def near_halves(value):
    h = lax.axis_index("half")
    kept = lax.dynamic_index_in_dim(value, h, 0, keepdims=False)
    sent = lax.dynamic_index_in_dim(value, 1 - h, 0, keepdims=False)
    return kept.astype(f32) + axis_swap(sent, "half", 1).astype(f32)


def near_blocks(kept, wire):
    n = lax.axis_size("dp")
    z = lax.axis_index("dp")
    pieces = [lax.dynamic_index_in_dim(kept, z, 0, keepdims=False)]
    for k in range(1, n):
        block = lax.dynamic_index_in_dim(wire, lax.rem(z + k, n), 0, keepdims=False)
        pieces.append(axis_shift(block, "dp", k))
    return pieces


def raise_two(values):
    h, w, n, c = values.shape
    wide = jnp.stack([values, values], axis=2).reshape(h, 2 * w, n, c)
    return jnp.stack([wide, wide], axis=1).reshape(2 * h, 2 * w, n, c)


def sum_two(values):
    h, w, n, c = values.shape
    shaped = values.reshape(h // 2, 2, w // 2, 2, n, c)
    return (shaped[:, 0, :, 0] + shaped[:, 0, :, 1]) + (shaped[:, 1, :, 0] + shaped[:, 1, :, 1])


def owned_rows(row_ref, k, size):
    return pl.ds(pl.multiple_of(lax.bitwise_xor(row_ref[0], k) * size, size), size)


def flat(values):
    return values.reshape(-1, values.shape[-1])


def conv_one_kernel(row_ref, *refs):
    blocks, (w_ref, out_ref, sums_ref, acc_ref) = refs[:-4], refs[-4:]
    h2, w2, n, c = out_ref.shape
    t = pl.program_id(0)
    dy, dx = lax.div(t, 3), lax.rem(t, 3)

    @pl.when(t == 0)
    def _():
        acc_ref[...] = jnp.zeros_like(acc_ref)

    product = sum(
        times(x_ref[0], w_ref[0, owned_rows(row_ref, k, x_ref.shape[2]), :])
        for k, x_ref in enumerate(blocks)
    )
    raised = raise_two(product.reshape(h2 // 2, w2 // 2, n, c))
    acc_ref[pl.ds(2 - dy, h2), pl.ds(2 - dx, w2)] += raised

    @pl.when(t == 8)
    def _():
        hidden = acc_ref[1 : h2 + 1, 1 : w2 + 1]
        out_ref[...] = hidden
        shaped = hidden.reshape(h2 * w2, n, c)
        first, second = jnp.sum(shaped, axis=0), jnp.sum(shaped * shaped, axis=0)
        m = n // MICRO
        for i in range(MICRO):
            sums_ref[i : i + 1, :] = jnp.sum(first[i * m : (i + 1) * m], axis=0, keepdims=True)
            sums_ref[MICRO + i : MICRO + i + 1, :] = jnp.sum(
                second[i * m : (i + 1) * m], axis=0, keepdims=True
            )


def conv_one(row, blocks, weight, pixels):
    h, w, n = pixels
    c = weight.shape[-1]
    return pl.pallas_call(
        conv_one_kernel,
        out_shape=(
            jax.ShapeDtypeStruct((2 * h, 2 * w, n, c), f32),
            jax.ShapeDtypeStruct((2 * MICRO, c), f32),
        ),
        grid_spec=pltpu.PrefetchScalarGridSpec(
            num_scalar_prefetch=1,
            grid=(9,),
            in_specs=[whole(b.shape) for b in blocks]
            + [pl.BlockSpec((1,) + weight.shape[1:], lambda t, r: (t, 0, 0))],
            out_specs=(whole((2 * h, 2 * w, n, c)), whole((2 * MICRO, c))),
            scratch_shapes=[pltpu.VMEM((2 * h + 2, 2 * w + 2, n, c), f32)],
        ),
        compiler_params=kernel_params(),
        name="conv_one",
    )(row, *blocks, weight)


def conv_two_kernel(count, row_ref, *refs):
    blocks, raws = refs[:count], refs[count : 2 * count]
    w_ref, skip_ref, colour_ref, sum_ref, act_ref, pic_ref, pad_ref, apad_ref = refs[2 * count :]
    h2, w2, n, c = sum_ref.shape
    t = pl.program_id(0)
    dy, dx = lax.div(t, 3), lax.rem(t, 3)

    @pl.when(t == 0)
    def _():
        pad_ref[...] = jnp.zeros_like(pad_ref)
        for k in range(count):
            pad_ref[k, 1 : h2 + 1, 1 : w2 + 1] = blocks[k][...]
        skipped = sum(
            times(x_ref[x_ref.shape[0] - 1], skip_ref[owned_rows(row_ref, k, x_ref.shape[2]), :])
            for k, x_ref in enumerate(raws)
        )
        sum_ref[...] = raise_two(skipped.reshape(h2 // 2, w2 // 2, n, c))

    product = sum(
        times(
            flat(pad_ref[k, pl.ds(dy, h2), pl.ds(dx, w2)]), w_ref[0, owned_rows(row_ref, k, c), :]
        )
        for k in range(count)
    )
    sum_ref[...] += product.reshape(sum_ref.shape)

    @pl.when(t == 8)
    def _():
        active = jax.nn.silu(sum_ref[...]).astype(bf16)
        act_ref[...] = active
        apad_ref[...] = jnp.zeros_like(apad_ref)
        apad_ref[1 : h2 + 1, 1 : w2 + 1] = active
        picture = jnp.zeros(pic_ref.shape, f32)
        for tap in range(9):
            y, x = divmod(tap, 3)
            picture = picture + contract_last(
                colour_ref[tap], flat(apad_ref[y : y + h2, x : x + w2])
            )
        pic_ref[...] = picture


def conv_two(row, blocks, raws, weight, skip, colour):
    h2, w2, n, c = blocks[0].shape
    return pl.pallas_call(
        functools.partial(conv_two_kernel, len(blocks)),
        out_shape=(
            jax.ShapeDtypeStruct((h2, w2, n, c), f32),
            jax.ShapeDtypeStruct((h2, w2, n, c), bf16),
            jax.ShapeDtypeStruct((PAD, h2 * w2 * n), f32),
        ),
        grid_spec=pltpu.PrefetchScalarGridSpec(
            num_scalar_prefetch=1,
            grid=(9,),
            in_specs=[whole(b.shape) for b in blocks + raws]
            + [
                pl.BlockSpec((1,) + weight.shape[1:], lambda t, r: (t, 0, 0)),
                whole(skip.shape),
                whole(colour.shape),
            ],
            out_specs=(whole((h2, w2, n, c)), whole((h2, w2, n, c)), whole((PAD, h2 * w2 * n))),
            scratch_shapes=[
                pltpu.VMEM((len(blocks), h2 + 2, w2 + 2, n, c), bf16),
                pltpu.VMEM((h2 + 2, w2 + 2, n, c), bf16),
            ],
        ),
        compiler_params=kernel_params(28),
        name="conv_two",
    )(row, *blocks, *raws, weight, skip, colour)


def critic_kernel(
    dims, pic_ref, first_ref, second_ref, skip_ref, head_ref, count_ref, out_ref, loss_ref, small_ref, pad_ref
):
    h2, w2, n = dims
    h, w = h2 // 2, w2 // 2
    c = second_ref.shape[-1]
    taps = [divmod(tap, 3) for tap in range(9)]
    shade = jnp.tanh(jnp.transpose(pic_ref[...]))
    picture = shade.astype(bf16).reshape(h2, w2, n, PAD)
    small_ref[...] = jnp.zeros_like(small_ref)
    small_ref[1 : h2 + 1, 1 : w2 + 1] = picture
    pad_ref[...] = jnp.zeros_like(pad_ref)
    front_pre = sum(
        times(flat(small_ref[y : y + h2, x : x + w2]), first_ref[3 * y + x]) for y, x in taps
    )
    pad_ref[1 : h2 + 1, 1 : w2 + 1] = jax.nn.silu(front_pre).astype(bf16).reshape(h2, w2, n, c)
    merged = sum(times(flat(pad_ref[y : y + h2, x : x + w2]), second_ref[3 * y + x]) for y, x in taps)
    merged = 0.25 * flat(sum_two(merged.reshape(h2, w2, n, c)))
    small = 0.25 * flat(sum_two(picture.astype(f32)))
    skip = skip_ref[...].astype(f32)
    for i in range(3):
        merged = merged + small[:, i : i + 1] * skip[i : i + 1, :]
    feature = jnp.sum(jax.nn.silu(merged).reshape(h * w, n, c), axis=0)
    weights = head_ref[...] * count_ref[...]
    loss_ref[...] = jnp.broadcast_to(-jnp.sum(feature * weights, keepdims=True), loss_ref.shape)
    grad_merged = (silu_slope(merged).reshape(h * w, n, c) * -weights[None]).astype(bf16)
    grad_merged = grad_merged.reshape(h, w, n, c)
    grad_pool = raise_two(grad_merged) * jnp.bfloat16(0.25)
    pad_ref[1 : h2 + 1, 1 : w2 + 1] = grad_pool
    grad_front = sum(
        contract_last(flat(pad_ref[2 - y : 2 - y + h2, 2 - x : 2 - x + w2]), second_ref[3 * y + x])
        for y, x in taps
    )
    grad_front_pre = (grad_front * silu_slope(front_pre)).astype(bf16)
    pad_ref[1 : h2 + 1, 1 : w2 + 1] = grad_front_pre.reshape(h2, w2, n, c)
    grad_picture = sum(
        contract_last(flat(pad_ref[2 - y : 2 - y + h2, 2 - x : 2 - x + w2]), first_ref[3 * y + x])
        for y, x in taps
    )
    grad_skip = contract_last(flat(grad_merged), skip_ref[...]).reshape(h, w, n, PAD)
    grad_picture = grad_picture + 0.25 * flat(raise_two(grad_skip))
    grad_pre = (grad_picture * (1.0 - shade * shade)).astype(bf16)
    small_ref[1 : h2 + 1, 1 : w2 + 1] = grad_pre.reshape(h2, w2, n, PAD)
    out_ref[...] = jnp.concatenate(
        [flat(small_ref[2 - y : 2 - y + h2, 2 - x : 2 - x + w2]) for y, x in taps]
        + [jnp.zeros((h2 * w2 * n, 128 - 9 * PAD), bf16)],
        axis=1,
    )


def critic(picture, disc_first, disc_second, disc_skip, head, counted, dims):
    h2, w2, n = dims
    c = disc_second.shape[-1]
    return pl.pallas_call(
        functools.partial(critic_kernel, dims),
        out_shape=(
            jax.ShapeDtypeStruct((h2 * w2 * n, 128), bf16),
            jax.ShapeDtypeStruct((8, 128), f32),
        ),
        scratch_shapes=[
            pltpu.VMEM((h2 + 2, w2 + 2, n, PAD), bf16),
            pltpu.VMEM((h2 + 2, w2 + 2, n, c), bf16),
        ],
        compiler_params=kernel_params(28),
        name="critic",
    )(picture, disc_first, disc_second, disc_skip, head, counted)


def back_two_kernel(count, row_ref, g_ref, sum_ref, act_ref, colour_ref, w_ref, *refs):
    gpad_ref, gcol_ref = refs[0], refs[1]
    outs, acc_ref = refs[2:-1], refs[-1]
    h2, w2, n, c = sum_ref.shape
    t = pl.program_id(0)
    dy, dx = lax.div(t, 3), lax.rem(t, 3)

    @pl.when(t == 0)
    def _():
        grad_active = times(g_ref[...], colour_ref[...]).reshape(h2, w2, n, c)
        gpad_ref[...] = jnp.zeros_like(gpad_ref)
        gpad_ref[1 : h2 + 1, 1 : w2 + 1] = (grad_active * silu_slope(sum_ref[...])).astype(bf16)
        gcol_ref[...] = lax.dot_general(
            g_ref[...], flat(act_ref[...]), (((0,), (0,)), ((), ())), preferred_element_type=f32
        )
        acc_ref[...] = jnp.zeros_like(acc_ref)

    shifted = flat(gpad_ref[pl.ds(2 - dy, h2), pl.ds(2 - dx, w2)])
    for k in range(count):
        acc_ref[k] += contract_last(shifted, w_ref[0, owned_rows(row_ref, k, c), :])

    @pl.when(t == 8)
    def _():
        for k in range(count):
            outs[k][...] = acc_ref[k].astype(bf16)


def back_two(row, grads, summed, active, colour, weight, count):
    h2, w2, n, c = summed.shape
    rows = h2 * w2 * n
    return pl.pallas_call(
        functools.partial(back_two_kernel, count),
        out_shape=(
            jax.ShapeDtypeStruct((h2 + 2, w2 + 2, n, c), bf16),
            jax.ShapeDtypeStruct((128, c), f32),
        )
        + tuple(jax.ShapeDtypeStruct((rows, c), bf16) for _ in range(count)),
        grid_spec=pltpu.PrefetchScalarGridSpec(
            num_scalar_prefetch=1,
            grid=(9,),
            in_specs=[
                whole(grads.shape),
                whole(summed.shape),
                whole(active.shape),
                whole(colour.shape),
                pl.BlockSpec((1,) + weight.shape[1:], lambda t, r: (t, 0, 0)),
            ],
            out_specs=(whole((h2 + 2, w2 + 2, n, c)), whole((128, c)))
            + tuple(whole((rows, c)) for _ in range(count)),
            scratch_shapes=[pltpu.VMEM((count, rows, c), f32)],
        ),
        compiler_params=kernel_params(28),
        name="back_two",
    )(row, grads, summed, active, colour, weight)


def weight_two_kernel(count, row_ref, gpad_ref, *refs):
    blocks, raws, (out_ref, skip_ref) = refs[:count], refs[count : 2 * count], refs[2 * count :]
    h2, w2, n, c = (gpad_ref.shape[0] - 2, gpad_ref.shape[1] - 2) + gpad_ref.shape[2:]
    t = pl.program_id(0)
    dy, dx = lax.div(t, 3), lax.rem(t, 3)
    shifted = flat(gpad_ref[pl.ds(2 - dy, h2), pl.ds(2 - dx, w2)])
    for k in range(count):
        out_ref[0, owned_rows(row_ref, k, c), :] = times(blocks[k][...], shifted).astype(bf16)

    @pl.when(t == 8)
    def _():
        phases = gpad_ref[1 : h2 + 1, 1 : w2 + 1].reshape(h2 // 2, 2, w2 // 2, 2, n, c)
        for k in range(count):
            size = raws[k].shape[0]
            skip_ref[owned_rows(row_ref, k, size), :] = sum(
                times(raws[k][...], flat(phases[:, a, :, b])) for a in range(2) for b in range(2)
            ).astype(bf16)


def weight_two(row, gpad, blocks, raws):
    c = gpad.shape[-1]
    count = len(blocks)
    tall, wide = count * blocks[0].shape[0], count * raws[0].shape[0]
    return pl.pallas_call(
        functools.partial(weight_two_kernel, count),
        out_shape=(
            jax.ShapeDtypeStruct((9, tall, c), bf16),
            jax.ShapeDtypeStruct((wide, c), bf16),
        ),
        grid_spec=pltpu.PrefetchScalarGridSpec(
            num_scalar_prefetch=1,
            grid=(9,),
            in_specs=[whole(gpad.shape)] + [whole(b.shape) for b in blocks + raws],
            out_specs=(pl.BlockSpec((1, tall, c), lambda t, r: (t, 0, 0)), whole((wide, c))),
        ),
        compiler_params=kernel_params(28),
        name="weight_two",
    )(row, gpad, *blocks, *raws)


def back_one_kernel(count, row_ref, g_ref, w_ref, *refs):
    blocks, out_ref, outs = refs[:count], refs[count], refs[count + 1 : 2 * count + 1]
    pad_ref, acc_ref = refs[2 * count + 1 :]
    h2, w2, n, c = g_ref.shape
    size = blocks[0].shape[0]
    t = pl.program_id(0)
    dy, dx = lax.div(t, 3), lax.rem(t, 3)

    @pl.when(t == 0)
    def _():
        pad_ref[...] = jnp.zeros_like(pad_ref)
        pad_ref[1 : h2 + 1, 1 : w2 + 1] = g_ref[...]
        acc_ref[...] = jnp.zeros_like(acc_ref)

    shifted = pad_ref[pl.ds(2 - dy, h2), pl.ds(2 - dx, w2)].astype(f32)
    pooled = flat(sum_two(shifted)).astype(bf16)
    for k in range(count):
        rows = owned_rows(row_ref, k, size)
        acc_ref[k] += contract_last(pooled, w_ref[0, rows, :])
        out_ref[0, rows, :] = times(blocks[k][...], pooled).astype(bf16)

    @pl.when(t == 8)
    def _():
        for k in range(count):
            outs[k][...] = acc_ref[k].astype(bf16)


def back_one(row, grads, weight, blocks):
    h2, w2, n, c = grads.shape
    count = len(blocks)
    size, rows = blocks[0].shape
    return pl.pallas_call(
        functools.partial(back_one_kernel, count),
        out_shape=(jax.ShapeDtypeStruct((9, count * size, c), bf16),)
        + tuple(jax.ShapeDtypeStruct((rows, size), bf16) for _ in range(count)),
        grid_spec=pltpu.PrefetchScalarGridSpec(
            num_scalar_prefetch=1,
            grid=(9,),
            in_specs=[
                whole(grads.shape),
                pl.BlockSpec((1,) + weight.shape[1:], lambda t, r: (t, 0, 0)),
            ]
            + [whole(b.shape) for b in blocks],
            out_specs=(pl.BlockSpec((1, count * size, c), lambda t, r: (t, 0, 0)),)
            + tuple(whole((rows, size)) for _ in range(count)),
            scratch_shapes=[
                pltpu.VMEM((h2 + 2, w2 + 2, n, c), bf16),
                pltpu.VMEM((count, rows, size), f32),
            ],
        ),
        compiler_params=kernel_params(28),
        name="back_one",
    )(row, grads, weight, *blocks)


def in_order(pieces, axis_name):
    piled = jnp.stack(pieces, axis=0)
    r = lax.axis_index(axis_name)
    return jnp.concatenate(
        [
            lax.dynamic_index_in_dim(piled, lax.bitwise_xor(r, j), 0, keepdims=False)
            for j in range(len(pieces))
        ],
        axis=0,
    )


def gram_share(owned, pieces):
    blocks = [
        lax.dot_general(piece, owned, (((0,), (0,)), ((), ())), preferred_element_type=f32)
        for piece in pieces
    ]
    return in_order(blocks, "row")


def gram_whole(panel):
    n = lax.axis_size("dp")
    h, z = lax.axis_index("half"), lax.axis_index("dp")
    total = group_sum_wide(panel)
    pieces = row_gather(total)
    piled = jnp.stack(pieces, axis=0)
    r = lax.axis_index("row")
    return jnp.concatenate(
        [
            lax.dynamic_index_in_dim(piled, lax.bitwise_xor(r, j), 0, keepdims=False)
            for j in range(len(pieces))
        ],
        axis=1,
    )


def group_sum_wide(value):
    return group_gather(group_scatter(value))


def mul(left, right):
    return jnp.dot(left, right, precision=high, preferred_element_type=f32)


def newton_columns(gram, own):
    scale = lax.rsqrt(jnp.trace(gram) + NEWTON_EPSILON)
    current = gram * (scale * scale)
    identity = jnp.eye(gram.shape[0], dtype=f32)
    maps = []
    for iteration in range(NS_ITERS):
        square = mul(current, current)
        mapping = NS_COEF[0] * identity + NS_COEF[1] * current + NS_COEF[2] * square
        maps.append(mapping)
        if iteration < NS_ITERS - 1:
            current = mul(mapping, mul(current, mapping))
    start = lax.axis_index("row") * own
    columns = lax.dynamic_slice_in_dim(maps[-1], start, own, 1)
    for mapping in maps[-2::-1]:
        columns = mul(mapping, columns)
    return columns * scale


def muon(master, moment, gradient, groups):
    moment_new = MOMENTUM * moment + gradient
    owned = moment_new.astype(bf16)
    pieces = row_gather(owned)
    own = owned.shape[1]
    gram = gram_whole(gram_share(owned, pieces))
    columns = newton_columns(gram, own).astype(bf16)
    r = lax.axis_index("row")
    direction = sum(
        times(
            piece,
            lax.dynamic_slice_in_dim(columns, lax.bitwise_xor(r, k) * own, own, 0),
        )
        for k, piece in enumerate(pieces)
    )
    factor = 0.2 * math.sqrt(max(master.shape[0] * groups, own * len(pieces)))
    return master - MUON_RATE * (factor * direction + DECAY * master), moment_new


def transposed(values):
    return jnp.transpose(values.astype(f32)).astype(values.dtype)


def place_kernel(count, sizes, index_ref, mine_ref, other_ref, *refs):
    outs = refs[-len(sizes) :]

    def write(values):
        turned = jnp.transpose(values.astype(f32)).astype(bf16)
        start = 0
        for size, out_ref in zip(sizes, outs):
            out_ref[...] = turned[start : start + size]
            start += size

    @pl.when(pl.program_id(0) < count)
    def _():
        write(mine_ref[0])

    @pl.when(pl.program_id(0) >= count)
    def _():
        write(other_ref[0])


def place(held, index, mine, other, sizes):
    count, c, wide = mine.shape
    groups = 2 * lax.axis_size("dp")
    given = [] if held is None else list(held)
    return pl.pallas_call(
        functools.partial(place_kernel, count, sizes),
        out_shape=tuple(jax.ShapeDtypeStruct((groups * size, c), bf16) for size in sizes),
        grid_spec=pltpu.PrefetchScalarGridSpec(
            num_scalar_prefetch=1,
            grid=(2 * count,),
            in_specs=[
                pl.BlockSpec((1, c, wide), lambda t, r: (jnp.minimum(t, count - 1), 0, 0)),
                pl.BlockSpec((1, c, wide), lambda t, r: (jnp.maximum(t - count, 0), 0, 0)),
            ]
            + [pl.BlockSpec(memory_space=pl.ANY) for _ in given],
            out_specs=tuple(pl.BlockSpec((size, c), lambda t, r: (r[t], 0)) for size in sizes),
        ),
        input_output_aliases={3 + i: i for i in range(len(given))},
        compiler_params=kernel_params(),
        name="place",
    )(jnp.stack(index).astype(jnp.int32), mine, other, *given)


def place_cores(held, spots, mine, sizes):
    n = lax.axis_size("dp")
    h = lax.axis_index("half")
    index = [h * n + spot for spot in spots] + [(1 - h) * n + spot for spot in spots]
    return place(held, index, mine, axis_swap(mine, "half", 1), sizes)


def weight_one_kernel(groups, where_ref, inverse_ref, *refs):
    pieces = refs[:groups]
    all_ref, moment_ref, out_ref, low_ref, pad_ref, pool_ref, grads, inputs_ref, sem = refs[groups:]
    copies = [
        pltpu.make_async_copy(piece, grads.at[g], sem.at[g]) for g, piece in enumerate(pieces)
    ]
    copies.append(pltpu.make_async_copy(all_ref, inputs_ref, sem.at[groups]))
    for copy in copies:
        copy.start()
    h2, w2, n, c = grads.shape[1:]
    size = h2 * w2 * n // 4
    row, d = where_ref[0], where_ref[1] * (groups // 2) + where_ref[2]
    owners = []
    for side in range(2):
        for k in range(groups // 2):
            spot = lax.rem(where_ref[2] + groups // 2 - k, groups // 2)
            owners.append((where_ref[1] if side == 0 else 1 - where_ref[1]) * (groups // 2) + spot)
    pad_ref[...] = jnp.zeros_like(pad_ref)
    for g in range(groups):
        copies[g].wait()
        pad_ref[1 : h2 + 1, 1 : w2 + 1] = grads[g]
        for j in range(2):
            dy, dx = lax.div(d + j, 3), lax.rem(d + j, 3)
            shifted = pad_ref[pl.ds(2 - dy, h2), pl.ds(2 - dx, w2)].astype(f32)
            pool_ref[j, g * size : (g + 1) * size, :] = flat(sum_two(shifted)).astype(bf16)
    copies[groups].wait()
    inverse = inverse_ref[0, 0]
    for q in range(groups + 1):
        i = lax.rem(d + q, groups)
        j = lax.div(d + q, groups)
        start = lax.bitwise_xor(row, lax.div(i, 2)) * (2 * c) + lax.rem(i, 2) * c
        start = pl.multiple_of(start, c)
        total = sum(
            times(inputs_ref[owners[g], pl.ds(start, c), :], pool_ref[j, g * size : (g + 1) * size, :])
            for g in range(groups)
        )
        span = slice(q * c, (q + 1) * c)
        moment = MOMENTUM * moment_ref[:, span] + jnp.transpose(total) * inverse
        out_ref[:, span] = moment
        low_ref[:, span] = moment.astype(bf16)


def weight_one_moment(where, inverse, grads, inputs, moment):
    h2, w2, n, c = grads[0].shape
    groups = len(grads)
    vmem = pl.BlockSpec(memory_space=pltpu.VMEM)
    smem = pl.BlockSpec(memory_space=pltpu.SMEM)
    flops = 2 * moment.shape[1] * c * groups * h2 * w2 * n // 4
    return pl.pallas_call(
        functools.partial(weight_one_kernel, groups),
        out_shape=(
            jax.ShapeDtypeStruct(moment.shape, f32),
            jax.ShapeDtypeStruct(moment.shape, bf16),
        ),
        in_specs=[smem, smem] + [pl.BlockSpec(memory_space=pl.ANY)] * (groups + 1) + [vmem],
        out_specs=(vmem, vmem),
        scratch_shapes=[
            pltpu.VMEM((h2 + 2, w2 + 2, n, c), bf16),
            pltpu.VMEM((2, groups * h2 * w2 * n // 4, c), bf16),
            pltpu.VMEM((groups,) + grads[0].shape, bf16),
            pltpu.VMEM(inputs.shape, bf16),
            pltpu.SemaphoreType.DMA((groups + 1,)),
        ],
        compiler_params=kernel_params(28),
        cost_estimate=pl.CostEstimate(flops=4 * flops, bytes_accessed=0, transcendentals=0),
        name="weight_one",
    )(where, inverse, *grads, inputs, moment)


def weight_pack_kernel(count, row_ref, gpad_ref, *refs):
    blocks, raws, (out_ref, tall_ref) = refs[:count], refs[count : 2 * count], refs[2 * count :]
    h2, w2, n, c = (gpad_ref.shape[0] - 2, gpad_ref.shape[1] - 2) + gpad_ref.shape[2:]
    groups = out_ref.shape[0]
    unit = count * c // groups
    half = unit // 2
    t = pl.program_id(0)
    dy, dx = lax.div(t, 3), lax.rem(t, 3)
    shifted = flat(gpad_ref[pl.ds(2 - dy, h2), pl.ds(2 - dx, w2)])
    for k in range(count):
        tall_ref[owned_rows(row_ref, k, c), :] = times(blocks[k][...], shifted)
    for i in range(groups):
        rows = tall_ref[i * unit : (i + 1) * unit, :]
        u = groups * t + i
        packed = jnp.concatenate([rows[:half], rows[half:]], axis=1).astype(bf16)
        spot = pl.multiple_of(lax.rem(u, groups + 1) * half, half)
        out_ref[lax.div(u, groups + 1), pl.ds(spot, half), :] = packed

    @pl.when(t == 8)
    def _():
        phases = gpad_ref[1 : h2 + 1, 1 : w2 + 1].reshape(h2 // 2, 2, w2 // 2, 2, n, c)
        size = raws[0].shape[0]
        each = count * size // groups
        for k in range(count):
            block = sum(
                times(raws[k][...], flat(phases[:, a, :, b])) for a in range(2) for b in range(2)
            )
            for m in range(size // each):
                rows = block[m * each : (m + 1) * each]
                packed = jnp.concatenate([rows[: each // 2], rows[each // 2 :]], axis=1)
                spot = lax.bitwise_xor(row_ref[0], k) * (size // each) + m
                out_ref[spot, (groups + 1) * half :, :] = packed.astype(bf16)


def weight_pack(row, gpad, blocks, raws, groups):
    c = gpad.shape[-1]
    count = len(blocks)
    tall, wide = count * blocks[0].shape[0], count * raws[0].shape[0]
    shape = (groups, (9 * tall + wide) // (2 * groups), 2 * c)
    flops = 2 * 9 * tall * c * blocks[0].shape[1]
    return pl.pallas_call(
        functools.partial(weight_pack_kernel, count),
        out_shape=jax.ShapeDtypeStruct(shape, bf16),
        grid_spec=pltpu.PrefetchScalarGridSpec(
            num_scalar_prefetch=1,
            grid=(9,),
            in_specs=[whole(gpad.shape)] + [whole(b.shape) for b in blocks + raws],
            out_specs=whole(shape),
            scratch_shapes=[pltpu.VMEM((tall, c), f32)],
        ),
        compiler_params=kernel_params(28),
        cost_estimate=pl.CostEstimate(flops=3 * flops, bytes_accessed=0, transcendentals=0),
        name="weight_two",
    )(row, gpad, *blocks, *raws)


def moments_kernel(count, inverse_ref, *refs):
    pieces = refs[:count]
    tall_ref, skip_ref, tall_out, skip_out, low_ref = refs[count:]
    c, size = tall_ref.shape
    total = pieces[0][...].astype(f32)
    for piece in pieces[1:]:
        total = total + piece[...].astype(f32)
    total = total * inverse_ref[0, 0]
    units = 9
    half = size // (2 * units)
    for q in range(units):
        rows = total[q * half : (q + 1) * half]
        rows = jnp.concatenate([rows[:, :c], rows[:, c:]], axis=0)
        span = slice(2 * q * half, 2 * (q + 1) * half)
        moment = MOMENTUM * tall_ref[:, span] + jnp.transpose(rows)
        tall_out[:, span] = moment
        low_ref[:, span] = moment.astype(bf16)
    rows = total[units * half :]
    rows = jnp.concatenate([rows[:, :c], rows[:, c:]], axis=0)
    moment = MOMENTUM * skip_ref[...] + jnp.transpose(rows)
    skip_out[...] = moment
    low_ref[:, size:] = moment.astype(bf16)


def moments_two(inverse, pieces, tall, skip):
    vmem = pl.BlockSpec(memory_space=pltpu.VMEM)
    return pl.pallas_call(
        functools.partial(moments_kernel, len(pieces)),
        out_shape=(
            jax.ShapeDtypeStruct(tall.shape, f32),
            jax.ShapeDtypeStruct(skip.shape, f32),
            jax.ShapeDtypeStruct((tall.shape[0], tall.shape[1] + skip.shape[1]), bf16),
        ),
        in_specs=[pl.BlockSpec(memory_space=pltpu.SMEM)] + [vmem] * (len(pieces) + 2),
        out_specs=(vmem, vmem, vmem),
        compiler_params=kernel_params(),
        name="moments",
    )(inverse, *pieces, tall, skip)


def gram_kernel(count, spans, row_ref, *refs):
    pieces, out_ref, hold_ref = refs[:count], refs[count], refs[count + 1]
    for m, (start, stop) in enumerate(spans):
        owned = pieces[0][:, start:stop]
        for k in range(count):
            hold_ref[k] = contract_last(owned, pieces[k][:, start:stop])
        out_ref[m] = jnp.concatenate(
            [hold_ref[lax.bitwise_xor(row_ref[0], j)] for j in range(count)], axis=1
        )


def gram_rows(row, pieces, spans):
    c = pieces[0].shape[0]
    count = len(pieces)
    vmem = pl.BlockSpec(memory_space=pltpu.VMEM)
    return pl.pallas_call(
        functools.partial(gram_kernel, count, spans),
        out_shape=jax.ShapeDtypeStruct((len(spans), c, count * c), f32),
        in_specs=[pl.BlockSpec(memory_space=pltpu.SMEM)] + [vmem] * count,
        out_specs=vmem,
        scratch_shapes=[pltpu.VMEM((count, c, c), f32)],
        compiler_params=kernel_params(),
        cost_estimate=pl.CostEstimate(
            flops=6 * count * c * c * pieces[0].shape[1], bytes_accessed=0, transcendentals=0
        ),
        name="gram",
    )(row, *pieces)


def gram_terms(halves):
    kept = near_halves(halves)
    return near_blocks(kept, kept)


def gram_total(terms):
    return placed_in_order(straight(sum(terms)))


def newton_kernel(count, sides, where_ref, *refs):
    pieces = refs[: sides * count]
    out_ref, a_ref, ah, al, ph, pl_low, th, tl = refs[sides * count :]
    size = a_ref.shape[0]
    own = size // count
    block = size // 3
    row, h = where_ref[0], where_ref[1]
    for q in range(count):
        for side in range(sides):
            piece = pieces[side * count + q]
            s = piece.shape[2]
            half = 0 if sides == 1 else (h if side == 0 else 1 - h)
            for p in range(piece.shape[0]):
                start = lax.bitwise_xor(row, q) * own + half * (own // 2) + p * s
                a_ref[pl.ds(pl.multiple_of(start, s), s), :] = piece[p, 0]

    def eye(shape, offset):
        rows = lax.broadcasted_iota(jnp.int32, shape, 0) + offset
        return rows == lax.broadcasted_iota(jnp.int32, shape, 1)

    whole_gram = a_ref[...]
    trace = jnp.sum(jnp.where(eye(whole_gram.shape, 0), whole_gram, 0.0), keepdims=True)
    scale = lax.rsqrt(trace + NEWTON_EPSILON)
    a_ref[...] = whole_gram * (scale * scale)

    def split(values):
        top = values.astype(bf16)
        return top, (values - top.astype(f32)).astype(bf16)

    def three(xh, xl, yh, yl):
        return times(xh, yh) + (times(xh, yl) + times(xl, yh))

    spans = [slice(i * block, (i + 1) * block) for i in range(3)]

    def symmetric(xh, xl, yh, yl, write):
        for i in range(3):
            for j in range(i, 3):
                a, b = spans[i], spans[j]
                value = three(xh[a, :], xl[a, :], yh[:, b], yl[:, b])
                write(i, j, value)

    def store(high_ref, low_ref, i, j, value):
        top, low = split(value)
        high_ref[spans[i], spans[j]] = top
        low_ref[spans[i], spans[j]] = low
        if i != j:
            turned = jnp.transpose(value)
            top, low = split(turned)
            high_ref[spans[j], spans[i]] = top
            low_ref[spans[j], spans[i]] = low

    top, low = split(a_ref[...])
    ah[...] = top
    al[...] = low

    def step(k, carry):
        hp, lp = ph.at[k], pl_low.at[k]

        def write_map(i, j, value):
            value = NS_COEF[1] * a_ref[spans[i], spans[j]] + NS_COEF[2] * value
            if i == j:
                value = value + jnp.where(eye(value.shape, 0), NS_COEF[0], 0.0)
            store(hp, lp, i, j, value)

        symmetric(ah, al, ah, al, write_map)
        symmetric(ah, al, hp, lp, functools.partial(store, th, tl))

        def write_gram(i, j, value):
            a_ref[spans[i], spans[j]] = value
            store(ah, al, i, j, value)
            if i != j:
                a_ref[spans[j], spans[i]] = jnp.transpose(value)

        symmetric(hp, lp, th, tl, write_gram)
        return carry

    lax.fori_loop(0, NS_ITERS - 1, step, 0)
    mine = pl.ds(pl.multiple_of(row * own, own), own)
    last = a_ref[mine, :]
    columns = NS_COEF[1] * last + NS_COEF[2] * three(ah[mine, :], al[mine, :], ah[...], al[...])
    columns = columns + jnp.where(eye(columns.shape, row * own), NS_COEF[0], 0.0)

    def fold(k, columns):
        high_part, low_part = split(columns)
        k = NS_ITERS - 2 - k
        return three(high_part, low_part, ph[k], pl_low[k])

    columns = lax.fori_loop(0, NS_ITERS - 1, fold, columns) * scale
    for j in range(count):
        out_ref[0, j] = columns[:, j * own : (j + 1) * own].astype(bf16)


def newton(where, pieces, count):
    sides = len(pieces) // count
    n, m, s, size = pieces[0].shape
    own = size // count
    square = (size, size)
    maps = (NS_ITERS - 1,) + square
    return pl.pallas_call(
        functools.partial(newton_kernel, count, sides),
        out_shape=jax.ShapeDtypeStruct((m, count, own, own), bf16),
        grid_spec=pltpu.PrefetchScalarGridSpec(
            num_scalar_prefetch=1,
            grid=(m,),
            in_specs=[pl.BlockSpec((n, 1, s, size), lambda t, r: (0, t, 0, 0)) for _ in pieces],
            out_specs=pl.BlockSpec((1, count, own, own), lambda t, r: (t, 0, 0, 0)),
            scratch_shapes=[
                pltpu.VMEM(square, f32),
                pltpu.VMEM(square, bf16),
                pltpu.VMEM(square, bf16),
                pltpu.VMEM(maps, bf16),
                pltpu.VMEM(maps, bf16),
                pltpu.VMEM(square, bf16),
                pltpu.VMEM(square, bf16),
            ],
        ),
        compiler_params=kernel_params(36),
        cost_estimate=pl.CostEstimate(
            flops=m * 64 * size**3, bytes_accessed=0, transcendentals=0
        ),
        name="newton",
    )(where, *pieces)


def update_kernel(count, spans, factors, row_ref, map_ref, *refs):
    pieces, masters, outs = refs[:count], refs[count : count + len(spans)], refs[count + len(spans) :]
    for m, (start, stop) in enumerate(spans):
        direction = sum(
            times(map_ref[m, lax.bitwise_xor(row_ref[0], k)], pieces[k][:, start:stop])
            for k in range(count)
        )
        master = masters[m][...]
        outs[m][...] = master - MUON_RATE * (factors[m] * direction + DECAY * master)


def update(row, maps, pieces, masters, spans, factors):
    count = len(pieces)
    vmem = pl.BlockSpec(memory_space=pltpu.VMEM)
    return pl.pallas_call(
        functools.partial(update_kernel, count, spans, factors),
        out_shape=tuple(jax.ShapeDtypeStruct(master.shape, f32) for master in masters),
        in_specs=[pl.BlockSpec(memory_space=pltpu.SMEM)] + [vmem] * (1 + count + len(masters)),
        out_specs=(vmem,) * len(masters),
        compiler_params=kernel_params(),
        name="update",
    )(row, maps, *pieces, *masters)


def back_in_kernel(count, row_ref, g_ref, w_ref, *refs):
    outs, (pad_ref, acc_ref) = refs[:count], refs[count:]
    h2, w2, n, c = g_ref.shape
    size = outs[0].shape[1]
    t = pl.program_id(0)
    dy, dx = lax.div(t, 3), lax.rem(t, 3)

    @pl.when(t == 0)
    def _():
        pad_ref[...] = jnp.zeros_like(pad_ref)
        pad_ref[1 : h2 + 1, 1 : w2 + 1] = g_ref[...]
        acc_ref[...] = jnp.zeros_like(acc_ref)

    shifted = pad_ref[pl.ds(2 - dy, h2), pl.ds(2 - dx, w2)].astype(f32)
    pooled = flat(sum_two(shifted)).astype(bf16)
    for k in range(count):
        acc_ref[k] += contract_last(pooled, w_ref[0, owned_rows(row_ref, k, size), :])

    @pl.when(t == 8)
    def _():
        for k in range(count):
            outs[k][...] = acc_ref[k].astype(bf16)


def back_in(row, grads, weight, count):
    h2, w2, n, c = grads.shape
    size, rows = weight.shape[1] // count, h2 * w2 * n // 4
    return pl.pallas_call(
        functools.partial(back_in_kernel, count),
        out_shape=tuple(jax.ShapeDtypeStruct((rows, size), bf16) for _ in range(count)),
        grid_spec=pltpu.PrefetchScalarGridSpec(
            num_scalar_prefetch=1,
            grid=(9,),
            in_specs=[
                whole(grads.shape),
                pl.BlockSpec((1,) + weight.shape[1:], lambda t, r: (t, 0, 0)),
            ],
            out_specs=tuple(whole((rows, size)) for _ in range(count)),
            scratch_shapes=[
                pltpu.VMEM((h2 + 2, w2 + 2, n, c), bf16),
                pltpu.VMEM((count, rows, size), f32),
            ],
        ),
        compiler_params=kernel_params(28),
        cost_estimate=pl.CostEstimate(
            flops=6 * 9 * rows * count * size * c, bytes_accessed=0, transcendentals=0
        ),
        name="back_one",
    )(row, grads, weight)


def adam_update(weight, gradient, mean_old, square_old, rate):
    mean_new = BETA_ONE * mean_old + (1.0 - BETA_ONE) * gradient
    square_new = BETA_TWO * square_old + (1.0 - BETA_TWO) * gradient * gradient
    ratio = (
        mean_new
        / (1.0 - BETA_ONE**STEP)
        / (jnp.sqrt(square_new / (1.0 - BETA_TWO**STEP)) + ADAM_EPS)
    )
    return (weight - rate * (ratio + DECAY * weight), mean_new, square_new)


def moments_of(totals, count):
    centre = totals[:MICRO] / count
    return centre, lax.rsqrt(totals[MICRO:] / count - centre * centre + BN_EPS)


def per_image(values, n):
    return jnp.repeat(values, n // MICRO, axis=0)


def per_micro(values):
    return jnp.sum(values.reshape(MICRO, -1, values.shape[-1]), axis=1)


def wide_device(
    features,
    noise,
    labels,
    counted,
    disc_first,
    disc_second,
    disc_skip,
    disc_head,
    disc_table,
    conv_first,
    conv_second,
    conv_skip,
    momentum_first,
    momentum_second,
    momentum_skip,
    class_table,
    table_mean,
    table_square,
    norm_first,
    first_mean,
    first_square,
    norm_second,
    second_mean,
    second_square,
    colour_conv,
    colour_mean,
    colour_square,
):
    groups = lax.axis_size("half") * lax.axis_size("dp")
    ranks = lax.axis_size("row")
    row = lax.axis_index("row").astype(jnp.int32).reshape(1)
    n, h, w, c_in = features.shape
    c_out = conv_first.shape[1]
    count_low = float(n // MICRO * h * w * groups)
    count_high = 4.0 * count_low

    inputs = jnp.transpose(features, (1, 2, 0, 3))
    raw = inputs.astype(f32)
    sums_low = jnp.concatenate(
        [per_micro(jnp.sum(raw, axis=(0, 1))), per_micro(jnp.sum(raw * raw, axis=(0, 1)))], axis=0
    )
    totals_low = group_sum(sums_low)
    weight_one = group_gather(conv_first.astype(bf16)).reshape(9, ranks * c_in, c_out)

    onehot = (labels[:, None] == jnp.arange(NCLS)[None, :]).astype(f32)
    conds = jnp.concatenate([jnp.dot(onehot, class_table, precision=highest), noise], axis=1)
    class_disc = jnp.dot(onehot, disc_table, precision=highest)
    mods_one = jnp.einsum("bk,kgc->bgc", conds, norm_first, precision=highest)
    mods_two = jnp.einsum("bk,kgc->bgc", conds, norm_second, precision=highest)

    centre_one, spread_one = moments_of(totals_low, count_low)
    centre_one, spread_one = per_image(centre_one, n), per_image(spread_one, n)
    gain_one, gain_two = 1.0 + mods_one[:, 0], 1.0 + mods_two[:, 0]
    normed_one = (raw - centre_one) * spread_one
    pre_one = normed_one * gain_one + mods_one[:, 1]
    acted_one = flat(jax.nn.silu(pre_one).astype(bf16))
    ones = row_gather(acted_one)
    raws = row_gather(flat(inputs))

    hidden, sums_high = conv_one(row, [one[None] for one in ones], weight_one, (h, w, n))
    held_second, held_skip, _ = lax.optimization_barrier(
        (conv_second.astype(bf16), conv_skip.astype(bf16), weight_one[0, 0, 0])
    )
    weight_skip = group_gather(held_skip)
    weight_two = group_gather(held_second).reshape(9, ranks * c_out, c_out)
    totals_high = group_sum(sums_high)
    centre_two, spread_two = moments_of(totals_high, count_high)
    centre_two, spread_two = per_image(centre_two, n), per_image(spread_two, n)
    normed_two = (hidden - centre_two) * spread_two
    pre_two = normed_two * gain_two + mods_two[:, 1]
    acted_two = jax.nn.silu(pre_two).astype(bf16)
    twos = row_gather(acted_two)

    colour = jnp.pad(
        jnp.transpose(colour_conv, (0, 2, 1)).astype(bf16), ((0, 0), (0, PAD - 3), (0, 0))
    )
    summed, active, picture = conv_two(row, twos, [one[None] for one in raws], weight_two, weight_skip, colour)
    picture = row_sum(picture)

    first_taps = jnp.pad(disc_first.reshape(9, 3, -1), ((0, 0), (0, PAD - 3), (0, 0)))
    second_taps = disc_second.reshape(9, -1, disc_second.shape[-1])
    skip_taps = jnp.pad(disc_skip, ((0, PAD - 3), (0, 0)))
    mark = counted.astype(f32)[:, None]
    grads, loss_part = critic(
        picture,
        first_taps,
        second_taps,
        skip_taps,
        disc_head[None, :] + class_disc,
        mark,
        (2 * h, 2 * w, n),
    )
    colour_rows = jnp.pad(colour.reshape(9 * PAD, c_out), ((0, 128 - 9 * PAD), (0, 0)))
    backs = back_two(row, grads, summed, active, colour_rows, weight_two, ranks)
    gpad, grad_colour, pieces = backs[0], backs[1], backs[2:]
    grad_two, grad_skip = weight_two_grads(row, gpad, twos, raws)
    grad_acted_two = row_scatter(list(pieces)).reshape(hidden.shape)

    grad_pre_two = grad_acted_two * silu_slope(pre_two)
    gains_two = jnp.sum(grad_pre_two * normed_two, axis=(0, 1))
    shifts_two = jnp.sum(grad_pre_two, axis=(0, 1))
    back_sums = group_sum(
        jnp.concatenate([per_micro(gain_two * shifts_two), per_micro(gain_two * gains_two)], axis=0)
    )
    mean_g = per_image(back_sums[:MICRO] / count_high, n)
    mean_gy = per_image(back_sums[MICRO:] / count_high, n)
    grad_hidden = (spread_two * (grad_pre_two * gain_two - mean_g - normed_two * mean_gy)).astype(
        bf16
    )
    ones_turned = [jnp.transpose(one) for one in ones]
    backs = back_one(row, grad_hidden, weight_one, ones_turned)
    grad_one, pieces = flat(backs[0]), backs[1:]
    grad_acted_one = row_scatter(list(pieces)).reshape(raw.shape)
    grad_pre_one = grad_acted_one * silu_slope(pre_one)
    gains_one = jnp.sum(grad_pre_one * normed_one, axis=(0, 1))
    shifts_one = jnp.sum(grad_pre_one, axis=(0, 1))
    grad_mods_one = jnp.stack([gains_one, shifts_one], axis=1)
    grad_mods_two = jnp.stack([gains_two, shifts_two], axis=1)

    grad_cond = jnp.einsum("bgc,kgc->bk", grad_mods_one, norm_first[:EMB], precision=highest)
    grad_cond = grad_cond + jnp.einsum(
        "bgc,kgc->bk", grad_mods_two, norm_second[:EMB], precision=highest
    )
    grad_cond = row_sum(grad_cond)

    count_part = jnp.sum(counted).astype(f32)
    small = jnp.concatenate(
        [
            grad_colour[: 9 * PAD],
            jnp.broadcast_to(loss_part[:1, :1], (1, c_out)),
            jnp.broadcast_to(count_part, (1, c_out)),
        ],
        axis=0,
    )
    small = group_sum(small)
    loss_sum, fake_count = small[9 * PAD, 0], small[9 * PAD + 1, 0]
    inverse = 1.0 / fake_count
    g_colour = jnp.transpose(small[: 9 * PAD].reshape(9, PAD, c_out)[:, :3], (0, 2, 1))

    known = group_pile(jnp.concatenate([conds, labels.astype(f32)[:, None]], axis=1))
    found = group_pile(
        jnp.concatenate(
            [grad_mods_one.reshape(n, -1), grad_mods_two.reshape(n, -1), grad_cond], axis=1
        )
    )
    conds_all, labels_all = known[:, :-1], known[:, -1].astype(jnp.int32)
    onehot_all = (labels_all[:, None] == jnp.arange(NCLS)[None, :]).astype(f32)
    cut_one, cut_two = 2 * c_in, 2 * c_in + 2 * c_out
    g_norm = lax.dot_general(
        conds_all,
        found[:, :cut_two],
        (((0,), (0,)), ((), ())),
        precision=highest,
        preferred_element_type=f32,
    )
    g_norm_one = g_norm[:, :cut_one].reshape(norm_first.shape)
    g_norm_two = g_norm[:, cut_one:].reshape(norm_second.shape)
    g_table = lax.dot_general(
        onehot_all,
        found[:, cut_two:],
        (((0,), (0,)), ((), ())),
        precision=highest,
        preferred_element_type=f32,
    )

    shares = [group_scatter(flat(g)) for g in (grad_one, grad_two, grad_skip)]
    muons = [
        muon(master, moment, share * inverse, groups)
        for master, moment, share in zip(
            (conv_first, conv_second, conv_skip),
            (momentum_first, momentum_second, momentum_skip),
            shares,
        )
    ]
    table_new = adam_update(class_table, g_table * inverse, table_mean, table_square, ADAM_RATE)
    first_new = adam_update(norm_first, g_norm_one * inverse, first_mean, first_square, ADAM_RATE)
    second_new = adam_update(
        norm_second, g_norm_two * inverse, second_mean, second_square, ADAM_RATE
    )
    colour_new = adam_update(
        colour_conv, g_colour * inverse, colour_mean, colour_square, COLOUR_RATE
    )
    return (
        (loss_sum, fake_count)
        + tuple(m[0] for m in muons)
        + tuple(m[1] for m in muons)
        + table_new
        + first_new
        + second_new
        + colour_new
    )


def near_device(
    features,
    noise,
    labels,
    counted,
    disc_first,
    disc_second,
    disc_skip,
    disc_head,
    disc_table,
    conv_first,
    conv_second,
    conv_skip,
    momentum_first,
    momentum_second,
    momentum_skip,
    class_table,
    table_mean,
    table_square,
    norm_first,
    first_mean,
    first_square,
    norm_second,
    second_mean,
    second_square,
    colour_conv,
    colour_mean,
    colour_square,
):
    groups = lax.axis_size("half") * lax.axis_size("dp")
    ranks = lax.axis_size("row")
    row = lax.axis_index("row").astype(jnp.int32).reshape(1)
    n, h, w, c_in = features.shape
    c_out = conv_first.shape[1]
    count_low = float(n // MICRO * h * w * groups)
    count_high = 4.0 * count_low

    where = jnp.stack(
        [lax.axis_index("row"), lax.axis_index("half"), lax.axis_index("dp")]
    ).astype(jnp.int32)
    n_dp, half, spot = lax.axis_size("dp"), lax.axis_index("half"), lax.axis_index("dp")
    turned = conv_first.T.astype(bf16)
    below, above = [turned, step_below(turned, 1)], [turned, step_above(turned, 1)]
    inputs = jnp.transpose(features, (1, 2, 0, 3))
    raw = inputs.astype(f32)
    sums_low = jnp.concatenate(
        [
            per_micro(jnp.sum(raw, axis=(0, 1))),
            per_micro(jnp.sum(raw * raw, axis=(0, 1))),
            jnp.broadcast_to(jnp.sum(counted).astype(f32), (1, c_in)),
        ],
        axis=0,
    )
    totals_low = near_sum(sums_low)
    below.append(step_below(below[1], 2))
    above.append(step_above(above[1], 2))
    fake_count = totals_low[2 * MICRO, 0]
    inverse = 1.0 / fake_count

    onehot = (labels[:, None] == jnp.arange(NCLS)[None, :]).astype(f32)
    conds = jnp.concatenate([jnp.dot(onehot, class_table, precision=highest), noise], axis=1)
    class_disc = jnp.dot(onehot, disc_table, precision=highest)
    mods_one = jnp.einsum("bk,kgc->bgc", conds, norm_first, precision=highest)
    mods_two = jnp.einsum("bk,kgc->bgc", conds, norm_second, precision=highest)

    centre_one, spread_one = moments_of(totals_low[: 2 * MICRO], count_low)
    centre_one, spread_one = per_image(centre_one, n), per_image(spread_one, n)
    gain_one, gain_two = 1.0 + mods_one[:, 0], 1.0 + mods_two[:, 0]
    normed_one = (raw - centre_one) * spread_one
    pre_one = normed_one * gain_one + mods_one[:, 1]
    acted_one = flat(jax.nn.silu(pre_one).astype(bf16))
    pairs = row_gather(jnp.stack([acted_one, flat(inputs)], axis=0))
    sizes = (conv_first.shape[0],)
    down, up = lax.rem(spot + 3, 4), lax.rem(spot + 1, 4)
    held = place_cores(None, [spot, down, up], jnp.stack([turned, below[1], above[1]]), sizes)
    below.append(step_below(after(below[2], *pairs), 3))
    above.append(step_above(after(above[2], *pairs), 3))
    middle = jnp.where(spot >= 2, below[2], above[2])
    held = place_cores(held, [lax.rem(spot + 2, 4)], middle[None], sizes)
    below[3], above[3] = after(below[3], *held), after(above[3], *held)
    last = jnp.where(spot == 3, below[3], jnp.where(spot == 0, above[3], turned))
    end = jnp.where(spot == 3, 0, jnp.where(spot == 0, 3, spot))
    (weight_one,) = place_cores(held, [end], last[None], sizes)
    weight_one = weight_one.reshape(9, ranks * c_in, c_out)

    hidden, sums_high = conv_one(row, pairs, weight_one, (h, w, n))
    other = jnp.concatenate([conv_second.T, conv_skip.T], axis=1).astype(bf16)
    other = jnp.pad(other, ((0, 0), (0, -other.shape[1] % 128)))
    others = lax.all_gather(after(other, below[3], above[3]), GROUP, axis=0)
    weight_two, weight_skip = place(
        None,
        list(range(groups)),
        others[: groups // 2],
        others[groups // 2 :],
        (conv_second.shape[0], conv_skip.shape[0]),
    )
    weight_two = weight_two.reshape(9, ranks * c_out, c_out)
    totals_high = near_sum(sums_high)
    centre_two, spread_two = moments_of(totals_high, count_high)
    centre_two, spread_two = per_image(centre_two, n), per_image(spread_two, n)
    normed_two = (hidden - centre_two) * spread_two
    pre_two = normed_two * gain_two + mods_two[:, 1]
    acted_two = jax.nn.silu(pre_two).astype(bf16)
    twos = row_gather(acted_two)
    kept_pairs = [after(pair, sums_high) for pair in pairs]
    turned = jnp.concatenate([jnp.transpose(pair[0]) for pair in kept_pairs], axis=0)
    ones_all = lax.all_gather(after(turned, others), GROUP, axis=0)

    colour = jnp.pad(
        jnp.transpose(colour_conv, (0, 2, 1)).astype(bf16), ((0, 0), (0, PAD - 3), (0, 0))
    )
    summed, active, picture = conv_two(row, twos, pairs, weight_two, weight_skip, colour)
    picture = row_sum(picture)

    first_taps = jnp.pad(disc_first.reshape(9, 3, -1), ((0, 0), (0, PAD - 3), (0, 0)))
    second_taps = disc_second.reshape(9, -1, disc_second.shape[-1])
    skip_taps = jnp.pad(disc_skip, ((0, PAD - 3), (0, 0)))
    mark = counted.astype(f32)[:, None]
    grads, loss_part = critic(
        picture,
        first_taps,
        second_taps,
        skip_taps,
        disc_head[None, :] + class_disc,
        mark,
        (2 * h, 2 * w, n),
    )
    colour_rows = jnp.pad(colour.reshape(9 * PAD, c_out), ((0, 128 - 9 * PAD), (0, 0)))
    backs = back_two(row, grads, summed, active, colour_rows, weight_two, ranks)
    gpad, grad_colour = backs[0], backs[1]
    pieces = row_exchange(list(backs[2:]))
    packed = weight_pack(
        row,
        gpad,
        [jnp.transpose(flat(after(two, active))) for two in twos],
        [jnp.transpose(after(pair, active)[1]) for pair in pairs],
        groups,
    )
    kept = near_halves(packed.reshape((2, groups // 2) + packed.shape[1:]))
    pieces[-1] = after(pieces[-1], packed)
    grad_acted_two = sum(piece.astype(f32) for piece in pieces).reshape(hidden.shape)

    grad_pre_two = grad_acted_two * silu_slope(pre_two)
    gains_two = jnp.sum(grad_pre_two * normed_two, axis=(0, 1))
    shifts_two = jnp.sum(grad_pre_two, axis=(0, 1))
    back_sums = jnp.concatenate(
        [per_micro(gain_two * shifts_two), per_micro(gain_two * gains_two)], axis=0
    )
    back_sums = near_sum(back_sums)
    mean_g = per_image(back_sums[:MICRO] / count_high, n)
    mean_gy = per_image(back_sums[MICRO:] / count_high, n)
    grad_hidden = (spread_two * (grad_pre_two * gain_two - mean_g - normed_two * mean_gy)).astype(
        bf16
    )
    hidden_all = straight(grad_hidden)
    pieces = back_in(row, after(grad_hidden, hidden_all[1]), weight_one, ranks)
    hidden_all = both_cores(hidden_all)
    kept = after(kept, *hidden_all)
    shares = near_blocks(kept, kept.astype(bf16))
    scaled = inverse.reshape(1, 1)
    moment_one, low_one = weight_one_moment(
        where, scaled, hidden_all, ones_all, momentum_first.T
    )
    one_held = row_gather(low_one)
    one_held[1] = after(one_held[1], *shares)
    panel = gram_rows(row, one_held, [(0, conv_first.shape[0])])
    panel = panel.reshape(2, 4, 1, c_out // 8, -1)
    shares[0] = after(shares[0], panel)
    moment_two, moment_skip, low_two = moments_two(
        scaled, shares, momentum_second.T, momentum_skip.T
    )
    total_one = gram_total(gram_terms(panel))
    two_held = row_gather(low_two)
    spans = [(0, conv_second.shape[0]), (conv_second.shape[0], low_two.shape[1])]
    panels = gram_rows(row, [after(two_held[0], total_one)] + two_held[1:], spans)
    total_two = gram_total(gram_terms(panels.reshape(2, 4, 1, c_out // 4, -1)))
    grams_one = both_cores(row_gather(total_one))
    grams_one[0] = after(grams_one[0], total_two)
    maps_one = newton(where, grams_one, ranks)
    factor = 0.2 * math.sqrt(max(conv_first.shape[0] * groups, c_out * ranks))
    (first_out,) = update(
        row, maps_one, one_held, [conv_first.T], [(0, conv_first.shape[0])], [factor]
    )
    grams_two = row_gather(total_two)
    grams_two[0] = after(grams_two[0], maps_one)
    maps_two = newton(where, grams_two, ranks)
    other_map = axis_swap(maps_two, "half", 1)
    maps_two = jnp.where(
        half == 0,
        jnp.concatenate([maps_two, other_map], axis=0),
        jnp.concatenate([other_map, maps_two], axis=0),
    )
    factors = [
        0.2 * math.sqrt(max(rows * groups, c_out * ranks))
        for rows in (conv_second.shape[0], conv_skip.shape[0])
    ]
    second_out, skip_out = update(
        row, maps_two, two_held, [conv_second.T, conv_skip.T], spans, factors
    )
    weights_new = (first_out.T, second_out.T, skip_out.T)
    moments_new = (moment_one.T, moment_two.T, moment_skip.T)
    grad_acted_one = row_scatter(list(pieces)).reshape(raw.shape)
    grad_pre_one = grad_acted_one * silu_slope(pre_one)
    gains_one = jnp.sum(grad_pre_one * normed_one, axis=(0, 1))
    shifts_one = jnp.sum(grad_pre_one, axis=(0, 1))
    grad_mods_one = jnp.stack([gains_one, shifts_one], axis=1)
    grad_mods_two = jnp.stack([gains_two, shifts_two], axis=1)

    grad_cond = jnp.einsum("bgc,kgc->bk", grad_mods_one, norm_first[:EMB], precision=highest)
    grad_cond = grad_cond + jnp.einsum(
        "bgc,kgc->bk", grad_mods_two, norm_second[:EMB], precision=highest
    )
    grad_cond = jnp.sum(spread(after(grad_cond, total_one), ("row",)), axis=0)

    small = jnp.concatenate(
        [
            grad_colour[: 9 * PAD],
            jnp.broadcast_to(loss_part[:1, :1], (1, c_out)),
        ],
        axis=0,
    )

    found = jnp.concatenate(
        [
            grad_mods_one.reshape(n, -1),
            grad_mods_two.reshape(n, -1),
            grad_cond,
            conds,
            labels.astype(f32)[:, None],
        ],
        axis=1,
    )
    found = jnp.pad(found, ((0, 0), (0, -found.shape[1] % 128)))
    wide = found.shape[1]
    extra = small.reshape(-1)
    extra = jnp.pad(extra, (0, -extra.shape[0] % (8 * wide))).reshape(-1, wide)
    packet = spread(after(jnp.concatenate([found, extra], axis=0), total_two), GROUP)
    found = packet[:, :n].reshape(-1, wide)
    small = jnp.sum(packet[:, n:], axis=0).reshape(-1)[: small.size].reshape(small.shape)
    loss_sum = small[9 * PAD, 0]
    g_colour = jnp.transpose(small[: 9 * PAD].reshape(9, PAD, c_out)[:, :3], (0, 2, 1))
    cut = 2 * c_in + 2 * c_out + EMB
    found, known = found[:, :cut], found[:, cut : cut + conds.shape[1] + 1]
    conds_all, labels_all = known[:, :-1], known[:, -1].astype(jnp.int32)
    onehot_all = (labels_all[:, None] == jnp.arange(NCLS)[None, :]).astype(f32)
    cut_one, cut_two = 2 * c_in, 2 * c_in + 2 * c_out
    g_norm = lax.dot_general(
        conds_all,
        found[:, :cut_two],
        (((0,), (0,)), ((), ())),
        precision=highest,
        preferred_element_type=f32,
    )
    g_norm_one = g_norm[:, :cut_one].reshape(norm_first.shape)
    g_norm_two = g_norm[:, cut_one:].reshape(norm_second.shape)
    g_table = lax.dot_general(
        onehot_all,
        found[:, cut_two:],
        (((0,), (0,)), ((), ())),
        precision=highest,
        preferred_element_type=f32,
    )

    table_new = adam_update(class_table, g_table * inverse, table_mean, table_square, ADAM_RATE)
    first_new = adam_update(norm_first, g_norm_one * inverse, first_mean, first_square, ADAM_RATE)
    second_new = adam_update(
        norm_second, g_norm_two * inverse, second_mean, second_square, ADAM_RATE
    )
    colour_new = adam_update(
        colour_conv, g_colour * inverse, colour_mean, colour_square, COLOUR_RATE
    )
    return (
        (loss_sum, fake_count)
        + weights_new
        + moments_new
        + table_new
        + first_new
        + second_new
        + colour_new
    )


def weight_two_grads(row, gpad, twos, raws):
    turned = [jnp.transpose(flat(two)) for two in twos]
    return weight_two(row, gpad, turned, [jnp.transpose(one) for one in raws])


def solution(mesh):
    group = ("half", "dp")
    placed = (
        (P(group, None, None, "row"), P(group, None), P(group), P(group))
        + (P(),) * 5
        + (P(group, "row"),) * 6
        + (P(),) * 3
        + (P(None, None, "row"),) * 6
        + (P(None, "row", None),) * 3
    )
    near = mesh.shape["dp"] == 4 and mesh.shape["half"] == 2 and mesh.shape["row"] == 4
    return jax.shard_map(
        near_device if near else wide_device,
        mesh=mesh,
        in_specs=placed,
        out_specs=(P(), P())
        + (P(group, "row"),) * 6
        + (P(),) * 3
        + (P(None, None, "row"),) * 6
        + (P(None, "row", None),) * 3,
        check_vma=False,
    )
```

```python
import functools
import math

import jax
import jax.numpy as jnp
from jax import lax
from jax.experimental import pallas as pl
from jax.experimental.pallas import tpu as pltpu
from jax.sharding import PartitionSpec as P

EMB = 128
NCLS = 1000
MICRO = 2
NS_ITERS = 5
STEP = 10

highest = lax.Precision.HIGHEST
high = lax.Precision.HIGH
bf16 = jnp.bfloat16
f32 = jnp.float32
BN_EPS = 1e-05
NEWTON_EPSILON = 1e-07
NS_COEF = (3.4445, -4.775, 2.0315)
MOMENTUM = 0.9
MUON_RATE = 0.03
DECAY = 0.01
BETA_ONE = 0.9
BETA_TWO = 0.95
ADAM_EPS = 1e-08
ADAM_RATE = 0.05
COLOUR_RATE = 0.01
PAD = 8
MIB = 1024 * 1024


def kernel_params(size=20):
    return pltpu.CompilerParams(vmem_limit_bytes=size * MIB)


def whole(shape):
    return pl.BlockSpec(shape, lambda t, r: (0,) * len(shape))


def silu_slope(values):
    sigmoid_value = jax.nn.sigmoid(values)
    return sigmoid_value * (1.0 + values * (1.0 - sigmoid_value))


def contract_last(left, right):
    return lax.dot_general(left, right, (((1,), (1,)), ((), ())), preferred_element_type=f32)


def times(left, right):
    return jnp.dot(left, right, preferred_element_type=f32)


def axis_swap(value, axis, k):
    n = lax.axis_size(axis)
    return lax.ppermute(value, axis, [(i, i ^ k) for i in range(n)])


def axis_shift(value, axis, k):
    n = lax.axis_size(axis)
    return lax.ppermute(value, axis, [(i, (i + k) % n) for i in range(n)])


def row_gather(value):
    return [value] + [axis_swap(value, "row", k) for k in range(1, lax.axis_size("row"))]


def row_sum(value):
    return sum(row_gather(value))


def row_exchange(pieces):
    return [pieces[0]] + [axis_swap(pieces[k], "row", k) for k in range(1, len(pieces))]


def row_scatter(pieces):
    return sum(piece.astype(f32) for piece in row_exchange(pieces))


GROUP = ("half", "dp")


def group_sum(value):
    return lax.psum(value, GROUP)


def group_pile(value):
    return lax.all_gather(value, GROUP, axis=0, tiled=True)


def group_gather(value):
    return lax.all_gather(value, GROUP, axis=0, tiled=True)


def group_scatter(value):
    return lax.psum_scatter(value, GROUP, scatter_dimension=0, tiled=True).astype(f32)


def spread(value, axis):
    n = math.prod(lax.axis_size(name) for name in axis)
    return lax.all_to_all(jnp.broadcast_to(value[None], (n,) + value.shape), axis, 0, 0)


def near_sum(value):
    return jnp.sum(spread(value, GROUP), axis=0)


def together(*values):
    return lax.optimization_barrier(values)


def after(value, *others):
    return lax.optimization_barrier((value,) + others)[0]


def step_below(value, s):
    n = lax.axis_size("dp")
    return lax.ppermute(value, "dp", [(i, i + 1) for i in range(s - 1, n - 1)])


def step_above(value, s):
    n = lax.axis_size("dp")
    return lax.ppermute(value, "dp", [(i, i - 1) for i in range(1, n - s + 1)])


def straight(value):
    return [value] + [axis_shift(value, "dp", k) for k in range(1, lax.axis_size("dp"))]


def both_cores(pieces):
    return pieces + [axis_swap(piece, "half", 1) for piece in pieces]


def placed_in_order(pieces):
    n = len(pieces)
    turned = [pieces[0]] + pieces[:0:-1]
    piled = jnp.stack(turned + turned[:-1], axis=0)
    start = lax.rem(n - lax.axis_index("dp"), n)
    return lax.dynamic_slice_in_dim(piled, start, n, 0)


def near_halves(value):
    h = lax.axis_index("half")
    kept = lax.dynamic_index_in_dim(value, h, 0, keepdims=False)
    sent = lax.dynamic_index_in_dim(value, 1 - h, 0, keepdims=False)
    return kept.astype(f32) + axis_swap(sent, "half", 1).astype(f32)


def near_blocks(kept, wire):
    n = lax.axis_size("dp")
    z = lax.axis_index("dp")
    pieces = [lax.dynamic_index_in_dim(kept, z, 0, keepdims=False)]
    for k in range(1, n):
        block = lax.dynamic_index_in_dim(wire, lax.rem(z + k, n), 0, keepdims=False)
        pieces.append(axis_shift(block, "dp", k))
    return pieces


def raise_two(values):
    h, w, n, c = values.shape
    wide = jnp.stack([values, values], axis=2).reshape(h, 2 * w, n, c)
    return jnp.stack([wide, wide], axis=1).reshape(2 * h, 2 * w, n, c)


def sum_two(values):
    h, w, n, c = values.shape
    shaped = values.reshape(h // 2, 2, w // 2, 2, n, c)
    return (shaped[:, 0, :, 0] + shaped[:, 0, :, 1]) + (shaped[:, 1, :, 0] + shaped[:, 1, :, 1])


def owned_rows(row_ref, k, size):
    return pl.ds(pl.multiple_of(lax.bitwise_xor(row_ref[0], k) * size, size), size)


def flat(values):
    return values.reshape(-1, values.shape[-1])


def conv_one_kernel(row_ref, *refs):
    blocks, (w_ref, out_ref, sums_ref, acc_ref) = refs[:-4], refs[-4:]
    h2, w2, n, c = out_ref.shape
    t = pl.program_id(0)
    dy, dx = lax.div(t, 3), lax.rem(t, 3)

    @pl.when(t == 0)
    def _():
        acc_ref[...] = jnp.zeros_like(acc_ref)

    product = sum(
        times(x_ref[0], w_ref[0, owned_rows(row_ref, k, x_ref.shape[2]), :])
        for k, x_ref in enumerate(blocks)
    )
    raised = raise_two(product.reshape(h2 // 2, w2 // 2, n, c))
    acc_ref[pl.ds(2 - dy, h2), pl.ds(2 - dx, w2)] += raised

    @pl.when(t == 8)
    def _():
        hidden = acc_ref[1 : h2 + 1, 1 : w2 + 1]
        out_ref[...] = hidden
        shaped = hidden.reshape(h2 * w2, n, c)
        first, second = jnp.sum(shaped, axis=0), jnp.sum(shaped * shaped, axis=0)
        m = n // MICRO
        for i in range(MICRO):
            sums_ref[i : i + 1, :] = jnp.sum(first[i * m : (i + 1) * m], axis=0, keepdims=True)
            sums_ref[MICRO + i : MICRO + i + 1, :] = jnp.sum(
                second[i * m : (i + 1) * m], axis=0, keepdims=True
            )


def conv_one(row, blocks, weight, pixels):
    h, w, n = pixels
    c = weight.shape[-1]
    return pl.pallas_call(
        conv_one_kernel,
        out_shape=(
            jax.ShapeDtypeStruct((2 * h, 2 * w, n, c), f32),
            jax.ShapeDtypeStruct((2 * MICRO, c), f32),
        ),
        grid_spec=pltpu.PrefetchScalarGridSpec(
            num_scalar_prefetch=1,
            grid=(9,),
            in_specs=[whole(b.shape) for b in blocks]
            + [pl.BlockSpec((1,) + weight.shape[1:], lambda t, r: (t, 0, 0))],
            out_specs=(whole((2 * h, 2 * w, n, c)), whole((2 * MICRO, c))),
            scratch_shapes=[pltpu.VMEM((2 * h + 2, 2 * w + 2, n, c), f32)],
        ),
        compiler_params=kernel_params(),
        name="conv_one",
    )(row, *blocks, weight)


def conv_two_kernel(count, row_ref, *refs):
    blocks, raws = refs[:count], refs[count : 2 * count]
    w_ref, skip_ref, colour_ref, sum_ref, act_ref, pic_ref, pad_ref, apad_ref = refs[2 * count :]
    h2, w2, n, c = sum_ref.shape
    t = pl.program_id(0)
    dy, dx = lax.div(t, 3), lax.rem(t, 3)

    @pl.when(t == 0)
    def _():
        pad_ref[...] = jnp.zeros_like(pad_ref)
        for k in range(count):
            pad_ref[k, 1 : h2 + 1, 1 : w2 + 1] = blocks[k][...]
        skipped = sum(
            times(x_ref[x_ref.shape[0] - 1], skip_ref[owned_rows(row_ref, k, x_ref.shape[2]), :])
            for k, x_ref in enumerate(raws)
        )
        sum_ref[...] = raise_two(skipped.reshape(h2 // 2, w2 // 2, n, c))

    product = sum(
        times(
            flat(pad_ref[k, pl.ds(dy, h2), pl.ds(dx, w2)]), w_ref[0, owned_rows(row_ref, k, c), :]
        )
        for k in range(count)
    )
    sum_ref[...] += product.reshape(sum_ref.shape)

    @pl.when(t == 8)
    def _():
        active = jax.nn.silu(sum_ref[...]).astype(bf16)
        act_ref[...] = active
        apad_ref[...] = jnp.zeros_like(apad_ref)
        apad_ref[1 : h2 + 1, 1 : w2 + 1] = active
        picture = jnp.zeros(pic_ref.shape, f32)
        for tap in range(9):
            y, x = divmod(tap, 3)
            picture = picture + contract_last(
                colour_ref[tap], flat(apad_ref[y : y + h2, x : x + w2])
            )
        pic_ref[...] = picture


def conv_two(row, blocks, raws, weight, skip, colour):
    h2, w2, n, c = blocks[0].shape
    return pl.pallas_call(
        functools.partial(conv_two_kernel, len(blocks)),
        out_shape=(
            jax.ShapeDtypeStruct((h2, w2, n, c), f32),
            jax.ShapeDtypeStruct((h2, w2, n, c), bf16),
            jax.ShapeDtypeStruct((PAD, h2 * w2 * n), f32),
        ),
        grid_spec=pltpu.PrefetchScalarGridSpec(
            num_scalar_prefetch=1,
            grid=(9,),
            in_specs=[whole(b.shape) for b in blocks + raws]
            + [
                pl.BlockSpec((1,) + weight.shape[1:], lambda t, r: (t, 0, 0)),
                whole(skip.shape),
                whole(colour.shape),
            ],
            out_specs=(whole((h2, w2, n, c)), whole((h2, w2, n, c)), whole((PAD, h2 * w2 * n))),
            scratch_shapes=[
                pltpu.VMEM((len(blocks), h2 + 2, w2 + 2, n, c), bf16),
                pltpu.VMEM((h2 + 2, w2 + 2, n, c), bf16),
            ],
        ),
        compiler_params=kernel_params(28),
        name="conv_two",
    )(row, *blocks, *raws, weight, skip, colour)


def critic_kernel(
    dims, pic_ref, first_ref, second_ref, skip_ref, head_ref, count_ref, out_ref, loss_ref, small_ref, pad_ref
):
    h2, w2, n = dims
    h, w = h2 // 2, w2 // 2
    c = second_ref.shape[-1]
    taps = [divmod(tap, 3) for tap in range(9)]
    shade = jnp.tanh(jnp.transpose(pic_ref[...]))
    picture = shade.astype(bf16).reshape(h2, w2, n, PAD)
    small_ref[...] = jnp.zeros_like(small_ref)
    small_ref[1 : h2 + 1, 1 : w2 + 1] = picture
    pad_ref[...] = jnp.zeros_like(pad_ref)
    front_pre = sum(
        times(flat(small_ref[y : y + h2, x : x + w2]), first_ref[3 * y + x]) for y, x in taps
    )
    pad_ref[1 : h2 + 1, 1 : w2 + 1] = jax.nn.silu(front_pre).astype(bf16).reshape(h2, w2, n, c)
    merged = sum(times(flat(pad_ref[y : y + h2, x : x + w2]), second_ref[3 * y + x]) for y, x in taps)
    merged = 0.25 * flat(sum_two(merged.reshape(h2, w2, n, c)))
    small = 0.25 * flat(sum_two(picture.astype(f32)))
    skip = skip_ref[...].astype(f32)
    for i in range(3):
        merged = merged + small[:, i : i + 1] * skip[i : i + 1, :]
    feature = jnp.sum(jax.nn.silu(merged).reshape(h * w, n, c), axis=0)
    weights = head_ref[...] * count_ref[...]
    loss_ref[...] = jnp.broadcast_to(-jnp.sum(feature * weights, keepdims=True), loss_ref.shape)
    grad_merged = (silu_slope(merged).reshape(h * w, n, c) * -weights[None]).astype(bf16)
    grad_merged = grad_merged.reshape(h, w, n, c)
    grad_pool = raise_two(grad_merged) * jnp.bfloat16(0.25)
    pad_ref[1 : h2 + 1, 1 : w2 + 1] = grad_pool
    grad_front = sum(
        contract_last(flat(pad_ref[2 - y : 2 - y + h2, 2 - x : 2 - x + w2]), second_ref[3 * y + x])
        for y, x in taps
    )
    grad_front_pre = (grad_front * silu_slope(front_pre)).astype(bf16)
    pad_ref[1 : h2 + 1, 1 : w2 + 1] = grad_front_pre.reshape(h2, w2, n, c)
    grad_picture = sum(
        contract_last(flat(pad_ref[2 - y : 2 - y + h2, 2 - x : 2 - x + w2]), first_ref[3 * y + x])
        for y, x in taps
    )
    grad_skip = contract_last(flat(grad_merged), skip_ref[...]).reshape(h, w, n, PAD)
    grad_picture = grad_picture + 0.25 * flat(raise_two(grad_skip))
    grad_pre = (grad_picture * (1.0 - shade * shade)).astype(bf16)
    small_ref[1 : h2 + 1, 1 : w2 + 1] = grad_pre.reshape(h2, w2, n, PAD)
    out_ref[...] = jnp.concatenate(
        [flat(small_ref[2 - y : 2 - y + h2, 2 - x : 2 - x + w2]) for y, x in taps]
        + [jnp.zeros((h2 * w2 * n, 128 - 9 * PAD), bf16)],
        axis=1,
    )


def critic(picture, disc_first, disc_second, disc_skip, head, counted, dims):
    h2, w2, n = dims
    c = disc_second.shape[-1]
    return pl.pallas_call(
        functools.partial(critic_kernel, dims),
        out_shape=(
            jax.ShapeDtypeStruct((h2 * w2 * n, 128), bf16),
            jax.ShapeDtypeStruct((8, 128), f32),
        ),
        scratch_shapes=[
            pltpu.VMEM((h2 + 2, w2 + 2, n, PAD), bf16),
            pltpu.VMEM((h2 + 2, w2 + 2, n, c), bf16),
        ],
        compiler_params=kernel_params(28),
        name="critic",
    )(picture, disc_first, disc_second, disc_skip, head, counted)


def back_two_kernel(count, row_ref, g_ref, sum_ref, act_ref, colour_ref, w_ref, *refs):
    gpad_ref, gcol_ref = refs[0], refs[1]
    outs, acc_ref = refs[2:-1], refs[-1]
    h2, w2, n, c = sum_ref.shape
    t = pl.program_id(0)
    dy, dx = lax.div(t, 3), lax.rem(t, 3)

    @pl.when(t == 0)
    def _():
        grad_active = times(g_ref[...], colour_ref[...]).reshape(h2, w2, n, c)
        gpad_ref[...] = jnp.zeros_like(gpad_ref)
        gpad_ref[1 : h2 + 1, 1 : w2 + 1] = (grad_active * silu_slope(sum_ref[...])).astype(bf16)
        gcol_ref[...] = lax.dot_general(
            g_ref[...], flat(act_ref[...]), (((0,), (0,)), ((), ())), preferred_element_type=f32
        )
        acc_ref[...] = jnp.zeros_like(acc_ref)

    shifted = flat(gpad_ref[pl.ds(2 - dy, h2), pl.ds(2 - dx, w2)])
    for k in range(count):
        acc_ref[k] += contract_last(shifted, w_ref[0, owned_rows(row_ref, k, c), :])

    @pl.when(t == 8)
    def _():
        for k in range(count):
            outs[k][...] = acc_ref[k].astype(bf16)


def back_two(row, grads, summed, active, colour, weight, count):
    h2, w2, n, c = summed.shape
    rows = h2 * w2 * n
    return pl.pallas_call(
        functools.partial(back_two_kernel, count),
        out_shape=(
            jax.ShapeDtypeStruct((h2 + 2, w2 + 2, n, c), bf16),
            jax.ShapeDtypeStruct((128, c), f32),
        )
        + tuple(jax.ShapeDtypeStruct((rows, c), bf16) for _ in range(count)),
        grid_spec=pltpu.PrefetchScalarGridSpec(
            num_scalar_prefetch=1,
            grid=(9,),
            in_specs=[
                whole(grads.shape),
                whole(summed.shape),
                whole(active.shape),
                whole(colour.shape),
                pl.BlockSpec((1,) + weight.shape[1:], lambda t, r: (t, 0, 0)),
            ],
            out_specs=(whole((h2 + 2, w2 + 2, n, c)), whole((128, c)))
            + tuple(whole((rows, c)) for _ in range(count)),
            scratch_shapes=[pltpu.VMEM((count, rows, c), f32)],
        ),
        compiler_params=kernel_params(28),
        name="back_two",
    )(row, grads, summed, active, colour, weight)


def weight_two_kernel(count, row_ref, gpad_ref, *refs):
    blocks, raws, (out_ref, skip_ref) = refs[:count], refs[count : 2 * count], refs[2 * count :]
    h2, w2, n, c = (gpad_ref.shape[0] - 2, gpad_ref.shape[1] - 2) + gpad_ref.shape[2:]
    t = pl.program_id(0)
    dy, dx = lax.div(t, 3), lax.rem(t, 3)
    shifted = flat(gpad_ref[pl.ds(2 - dy, h2), pl.ds(2 - dx, w2)])
    for k in range(count):
        out_ref[0, owned_rows(row_ref, k, c), :] = times(blocks[k][...], shifted).astype(bf16)

    @pl.when(t == 8)
    def _():
        phases = gpad_ref[1 : h2 + 1, 1 : w2 + 1].reshape(h2 // 2, 2, w2 // 2, 2, n, c)
        for k in range(count):
            size = raws[k].shape[0]
            skip_ref[owned_rows(row_ref, k, size), :] = sum(
                times(raws[k][...], flat(phases[:, a, :, b])) for a in range(2) for b in range(2)
            ).astype(bf16)


def weight_two(row, gpad, blocks, raws):
    c = gpad.shape[-1]
    count = len(blocks)
    tall, wide = count * blocks[0].shape[0], count * raws[0].shape[0]
    return pl.pallas_call(
        functools.partial(weight_two_kernel, count),
        out_shape=(
            jax.ShapeDtypeStruct((9, tall, c), bf16),
            jax.ShapeDtypeStruct((wide, c), bf16),
        ),
        grid_spec=pltpu.PrefetchScalarGridSpec(
            num_scalar_prefetch=1,
            grid=(9,),
            in_specs=[whole(gpad.shape)] + [whole(b.shape) for b in blocks + raws],
            out_specs=(pl.BlockSpec((1, tall, c), lambda t, r: (t, 0, 0)), whole((wide, c))),
        ),
        compiler_params=kernel_params(28),
        name="weight_two",
    )(row, gpad, *blocks, *raws)


def back_one_kernel(count, row_ref, g_ref, w_ref, *refs):
    blocks, out_ref, outs = refs[:count], refs[count], refs[count + 1 : 2 * count + 1]
    pad_ref, acc_ref = refs[2 * count + 1 :]
    h2, w2, n, c = g_ref.shape
    size = blocks[0].shape[0]
    t = pl.program_id(0)
    dy, dx = lax.div(t, 3), lax.rem(t, 3)

    @pl.when(t == 0)
    def _():
        pad_ref[...] = jnp.zeros_like(pad_ref)
        pad_ref[1 : h2 + 1, 1 : w2 + 1] = g_ref[...]
        acc_ref[...] = jnp.zeros_like(acc_ref)

    shifted = pad_ref[pl.ds(2 - dy, h2), pl.ds(2 - dx, w2)].astype(f32)
    pooled = flat(sum_two(shifted)).astype(bf16)
    for k in range(count):
        rows = owned_rows(row_ref, k, size)
        acc_ref[k] += contract_last(pooled, w_ref[0, rows, :])
        out_ref[0, rows, :] = times(blocks[k][...], pooled).astype(bf16)

    @pl.when(t == 8)
    def _():
        for k in range(count):
            outs[k][...] = acc_ref[k].astype(bf16)


def back_one(row, grads, weight, blocks):
    h2, w2, n, c = grads.shape
    count = len(blocks)
    size, rows = blocks[0].shape
    return pl.pallas_call(
        functools.partial(back_one_kernel, count),
        out_shape=(jax.ShapeDtypeStruct((9, count * size, c), bf16),)
        + tuple(jax.ShapeDtypeStruct((rows, size), bf16) for _ in range(count)),
        grid_spec=pltpu.PrefetchScalarGridSpec(
            num_scalar_prefetch=1,
            grid=(9,),
            in_specs=[
                whole(grads.shape),
                pl.BlockSpec((1,) + weight.shape[1:], lambda t, r: (t, 0, 0)),
            ]
            + [whole(b.shape) for b in blocks],
            out_specs=(pl.BlockSpec((1, count * size, c), lambda t, r: (t, 0, 0)),)
            + tuple(whole((rows, size)) for _ in range(count)),
            scratch_shapes=[
                pltpu.VMEM((h2 + 2, w2 + 2, n, c), bf16),
                pltpu.VMEM((count, rows, size), f32),
            ],
        ),
        compiler_params=kernel_params(28),
        name="back_one",
    )(row, grads, weight, *blocks)


def in_order(pieces, axis_name):
    piled = jnp.stack(pieces, axis=0)
    r = lax.axis_index(axis_name)
    return jnp.concatenate(
        [
            lax.dynamic_index_in_dim(piled, lax.bitwise_xor(r, j), 0, keepdims=False)
            for j in range(len(pieces))
        ],
        axis=0,
    )


def gram_share(owned, pieces):
    blocks = [
        lax.dot_general(piece, owned, (((0,), (0,)), ((), ())), preferred_element_type=f32)
        for piece in pieces
    ]
    return in_order(blocks, "row")


def gram_whole(panel):
    n = lax.axis_size("dp")
    h, z = lax.axis_index("half"), lax.axis_index("dp")
    total = group_sum_wide(panel)
    pieces = row_gather(total)
    piled = jnp.stack(pieces, axis=0)
    r = lax.axis_index("row")
    return jnp.concatenate(
        [
            lax.dynamic_index_in_dim(piled, lax.bitwise_xor(r, j), 0, keepdims=False)
            for j in range(len(pieces))
        ],
        axis=1,
    )


def group_sum_wide(value):
    return group_gather(group_scatter(value))


def mul(left, right):
    return jnp.dot(left, right, precision=high, preferred_element_type=f32)


def newton_columns(gram, own):
    scale = lax.rsqrt(jnp.trace(gram) + NEWTON_EPSILON)
    current = gram * (scale * scale)
    identity = jnp.eye(gram.shape[0], dtype=f32)
    maps = []
    for iteration in range(NS_ITERS):
        square = mul(current, current)
        mapping = NS_COEF[0] * identity + NS_COEF[1] * current + NS_COEF[2] * square
        maps.append(mapping)
        if iteration < NS_ITERS - 1:
            current = mul(mapping, mul(current, mapping))
    start = lax.axis_index("row") * own
    columns = lax.dynamic_slice_in_dim(maps[-1], start, own, 1)
    for mapping in maps[-2::-1]:
        columns = mul(mapping, columns)
    return columns * scale


def muon(master, moment, gradient, groups):
    moment_new = MOMENTUM * moment + gradient
    owned = moment_new.astype(bf16)
    pieces = row_gather(owned)
    own = owned.shape[1]
    gram = gram_whole(gram_share(owned, pieces))
    columns = newton_columns(gram, own).astype(bf16)
    r = lax.axis_index("row")
    direction = sum(
        times(
            piece,
            lax.dynamic_slice_in_dim(columns, lax.bitwise_xor(r, k) * own, own, 0),
        )
        for k, piece in enumerate(pieces)
    )
    factor = 0.2 * math.sqrt(max(master.shape[0] * groups, own * len(pieces)))
    return master - MUON_RATE * (factor * direction + DECAY * master), moment_new


def transposed(values):
    return jnp.transpose(values.astype(f32)).astype(values.dtype)


def place_kernel(count, sizes, index_ref, mine_ref, other_ref, *refs):
    outs = refs[-len(sizes) :]

    def write(values):
        turned = jnp.transpose(values.astype(f32)).astype(bf16)
        start = 0
        for size, out_ref in zip(sizes, outs):
            out_ref[...] = turned[start : start + size]
            start += size

    @pl.when(pl.program_id(0) < count)
    def _():
        write(mine_ref[0])

    @pl.when(pl.program_id(0) >= count)
    def _():
        write(other_ref[0])


def place(held, index, mine, other, sizes):
    count, c, wide = mine.shape
    groups = 2 * lax.axis_size("dp")
    given = [] if held is None else list(held)
    return pl.pallas_call(
        functools.partial(place_kernel, count, sizes),
        out_shape=tuple(jax.ShapeDtypeStruct((groups * size, c), bf16) for size in sizes),
        grid_spec=pltpu.PrefetchScalarGridSpec(
            num_scalar_prefetch=1,
            grid=(2 * count,),
            in_specs=[
                pl.BlockSpec((1, c, wide), lambda t, r: (jnp.minimum(t, count - 1), 0, 0)),
                pl.BlockSpec((1, c, wide), lambda t, r: (jnp.maximum(t - count, 0), 0, 0)),
            ]
            + [pl.BlockSpec(memory_space=pl.ANY) for _ in given],
            out_specs=tuple(pl.BlockSpec((size, c), lambda t, r: (r[t], 0)) for size in sizes),
        ),
        input_output_aliases={3 + i: i for i in range(len(given))},
        compiler_params=kernel_params(),
        name="place",
    )(jnp.stack(index).astype(jnp.int32), mine, other, *given)


def place_cores(held, spots, mine, sizes):
    n = lax.axis_size("dp")
    h = lax.axis_index("half")
    index = [h * n + spot for spot in spots] + [(1 - h) * n + spot for spot in spots]
    return place(held, index, mine, axis_swap(mine, "half", 1), sizes)


def weight_one_kernel(groups, where_ref, inverse_ref, *refs):
    pieces = refs[:groups]
    all_ref, moment_ref, out_ref, low_ref, pad_ref, pool_ref, grads, inputs_ref, sem = refs[groups:]
    copies = [
        pltpu.make_async_copy(piece, grads.at[g], sem.at[g]) for g, piece in enumerate(pieces)
    ]
    copies.append(pltpu.make_async_copy(all_ref, inputs_ref, sem.at[groups]))
    for copy in copies:
        copy.start()
    h2, w2, n, c = grads.shape[1:]
    size = h2 * w2 * n // 4
    row, d = where_ref[0], where_ref[1] * (groups // 2) + where_ref[2]
    owners = []
    for side in range(2):
        for k in range(groups // 2):
            spot = lax.rem(where_ref[2] + groups // 2 - k, groups // 2)
            owners.append((where_ref[1] if side == 0 else 1 - where_ref[1]) * (groups // 2) + spot)
    pad_ref[...] = jnp.zeros_like(pad_ref)
    for g in range(groups):
        copies[g].wait()
        pad_ref[1 : h2 + 1, 1 : w2 + 1] = grads[g]
        for j in range(2):
            dy, dx = lax.div(d + j, 3), lax.rem(d + j, 3)
            shifted = pad_ref[pl.ds(2 - dy, h2), pl.ds(2 - dx, w2)].astype(f32)
            pool_ref[j, g * size : (g + 1) * size, :] = flat(sum_two(shifted)).astype(bf16)
    copies[groups].wait()
    inverse = inverse_ref[0, 0]
    for q in range(groups + 1):
        i = lax.rem(d + q, groups)
        j = lax.div(d + q, groups)
        start = lax.bitwise_xor(row, lax.div(i, 2)) * (2 * c) + lax.rem(i, 2) * c
        start = pl.multiple_of(start, c)
        total = sum(
            times(inputs_ref[owners[g], pl.ds(start, c), :], pool_ref[j, g * size : (g + 1) * size, :])
            for g in range(groups)
        )
        span = slice(q * c, (q + 1) * c)
        moment = MOMENTUM * moment_ref[:, span] + jnp.transpose(total) * inverse
        out_ref[:, span] = moment
        low_ref[:, span] = moment.astype(bf16)


def weight_one_moment(where, inverse, grads, inputs, moment):
    h2, w2, n, c = grads[0].shape
    groups = len(grads)
    vmem = pl.BlockSpec(memory_space=pltpu.VMEM)
    smem = pl.BlockSpec(memory_space=pltpu.SMEM)
    flops = 2 * moment.shape[1] * c * groups * h2 * w2 * n // 4
    return pl.pallas_call(
        functools.partial(weight_one_kernel, groups),
        out_shape=(
            jax.ShapeDtypeStruct(moment.shape, f32),
            jax.ShapeDtypeStruct(moment.shape, bf16),
        ),
        in_specs=[smem, smem] + [pl.BlockSpec(memory_space=pl.ANY)] * (groups + 1) + [vmem],
        out_specs=(vmem, vmem),
        scratch_shapes=[
            pltpu.VMEM((h2 + 2, w2 + 2, n, c), bf16),
            pltpu.VMEM((2, groups * h2 * w2 * n // 4, c), bf16),
            pltpu.VMEM((groups,) + grads[0].shape, bf16),
            pltpu.VMEM(inputs.shape, bf16),
            pltpu.SemaphoreType.DMA((groups + 1,)),
        ],
        compiler_params=kernel_params(28),
        cost_estimate=pl.CostEstimate(flops=4 * flops, bytes_accessed=0, transcendentals=0),
        name="weight_one",
    )(where, inverse, *grads, inputs, moment)


def weight_pack_kernel(count, row_ref, gpad_ref, *refs):
    blocks, raws, (out_ref, tall_ref) = refs[:count], refs[count : 2 * count], refs[2 * count :]
    h2, w2, n, c = (gpad_ref.shape[0] - 2, gpad_ref.shape[1] - 2) + gpad_ref.shape[2:]
    groups = out_ref.shape[0]
    unit = count * c // groups
    half = unit // 2
    t = pl.program_id(0)
    dy, dx = lax.div(t, 3), lax.rem(t, 3)
    shifted = flat(gpad_ref[pl.ds(2 - dy, h2), pl.ds(2 - dx, w2)])
    for k in range(count):
        tall_ref[owned_rows(row_ref, k, c), :] = times(blocks[k][...], shifted)
    for i in range(groups):
        rows = tall_ref[i * unit : (i + 1) * unit, :]
        u = groups * t + i
        packed = jnp.concatenate([rows[:half], rows[half:]], axis=1).astype(bf16)
        spot = pl.multiple_of(lax.rem(u, groups + 1) * half, half)
        out_ref[lax.div(u, groups + 1), pl.ds(spot, half), :] = packed

    @pl.when(t == 8)
    def _():
        phases = gpad_ref[1 : h2 + 1, 1 : w2 + 1].reshape(h2 // 2, 2, w2 // 2, 2, n, c)
        size = raws[0].shape[0]
        each = count * size // groups
        for k in range(count):
            block = sum(
                times(raws[k][...], flat(phases[:, a, :, b])) for a in range(2) for b in range(2)
            )
            for m in range(size // each):
                rows = block[m * each : (m + 1) * each]
                packed = jnp.concatenate([rows[: each // 2], rows[each // 2 :]], axis=1)
                spot = lax.bitwise_xor(row_ref[0], k) * (size // each) + m
                out_ref[spot, (groups + 1) * half :, :] = packed.astype(bf16)


def weight_pack(row, gpad, blocks, raws, groups):
    c = gpad.shape[-1]
    count = len(blocks)
    tall, wide = count * blocks[0].shape[0], count * raws[0].shape[0]
    shape = (groups, (9 * tall + wide) // (2 * groups), 2 * c)
    flops = 2 * 9 * tall * c * blocks[0].shape[1]
    return pl.pallas_call(
        functools.partial(weight_pack_kernel, count),
        out_shape=jax.ShapeDtypeStruct(shape, bf16),
        grid_spec=pltpu.PrefetchScalarGridSpec(
            num_scalar_prefetch=1,
            grid=(9,),
            in_specs=[whole(gpad.shape)] + [whole(b.shape) for b in blocks + raws],
            out_specs=whole(shape),
            scratch_shapes=[pltpu.VMEM((tall, c), f32)],
        ),
        compiler_params=kernel_params(28),
        cost_estimate=pl.CostEstimate(flops=3 * flops, bytes_accessed=0, transcendentals=0),
        name="weight_two",
    )(row, gpad, *blocks, *raws)


def moments_kernel(count, inverse_ref, *refs):
    pieces = refs[:count]
    tall_ref, skip_ref, tall_out, skip_out, low_ref = refs[count:]
    c, size = tall_ref.shape
    total = pieces[0][...].astype(f32)
    for piece in pieces[1:]:
        total = total + piece[...].astype(f32)
    total = total * inverse_ref[0, 0]
    units = 9
    half = size // (2 * units)
    for q in range(units):
        rows = total[q * half : (q + 1) * half]
        rows = jnp.concatenate([rows[:, :c], rows[:, c:]], axis=0)
        span = slice(2 * q * half, 2 * (q + 1) * half)
        moment = MOMENTUM * tall_ref[:, span] + jnp.transpose(rows)
        tall_out[:, span] = moment
        low_ref[:, span] = moment.astype(bf16)
    rows = total[units * half :]
    rows = jnp.concatenate([rows[:, :c], rows[:, c:]], axis=0)
    moment = MOMENTUM * skip_ref[...] + jnp.transpose(rows)
    skip_out[...] = moment
    low_ref[:, size:] = moment.astype(bf16)


def moments_two(inverse, pieces, tall, skip):
    vmem = pl.BlockSpec(memory_space=pltpu.VMEM)
    return pl.pallas_call(
        functools.partial(moments_kernel, len(pieces)),
        out_shape=(
            jax.ShapeDtypeStruct(tall.shape, f32),
            jax.ShapeDtypeStruct(skip.shape, f32),
            jax.ShapeDtypeStruct((tall.shape[0], tall.shape[1] + skip.shape[1]), bf16),
        ),
        in_specs=[pl.BlockSpec(memory_space=pltpu.SMEM)] + [vmem] * (len(pieces) + 2),
        out_specs=(vmem, vmem, vmem),
        compiler_params=kernel_params(),
        name="moments",
    )(inverse, *pieces, tall, skip)


def gram_kernel(count, spans, row_ref, *refs):
    pieces, out_ref, hold_ref = refs[:count], refs[count], refs[count + 1]
    for m, (start, stop) in enumerate(spans):
        owned = pieces[0][:, start:stop]
        for k in range(count):
            hold_ref[k] = contract_last(owned, pieces[k][:, start:stop])
        out_ref[m] = jnp.concatenate(
            [hold_ref[lax.bitwise_xor(row_ref[0], j)] for j in range(count)], axis=1
        )


def gram_rows(row, pieces, spans):
    c = pieces[0].shape[0]
    count = len(pieces)
    vmem = pl.BlockSpec(memory_space=pltpu.VMEM)
    return pl.pallas_call(
        functools.partial(gram_kernel, count, spans),
        out_shape=jax.ShapeDtypeStruct((len(spans), c, count * c), f32),
        in_specs=[pl.BlockSpec(memory_space=pltpu.SMEM)] + [vmem] * count,
        out_specs=vmem,
        scratch_shapes=[pltpu.VMEM((count, c, c), f32)],
        compiler_params=kernel_params(),
        cost_estimate=pl.CostEstimate(
            flops=6 * count * c * c * pieces[0].shape[1], bytes_accessed=0, transcendentals=0
        ),
        name="gram",
    )(row, *pieces)


def gram_terms(halves):
    kept = near_halves(halves)
    return near_blocks(kept, kept)


def gram_total(terms):
    return placed_in_order(straight(sum(terms)))


def newton_kernel(count, sides, where_ref, *refs):
    pieces = refs[: sides * count]
    out_ref, a_ref, ah, al, maps_ref, th, tl = refs[sides * count :]
    size = a_ref.shape[0]
    own = size // count
    block = size // 3
    row, h = where_ref[0], where_ref[1]
    for q in range(count):
        for side in range(sides):
            piece = pieces[side * count + q]
            s = piece.shape[2]
            half = 0 if sides == 1 else (h if side == 0 else 1 - h)
            for p in range(piece.shape[0]):
                start = lax.bitwise_xor(row, q) * own + half * (own // 2) + p * s
                a_ref[pl.ds(pl.multiple_of(start, s), s), :] = piece[p, 0]

    def eye(shape, offset):
        rows = lax.broadcasted_iota(jnp.int32, shape, 0) + offset
        return rows == lax.broadcasted_iota(jnp.int32, shape, 1)

    whole_gram = a_ref[...]
    trace = jnp.sum(jnp.where(eye(whole_gram.shape, 0), whole_gram, 0.0), keepdims=True)
    scale = lax.rsqrt(trace + NEWTON_EPSILON)
    a_ref[...] = whole_gram * (scale * scale)

    def split(values):
        top = values.astype(bf16)
        return top, (values - top.astype(f32)).astype(bf16)

    def three(xh, xl, yh, yl):
        return times(xh, yh) + (times(xh, yl) + times(xl, yh))

    spans = [slice(i * block, (i + 1) * block) for i in range(3)]

    def symmetric(product, write):
        for i in range(3):
            for j in range(i, 3):
                write(i, j, product(spans[i], spans[j]))

    def store(high_ref, low_ref, i, j, value):
        top, low = split(value)
        high_ref[spans[i], spans[j]] = top
        low_ref[spans[i], spans[j]] = low
        if i != j:
            turned = jnp.transpose(value)
            top, low = split(turned)
            high_ref[spans[j], spans[i]] = top
            low_ref[spans[j], spans[i]] = low

    top, low = split(a_ref[...])
    ah[...] = top
    al[...] = low

    def step(k, carry):
        top = maps_ref.at[k]

        def write_map(i, j, value):
            value = NS_COEF[1] * a_ref[spans[i], spans[j]] + NS_COEF[2] * value
            if i == j:
                value = value + jnp.where(eye(value.shape, 0), NS_COEF[0], 0.0)
            top[spans[i], spans[j]] = value.astype(bf16)
            if i != j:
                top[spans[j], spans[i]] = jnp.transpose(value).astype(bf16)

        symmetric(lambda a, b: three(ah[a, :], al[a, :], ah[:, b], al[:, b]), write_map)
        symmetric(
            lambda a, b: times(ah[a, :], top[:, b]) + times(al[a, :], top[:, b]),
            functools.partial(store, th, tl),
        )

        def write_gram(i, j, value):
            a_ref[spans[i], spans[j]] = value
            store(ah, al, i, j, value)
            if i != j:
                a_ref[spans[j], spans[i]] = jnp.transpose(value)

        symmetric(lambda a, b: times(top[a, :], th[:, b]) + times(top[a, :], tl[:, b]), write_gram)
        return carry

    lax.fori_loop(0, NS_ITERS - 1, step, 0)
    mine = pl.ds(pl.multiple_of(row * own, own), own)
    last = a_ref[mine, :]
    columns = NS_COEF[1] * last + NS_COEF[2] * three(ah[mine, :], al[mine, :], ah[...], al[...])
    columns = columns + jnp.where(eye(columns.shape, row * own), NS_COEF[0], 0.0)

    def fold(k, columns):
        high_part, low_part = split(columns)
        top = maps_ref[NS_ITERS - 2 - k]
        return times(high_part, top) + times(low_part, top)

    columns = lax.fori_loop(0, NS_ITERS - 1, fold, columns) * scale
    for j in range(count):
        out_ref[0, j] = columns[:, j * own : (j + 1) * own].astype(bf16)


def newton(where, pieces, count):
    sides = len(pieces) // count
    n, m, s, size = pieces[0].shape
    own = size // count
    square = (size, size)
    maps = (NS_ITERS - 1,) + square
    return pl.pallas_call(
        functools.partial(newton_kernel, count, sides),
        out_shape=jax.ShapeDtypeStruct((m, count, own, own), bf16),
        grid_spec=pltpu.PrefetchScalarGridSpec(
            num_scalar_prefetch=1,
            grid=(m,),
            in_specs=[pl.BlockSpec((n, 1, s, size), lambda t, r: (0, t, 0, 0)) for _ in pieces],
            out_specs=pl.BlockSpec((1, count, own, own), lambda t, r: (t, 0, 0, 0)),
            scratch_shapes=[
                pltpu.VMEM(square, f32),
                pltpu.VMEM(square, bf16),
                pltpu.VMEM(square, bf16),
                pltpu.VMEM(maps, bf16),
                pltpu.VMEM(square, bf16),
                pltpu.VMEM(square, bf16),
            ],
        ),
        compiler_params=kernel_params(36),
        cost_estimate=pl.CostEstimate(
            flops=m * 50 * size**3, bytes_accessed=0, transcendentals=0
        ),
        name="newton",
    )(where, *pieces)


def update_kernel(count, spans, factors, row_ref, map_ref, *refs):
    pieces, masters, outs = refs[:count], refs[count : count + len(spans)], refs[count + len(spans) :]
    for m, (start, stop) in enumerate(spans):
        direction = sum(
            times(map_ref[m, lax.bitwise_xor(row_ref[0], k)], pieces[k][:, start:stop])
            for k in range(count)
        )
        master = masters[m][...]
        outs[m][...] = master - MUON_RATE * (factors[m] * direction + DECAY * master)


def update(row, maps, pieces, masters, spans, factors):
    count = len(pieces)
    vmem = pl.BlockSpec(memory_space=pltpu.VMEM)
    return pl.pallas_call(
        functools.partial(update_kernel, count, spans, factors),
        out_shape=tuple(jax.ShapeDtypeStruct(master.shape, f32) for master in masters),
        in_specs=[pl.BlockSpec(memory_space=pltpu.SMEM)] + [vmem] * (1 + count + len(masters)),
        out_specs=(vmem,) * len(masters),
        compiler_params=kernel_params(),
        name="update",
    )(row, maps, *pieces, *masters)


def back_in_kernel(count, row_ref, g_ref, w_ref, *refs):
    outs, (pad_ref, acc_ref) = refs[:count], refs[count:]
    h2, w2, n, c = g_ref.shape
    size = outs[0].shape[1]
    t = pl.program_id(0)
    dy, dx = lax.div(t, 3), lax.rem(t, 3)

    @pl.when(t == 0)
    def _():
        pad_ref[...] = jnp.zeros_like(pad_ref)
        pad_ref[1 : h2 + 1, 1 : w2 + 1] = g_ref[...]
        acc_ref[...] = jnp.zeros_like(acc_ref)

    shifted = pad_ref[pl.ds(2 - dy, h2), pl.ds(2 - dx, w2)].astype(f32)
    pooled = flat(sum_two(shifted)).astype(bf16)
    for k in range(count):
        acc_ref[k] += contract_last(pooled, w_ref[0, owned_rows(row_ref, k, size), :])

    @pl.when(t == 8)
    def _():
        for k in range(count):
            outs[k][...] = acc_ref[k].astype(bf16)


def back_in(row, grads, weight, count):
    h2, w2, n, c = grads.shape
    size, rows = weight.shape[1] // count, h2 * w2 * n // 4
    return pl.pallas_call(
        functools.partial(back_in_kernel, count),
        out_shape=tuple(jax.ShapeDtypeStruct((rows, size), bf16) for _ in range(count)),
        grid_spec=pltpu.PrefetchScalarGridSpec(
            num_scalar_prefetch=1,
            grid=(9,),
            in_specs=[
                whole(grads.shape),
                pl.BlockSpec((1,) + weight.shape[1:], lambda t, r: (t, 0, 0)),
            ],
            out_specs=tuple(whole((rows, size)) for _ in range(count)),
            scratch_shapes=[
                pltpu.VMEM((h2 + 2, w2 + 2, n, c), bf16),
                pltpu.VMEM((count, rows, size), f32),
            ],
        ),
        compiler_params=kernel_params(28),
        cost_estimate=pl.CostEstimate(
            flops=6 * 9 * rows * count * size * c, bytes_accessed=0, transcendentals=0
        ),
        name="back_one",
    )(row, grads, weight)


def adam_update(weight, gradient, mean_old, square_old, rate):
    mean_new = BETA_ONE * mean_old + (1.0 - BETA_ONE) * gradient
    square_new = BETA_TWO * square_old + (1.0 - BETA_TWO) * gradient * gradient
    ratio = (
        mean_new
        / (1.0 - BETA_ONE**STEP)
        / (jnp.sqrt(square_new / (1.0 - BETA_TWO**STEP)) + ADAM_EPS)
    )
    return (weight - rate * (ratio + DECAY * weight), mean_new, square_new)


def moments_of(totals, count):
    centre = totals[:MICRO] / count
    return centre, lax.rsqrt(totals[MICRO:] / count - centre * centre + BN_EPS)


def per_image(values, n):
    return jnp.repeat(values, n // MICRO, axis=0)


def per_micro(values):
    return jnp.sum(values.reshape(MICRO, -1, values.shape[-1]), axis=1)


def wide_device(
    features,
    noise,
    labels,
    counted,
    disc_first,
    disc_second,
    disc_skip,
    disc_head,
    disc_table,
    conv_first,
    conv_second,
    conv_skip,
    momentum_first,
    momentum_second,
    momentum_skip,
    class_table,
    table_mean,
    table_square,
    norm_first,
    first_mean,
    first_square,
    norm_second,
    second_mean,
    second_square,
    colour_conv,
    colour_mean,
    colour_square,
):
    groups = lax.axis_size("half") * lax.axis_size("dp")
    ranks = lax.axis_size("row")
    row = lax.axis_index("row").astype(jnp.int32).reshape(1)
    n, h, w, c_in = features.shape
    c_out = conv_first.shape[1]
    count_low = float(n // MICRO * h * w * groups)
    count_high = 4.0 * count_low

    inputs = jnp.transpose(features, (1, 2, 0, 3))
    raw = inputs.astype(f32)
    sums_low = jnp.concatenate(
        [per_micro(jnp.sum(raw, axis=(0, 1))), per_micro(jnp.sum(raw * raw, axis=(0, 1)))], axis=0
    )
    totals_low = group_sum(sums_low)
    weight_one = group_gather(conv_first.astype(bf16)).reshape(9, ranks * c_in, c_out)

    onehot = (labels[:, None] == jnp.arange(NCLS)[None, :]).astype(f32)
    conds = jnp.concatenate([jnp.dot(onehot, class_table, precision=highest), noise], axis=1)
    class_disc = jnp.dot(onehot, disc_table, precision=highest)
    mods_one = jnp.einsum("bk,kgc->bgc", conds, norm_first, precision=highest)
    mods_two = jnp.einsum("bk,kgc->bgc", conds, norm_second, precision=highest)

    centre_one, spread_one = moments_of(totals_low, count_low)
    centre_one, spread_one = per_image(centre_one, n), per_image(spread_one, n)
    gain_one, gain_two = 1.0 + mods_one[:, 0], 1.0 + mods_two[:, 0]
    normed_one = (raw - centre_one) * spread_one
    pre_one = normed_one * gain_one + mods_one[:, 1]
    acted_one = flat(jax.nn.silu(pre_one).astype(bf16))
    ones = row_gather(acted_one)
    raws = row_gather(flat(inputs))

    hidden, sums_high = conv_one(row, [one[None] for one in ones], weight_one, (h, w, n))
    held_second, held_skip, _ = lax.optimization_barrier(
        (conv_second.astype(bf16), conv_skip.astype(bf16), weight_one[0, 0, 0])
    )
    weight_skip = group_gather(held_skip)
    weight_two = group_gather(held_second).reshape(9, ranks * c_out, c_out)
    totals_high = group_sum(sums_high)
    centre_two, spread_two = moments_of(totals_high, count_high)
    centre_two, spread_two = per_image(centre_two, n), per_image(spread_two, n)
    normed_two = (hidden - centre_two) * spread_two
    pre_two = normed_two * gain_two + mods_two[:, 1]
    acted_two = jax.nn.silu(pre_two).astype(bf16)
    twos = row_gather(acted_two)

    colour = jnp.pad(
        jnp.transpose(colour_conv, (0, 2, 1)).astype(bf16), ((0, 0), (0, PAD - 3), (0, 0))
    )
    summed, active, picture = conv_two(row, twos, [one[None] for one in raws], weight_two, weight_skip, colour)
    picture = row_sum(picture)

    first_taps = jnp.pad(disc_first.reshape(9, 3, -1), ((0, 0), (0, PAD - 3), (0, 0)))
    second_taps = disc_second.reshape(9, -1, disc_second.shape[-1])
    skip_taps = jnp.pad(disc_skip, ((0, PAD - 3), (0, 0)))
    mark = counted.astype(f32)[:, None]
    grads, loss_part = critic(
        picture,
        first_taps,
        second_taps,
        skip_taps,
        disc_head[None, :] + class_disc,
        mark,
        (2 * h, 2 * w, n),
    )
    colour_rows = jnp.pad(colour.reshape(9 * PAD, c_out), ((0, 128 - 9 * PAD), (0, 0)))
    backs = back_two(row, grads, summed, active, colour_rows, weight_two, ranks)
    gpad, grad_colour, pieces = backs[0], backs[1], backs[2:]
    grad_two, grad_skip = weight_two_grads(row, gpad, twos, raws)
    grad_acted_two = row_scatter(list(pieces)).reshape(hidden.shape)

    grad_pre_two = grad_acted_two * silu_slope(pre_two)
    gains_two = jnp.sum(grad_pre_two * normed_two, axis=(0, 1))
    shifts_two = jnp.sum(grad_pre_two, axis=(0, 1))
    back_sums = group_sum(
        jnp.concatenate([per_micro(gain_two * shifts_two), per_micro(gain_two * gains_two)], axis=0)
    )
    mean_g = per_image(back_sums[:MICRO] / count_high, n)
    mean_gy = per_image(back_sums[MICRO:] / count_high, n)
    grad_hidden = (spread_two * (grad_pre_two * gain_two - mean_g - normed_two * mean_gy)).astype(
        bf16
    )
    ones_turned = [jnp.transpose(one) for one in ones]
    backs = back_one(row, grad_hidden, weight_one, ones_turned)
    grad_one, pieces = flat(backs[0]), backs[1:]
    grad_acted_one = row_scatter(list(pieces)).reshape(raw.shape)
    grad_pre_one = grad_acted_one * silu_slope(pre_one)
    gains_one = jnp.sum(grad_pre_one * normed_one, axis=(0, 1))
    shifts_one = jnp.sum(grad_pre_one, axis=(0, 1))
    grad_mods_one = jnp.stack([gains_one, shifts_one], axis=1)
    grad_mods_two = jnp.stack([gains_two, shifts_two], axis=1)

    grad_cond = jnp.einsum("bgc,kgc->bk", grad_mods_one, norm_first[:EMB], precision=highest)
    grad_cond = grad_cond + jnp.einsum(
        "bgc,kgc->bk", grad_mods_two, norm_second[:EMB], precision=highest
    )
    grad_cond = row_sum(grad_cond)

    count_part = jnp.sum(counted).astype(f32)
    small = jnp.concatenate(
        [
            grad_colour[: 9 * PAD],
            jnp.broadcast_to(loss_part[:1, :1], (1, c_out)),
            jnp.broadcast_to(count_part, (1, c_out)),
        ],
        axis=0,
    )
    small = group_sum(small)
    loss_sum, fake_count = small[9 * PAD, 0], small[9 * PAD + 1, 0]
    inverse = 1.0 / fake_count
    g_colour = jnp.transpose(small[: 9 * PAD].reshape(9, PAD, c_out)[:, :3], (0, 2, 1))

    known = group_pile(jnp.concatenate([conds, labels.astype(f32)[:, None]], axis=1))
    found = group_pile(
        jnp.concatenate(
            [grad_mods_one.reshape(n, -1), grad_mods_two.reshape(n, -1), grad_cond], axis=1
        )
    )
    conds_all, labels_all = known[:, :-1], known[:, -1].astype(jnp.int32)
    onehot_all = (labels_all[:, None] == jnp.arange(NCLS)[None, :]).astype(f32)
    cut_one, cut_two = 2 * c_in, 2 * c_in + 2 * c_out
    g_norm = lax.dot_general(
        conds_all,
        found[:, :cut_two],
        (((0,), (0,)), ((), ())),
        precision=highest,
        preferred_element_type=f32,
    )
    g_norm_one = g_norm[:, :cut_one].reshape(norm_first.shape)
    g_norm_two = g_norm[:, cut_one:].reshape(norm_second.shape)
    g_table = lax.dot_general(
        onehot_all,
        found[:, cut_two:],
        (((0,), (0,)), ((), ())),
        precision=highest,
        preferred_element_type=f32,
    )

    shares = [group_scatter(flat(g)) for g in (grad_one, grad_two, grad_skip)]
    muons = [
        muon(master, moment, share * inverse, groups)
        for master, moment, share in zip(
            (conv_first, conv_second, conv_skip),
            (momentum_first, momentum_second, momentum_skip),
            shares,
        )
    ]
    table_new = adam_update(class_table, g_table * inverse, table_mean, table_square, ADAM_RATE)
    first_new = adam_update(norm_first, g_norm_one * inverse, first_mean, first_square, ADAM_RATE)
    second_new = adam_update(
        norm_second, g_norm_two * inverse, second_mean, second_square, ADAM_RATE
    )
    colour_new = adam_update(
        colour_conv, g_colour * inverse, colour_mean, colour_square, COLOUR_RATE
    )
    return (
        (loss_sum, fake_count)
        + tuple(m[0] for m in muons)
        + tuple(m[1] for m in muons)
        + table_new
        + first_new
        + second_new
        + colour_new
    )


def near_device(
    features,
    noise,
    labels,
    counted,
    disc_first,
    disc_second,
    disc_skip,
    disc_head,
    disc_table,
    conv_first,
    conv_second,
    conv_skip,
    momentum_first,
    momentum_second,
    momentum_skip,
    class_table,
    table_mean,
    table_square,
    norm_first,
    first_mean,
    first_square,
    norm_second,
    second_mean,
    second_square,
    colour_conv,
    colour_mean,
    colour_square,
):
    groups = lax.axis_size("half") * lax.axis_size("dp")
    ranks = lax.axis_size("row")
    row = lax.axis_index("row").astype(jnp.int32).reshape(1)
    n, h, w, c_in = features.shape
    c_out = conv_first.shape[1]
    count_low = float(n // MICRO * h * w * groups)
    count_high = 4.0 * count_low

    where = jnp.stack(
        [lax.axis_index("row"), lax.axis_index("half"), lax.axis_index("dp")]
    ).astype(jnp.int32)
    n_dp, half, spot = lax.axis_size("dp"), lax.axis_index("half"), lax.axis_index("dp")
    turned = conv_first.T.astype(bf16)
    below, above = [turned, step_below(turned, 1)], [turned, step_above(turned, 1)]
    inputs = jnp.transpose(features, (1, 2, 0, 3))
    raw = inputs.astype(f32)
    sums_low = jnp.concatenate(
        [
            per_micro(jnp.sum(raw, axis=(0, 1))),
            per_micro(jnp.sum(raw * raw, axis=(0, 1))),
            jnp.broadcast_to(jnp.sum(counted).astype(f32), (1, c_in)),
        ],
        axis=0,
    )
    totals_low = near_sum(sums_low)
    below.append(step_below(below[1], 2))
    above.append(step_above(above[1], 2))
    fake_count = totals_low[2 * MICRO, 0]
    inverse = 1.0 / fake_count

    onehot = (labels[:, None] == jnp.arange(NCLS)[None, :]).astype(f32)
    conds = jnp.concatenate([jnp.dot(onehot, class_table, precision=highest), noise], axis=1)
    class_disc = jnp.dot(onehot, disc_table, precision=highest)
    mods_one = jnp.einsum("bk,kgc->bgc", conds, norm_first, precision=highest)
    mods_two = jnp.einsum("bk,kgc->bgc", conds, norm_second, precision=highest)

    centre_one, spread_one = moments_of(totals_low[: 2 * MICRO], count_low)
    centre_one, spread_one = per_image(centre_one, n), per_image(spread_one, n)
    gain_one, gain_two = 1.0 + mods_one[:, 0], 1.0 + mods_two[:, 0]
    normed_one = (raw - centre_one) * spread_one
    pre_one = normed_one * gain_one + mods_one[:, 1]
    acted_one = flat(jax.nn.silu(pre_one).astype(bf16))
    pairs = row_gather(jnp.stack([acted_one, flat(inputs)], axis=0))
    sizes = (conv_first.shape[0],)
    down, up = lax.rem(spot + 3, 4), lax.rem(spot + 1, 4)
    held = place_cores(None, [spot, down, up], jnp.stack([turned, below[1], above[1]]), sizes)
    below.append(step_below(after(below[2], *pairs), 3))
    above.append(step_above(after(above[2], *pairs), 3))
    middle = jnp.where(spot >= 2, below[2], above[2])
    held = place_cores(held, [lax.rem(spot + 2, 4)], middle[None], sizes)
    below[3], above[3] = after(below[3], *held), after(above[3], *held)
    last = jnp.where(spot == 3, below[3], jnp.where(spot == 0, above[3], turned))
    end = jnp.where(spot == 3, 0, jnp.where(spot == 0, 3, spot))
    (weight_one,) = place_cores(held, [end], last[None], sizes)
    weight_one = weight_one.reshape(9, ranks * c_in, c_out)

    hidden, sums_high = conv_one(row, pairs, weight_one, (h, w, n))
    other = jnp.concatenate([conv_second.T, conv_skip.T], axis=1).astype(bf16)
    other = jnp.pad(other, ((0, 0), (0, -other.shape[1] % 128)))
    others = lax.all_gather(after(other, below[3], above[3]), GROUP, axis=0)
    weight_two, weight_skip = place(
        None,
        list(range(groups)),
        others[: groups // 2],
        others[groups // 2 :],
        (conv_second.shape[0], conv_skip.shape[0]),
    )
    weight_two = weight_two.reshape(9, ranks * c_out, c_out)
    totals_high = near_sum(sums_high)
    centre_two, spread_two = moments_of(totals_high, count_high)
    centre_two, spread_two = per_image(centre_two, n), per_image(spread_two, n)
    normed_two = (hidden - centre_two) * spread_two
    pre_two = normed_two * gain_two + mods_two[:, 1]
    acted_two = jax.nn.silu(pre_two).astype(bf16)
    twos = row_gather(acted_two)
    kept_pairs = [after(pair, sums_high) for pair in pairs]
    turned = jnp.concatenate([jnp.transpose(pair[0]) for pair in kept_pairs], axis=0)
    ones_all = lax.all_gather(after(turned, others), GROUP, axis=0)

    colour = jnp.pad(
        jnp.transpose(colour_conv, (0, 2, 1)).astype(bf16), ((0, 0), (0, PAD - 3), (0, 0))
    )
    summed, active, picture = conv_two(row, twos, pairs, weight_two, weight_skip, colour)
    picture = row_sum(picture)

    first_taps = jnp.pad(disc_first.reshape(9, 3, -1), ((0, 0), (0, PAD - 3), (0, 0)))
    second_taps = disc_second.reshape(9, -1, disc_second.shape[-1])
    skip_taps = jnp.pad(disc_skip, ((0, PAD - 3), (0, 0)))
    mark = counted.astype(f32)[:, None]
    grads, loss_part = critic(
        picture,
        first_taps,
        second_taps,
        skip_taps,
        disc_head[None, :] + class_disc,
        mark,
        (2 * h, 2 * w, n),
    )
    colour_rows = jnp.pad(colour.reshape(9 * PAD, c_out), ((0, 128 - 9 * PAD), (0, 0)))
    backs = back_two(row, grads, summed, active, colour_rows, weight_two, ranks)
    gpad, grad_colour = backs[0], backs[1]
    pieces = row_exchange(list(backs[2:]))
    packed = weight_pack(
        row,
        gpad,
        [jnp.transpose(flat(after(two, active))) for two in twos],
        [jnp.transpose(after(pair, active)[1]) for pair in pairs],
        groups,
    )
    kept = near_halves(packed.reshape((2, groups // 2) + packed.shape[1:]))
    pieces[-1] = after(pieces[-1], packed)
    grad_acted_two = sum(piece.astype(f32) for piece in pieces).reshape(hidden.shape)

    grad_pre_two = grad_acted_two * silu_slope(pre_two)
    gains_two = jnp.sum(grad_pre_two * normed_two, axis=(0, 1))
    shifts_two = jnp.sum(grad_pre_two, axis=(0, 1))
    back_sums = jnp.concatenate(
        [per_micro(gain_two * shifts_two), per_micro(gain_two * gains_two)], axis=0
    )
    back_sums = near_sum(back_sums)
    mean_g = per_image(back_sums[:MICRO] / count_high, n)
    mean_gy = per_image(back_sums[MICRO:] / count_high, n)
    grad_hidden = (spread_two * (grad_pre_two * gain_two - mean_g - normed_two * mean_gy)).astype(
        bf16
    )
    hidden_all = straight(grad_hidden)
    scaled = inverse.reshape(1, 1)
    hidden_all = straight(grad_hidden)
    hidden_all = both_cores(list(together(*hidden_all)))
    moment_one, low_one = weight_one_moment(
        where, scaled, hidden_all, ones_all, momentum_first.T
    )
    kept, grad_hidden = after(kept, low_one), after(grad_hidden, low_one)
    one_held = row_gather(low_one)
    shares = near_blocks(kept, kept.astype(bf16))
    backs = back_in(row, grad_hidden, weight_one, ranks)
    *one_held, shares[1], shares[2], shares[3], backs = together(
        *one_held, *shares[1:], jnp.stack(backs, axis=0)
    )
    panel = gram_rows(row, one_held, [(0, conv_first.shape[0])])
    kept_one = near_halves(panel.reshape(2, 4, 1, c_out // 8, -1))
    moment_two, moment_skip, low_two = moments_two(
        scaled, [after(shares[0], panel)] + shares[1:], momentum_second.T, momentum_skip.T
    )
    kept_one = after(kept_one, low_two)
    two_held = spread(low_two, ("row",))
    total_one = gram_total(near_blocks(kept_one, kept_one))
    grams_one = row_gather(total_one)
    two_held = after(two_held, *grams_one[1:])
    two_held = [
        lax.dynamic_index_in_dim(two_held, lax.bitwise_xor(row[0], k), 0, keepdims=False)
        for k in range(ranks)
    ]
    spans = [(0, conv_second.shape[0]), (conv_second.shape[0], low_two.shape[1])]
    panels = gram_rows(row, two_held, spans)
    kept_two = near_halves(panels.reshape(2, 4, 1, c_out // 4, -1))
    backs = after(backs, *grams_one[1:])
    inward = lax.all_to_all(in_order(list(backs[:, None]), "row"), "row", 0, 0)
    grams_one = both_cores(grams_one)
    kept_two = after(kept_two, *grams_one)
    terms_two = near_blocks(kept_two, kept_two)
    terms_two[0] = after(terms_two[0], inward)
    total_two = placed_in_order(straight(sum(terms_two)))
    *grams_one, total_two = together(*grams_one, total_two)
    maps_one = newton(where, grams_one, ranks)
    factor = 0.2 * math.sqrt(max(conv_first.shape[0] * groups, c_out * ranks))
    grad_acted_one = jnp.sum(inward.astype(f32), axis=0).reshape(raw.shape)
    grad_pre_one = grad_acted_one * silu_slope(pre_one)
    gains_one = jnp.sum(grad_pre_one * normed_one, axis=(0, 1))
    shifts_one = jnp.sum(grad_pre_one, axis=(0, 1))
    grad_mods_one = jnp.stack([gains_one, shifts_one], axis=1)
    grad_mods_two = jnp.stack([gains_two, shifts_two], axis=1)

    grad_cond = jnp.einsum("bgc,kgc->bk", grad_mods_one, norm_first[:EMB], precision=highest)
    grad_cond = grad_cond + jnp.einsum(
        "bgc,kgc->bk", grad_mods_two, norm_second[:EMB], precision=highest
    )

    small = jnp.concatenate(
        [
            grad_colour[: 9 * PAD],
            jnp.broadcast_to(loss_part[:1, :1], (1, c_out)),
        ],
        axis=0,
    )

    grad_cond = jnp.sum(spread(grad_cond, ("row",)), axis=0)
    found = jnp.concatenate(
        [
            grad_mods_one.reshape(n, -1),
            grad_mods_two.reshape(n, -1),
            grad_cond,
            conds,
            labels.astype(f32)[:, None],
        ],
        axis=1,
    )
    found = jnp.pad(found, ((0, 0), (0, -found.shape[1] % 128)))
    wide = found.shape[1]
    extra = small.reshape(-1)
    extra = jnp.pad(extra, (0, -extra.shape[0] % (8 * wide))).reshape(-1, wide)
    packet = jnp.concatenate([found, extra], axis=0)
    packet = spread(after(packet, total_two), GROUP)
    found = packet[:, :n].reshape(-1, wide)
    small = jnp.sum(packet[:, n:], axis=0).reshape(-1)[: small.size].reshape(small.shape)
    loss_sum = small[9 * PAD, 0]
    g_colour = jnp.transpose(small[: 9 * PAD].reshape(9, PAD, c_out)[:, :3], (0, 2, 1))
    cut = 2 * c_in + 2 * c_out + EMB
    found, known = found[:, :cut], found[:, cut : cut + conds.shape[1] + 1]
    conds_all, labels_all = known[:, :-1], known[:, -1].astype(jnp.int32)
    onehot_all = (labels_all[:, None] == jnp.arange(NCLS)[None, :]).astype(f32)
    cut_one, cut_two = 2 * c_in, 2 * c_in + 2 * c_out
    g_norm = lax.dot_general(
        conds_all,
        found[:, :cut_two],
        (((0,), (0,)), ((), ())),
        precision=highest,
        preferred_element_type=f32,
    )
    g_norm_one = g_norm[:, :cut_one].reshape(norm_first.shape)
    g_norm_two = g_norm[:, cut_one:].reshape(norm_second.shape)
    g_table = lax.dot_general(
        onehot_all,
        found[:, cut_two:],
        (((0,), (0,)), ((), ())),
        precision=highest,
        preferred_element_type=f32,
    )

    table_new = adam_update(class_table, g_table * inverse, table_mean, table_square, ADAM_RATE)
    first_new = adam_update(norm_first, g_norm_one * inverse, first_mean, first_square, ADAM_RATE)
    second_new = adam_update(
        norm_second, g_norm_two * inverse, second_mean, second_square, ADAM_RATE
    )
    colour_new = adam_update(
        colour_conv, g_colour * inverse, colour_mean, colour_square, COLOUR_RATE
    )
    grams_two = row_gather(total_two)
    (first_out,) = update(
        row, maps_one, one_held, [conv_first.T], [(0, conv_first.shape[0])], [factor]
    )
    grams_two[0] = after(grams_two[0], first_out)
    maps_two = newton(where, grams_two, ranks)
    other_map = axis_swap(maps_two, "half", 1)
    maps_two = jnp.where(
        half == 0,
        jnp.concatenate([maps_two, other_map], axis=0),
        jnp.concatenate([other_map, maps_two], axis=0),
    )
    factors = [
        0.2 * math.sqrt(max(rows * groups, c_out * ranks))
        for rows in (conv_second.shape[0], conv_skip.shape[0])
    ]
    second_out, skip_out = update(
        row, maps_two, two_held, [conv_second.T, conv_skip.T], spans, factors
    )
    weights_new = (first_out.T, second_out.T, skip_out.T)
    moments_new = (moment_one.T, moment_two.T, moment_skip.T)
    return (
        (loss_sum, fake_count)
        + weights_new
        + moments_new
        + table_new
        + first_new
        + second_new
        + colour_new
    )


def weight_two_grads(row, gpad, twos, raws):
    turned = [jnp.transpose(flat(two)) for two in twos]
    return weight_two(row, gpad, turned, [jnp.transpose(one) for one in raws])


def solution(mesh):
    group = ("half", "dp")
    placed = (
        (P(group, None, None, "row"), P(group, None), P(group), P(group))
        + (P(),) * 5
        + (P(group, "row"),) * 6
        + (P(),) * 3
        + (P(None, None, "row"),) * 6
        + (P(None, "row", None),) * 3
    )
    near = mesh.shape["dp"] == 4 and mesh.shape["half"] == 2 and mesh.shape["row"] == 4
    return jax.shard_map(
        near_device if near else wide_device,
        mesh=mesh,
        in_specs=placed,
        out_specs=(P(), P())
        + (P(group, "row"),) * 6
        + (P(),) * 3
        + (P(None, None, "row"),) * 6
        + (P(None, "row", None),) * 3,
        check_vma=False,
    )
```

```python
import functools
import math

import jax
import jax.numpy as jnp
from jax import lax
from jax.experimental import pallas as pl
from jax.experimental.pallas import tpu as pltpu
from jax.sharding import PartitionSpec as P

EMB = 128
NCLS = 1000
MICRO = 2
NS_ITERS = 5
STEP = 10

highest = lax.Precision.HIGHEST
high = lax.Precision.HIGH
bf16 = jnp.bfloat16
f32 = jnp.float32
BN_EPS = 1e-05
NEWTON_EPSILON = 1e-07
NS_COEF = (3.4445, -4.775, 2.0315)
MOMENTUM = 0.9
MUON_RATE = 0.03
DECAY = 0.01
BETA_ONE = 0.9
BETA_TWO = 0.95
ADAM_EPS = 1e-08
ADAM_RATE = 0.05
COLOUR_RATE = 0.01
PAD = 8
MIB = 1024 * 1024


def kernel_params(size=20):
    return pltpu.CompilerParams(vmem_limit_bytes=size * MIB)


def whole(shape):
    return pl.BlockSpec(shape, lambda t, r: (0,) * len(shape))


def silu_slope(values):
    sigmoid_value = jax.nn.sigmoid(values)
    return sigmoid_value * (1.0 + values * (1.0 - sigmoid_value))


def contract_last(left, right):
    return lax.dot_general(left, right, (((1,), (1,)), ((), ())), preferred_element_type=f32)


def times(left, right):
    return jnp.dot(left, right, preferred_element_type=f32)


def axis_swap(value, axis, k):
    n = lax.axis_size(axis)
    return lax.ppermute(value, axis, [(i, i ^ k) for i in range(n)])


def axis_shift(value, axis, k):
    n = lax.axis_size(axis)
    return lax.ppermute(value, axis, [(i, (i + k) % n) for i in range(n)])


def row_gather(value):
    return [value] + [axis_swap(value, "row", k) for k in range(1, lax.axis_size("row"))]


def row_sum(value):
    return sum(row_gather(value))


def row_exchange(pieces):
    return [pieces[0]] + [axis_swap(pieces[k], "row", k) for k in range(1, len(pieces))]


def row_scatter(pieces):
    return sum(piece.astype(f32) for piece in row_exchange(pieces))


GROUP = ("half", "dp")


def group_sum(value):
    return lax.psum(value, GROUP)


def group_pile(value):
    return lax.all_gather(value, GROUP, axis=0, tiled=True)


def group_gather(value):
    return lax.all_gather(value, GROUP, axis=0, tiled=True)


def group_scatter(value):
    return lax.psum_scatter(value, GROUP, scatter_dimension=0, tiled=True).astype(f32)


def spread(value, axis):
    n = math.prod(lax.axis_size(name) for name in axis)
    return lax.all_to_all(jnp.broadcast_to(value[None], (n,) + value.shape), axis, 0, 0)


def near_sum(value):
    return jnp.sum(spread(value, GROUP), axis=0)


def together(*values):
    return lax.optimization_barrier(values)


def after(value, *others):
    return lax.optimization_barrier((value,) + others)[0]


def step_below(value, s):
    n = lax.axis_size("dp")
    return lax.ppermute(value, "dp", [(i, i + 1) for i in range(s - 1, n - 1)])


def step_above(value, s):
    n = lax.axis_size("dp")
    return lax.ppermute(value, "dp", [(i, i - 1) for i in range(1, n - s + 1)])


def straight(value):
    return [value] + [axis_shift(value, "dp", k) for k in range(1, lax.axis_size("dp"))]


def both_cores(pieces):
    return pieces + [axis_swap(piece, "half", 1) for piece in pieces]


def placed_in_order(pieces):
    n = len(pieces)
    turned = [pieces[0]] + pieces[:0:-1]
    piled = jnp.stack(turned + turned[:-1], axis=0)
    start = lax.rem(n - lax.axis_index("dp"), n)
    return lax.dynamic_slice_in_dim(piled, start, n, 0)


def near_halves(value):
    h = lax.axis_index("half")
    kept = lax.dynamic_index_in_dim(value, h, 0, keepdims=False)
    sent = lax.dynamic_index_in_dim(value, 1 - h, 0, keepdims=False)
    return kept.astype(f32) + axis_swap(sent, "half", 1).astype(f32)


def near_blocks(kept, wire):
    n = lax.axis_size("dp")
    z = lax.axis_index("dp")
    pieces = [lax.dynamic_index_in_dim(kept, z, 0, keepdims=False)]
    for k in range(1, n):
        block = lax.dynamic_index_in_dim(wire, lax.rem(z + k, n), 0, keepdims=False)
        pieces.append(axis_shift(block, "dp", k))
    return pieces


def raise_two(values):
    h, w, n, c = values.shape
    wide = jnp.stack([values, values], axis=2).reshape(h, 2 * w, n, c)
    return jnp.stack([wide, wide], axis=1).reshape(2 * h, 2 * w, n, c)


def sum_two(values):
    h, w, n, c = values.shape
    shaped = values.reshape(h // 2, 2, w // 2, 2, n, c)
    return (shaped[:, 0, :, 0] + shaped[:, 0, :, 1]) + (shaped[:, 1, :, 0] + shaped[:, 1, :, 1])


def owned_rows(row_ref, k, size):
    return pl.ds(pl.multiple_of(lax.bitwise_xor(row_ref[0], k) * size, size), size)


def flat(values):
    return values.reshape(-1, values.shape[-1])


def conv_one_kernel(row_ref, *refs):
    blocks, (w_ref, out_ref, sums_ref, acc_ref) = refs[:-4], refs[-4:]
    h2, w2, n, c = out_ref.shape
    t = pl.program_id(0)
    dy, dx = lax.div(t, 3), lax.rem(t, 3)

    @pl.when(t == 0)
    def _():
        acc_ref[...] = jnp.zeros_like(acc_ref)

    product = sum(
        times(x_ref[0], w_ref[0, owned_rows(row_ref, k, x_ref.shape[2]), :])
        for k, x_ref in enumerate(blocks)
    )
    raised = raise_two(product.reshape(h2 // 2, w2 // 2, n, c))
    acc_ref[pl.ds(2 - dy, h2), pl.ds(2 - dx, w2)] += raised

    @pl.when(t == 8)
    def _():
        hidden = acc_ref[1 : h2 + 1, 1 : w2 + 1]
        out_ref[...] = hidden
        shaped = hidden.reshape(h2 * w2, n, c)
        first, second = jnp.sum(shaped, axis=0), jnp.sum(shaped * shaped, axis=0)
        m = n // MICRO
        for i in range(MICRO):
            sums_ref[i : i + 1, :] = jnp.sum(first[i * m : (i + 1) * m], axis=0, keepdims=True)
            sums_ref[MICRO + i : MICRO + i + 1, :] = jnp.sum(
                second[i * m : (i + 1) * m], axis=0, keepdims=True
            )


def conv_one(row, blocks, weight, pixels):
    h, w, n = pixels
    c = weight.shape[-1]
    return pl.pallas_call(
        conv_one_kernel,
        out_shape=(
            jax.ShapeDtypeStruct((2 * h, 2 * w, n, c), f32),
            jax.ShapeDtypeStruct((2 * MICRO, c), f32),
        ),
        grid_spec=pltpu.PrefetchScalarGridSpec(
            num_scalar_prefetch=1,
            grid=(9,),
            in_specs=[whole(b.shape) for b in blocks]
            + [pl.BlockSpec((1,) + weight.shape[1:], lambda t, r: (t, 0, 0))],
            out_specs=(whole((2 * h, 2 * w, n, c)), whole((2 * MICRO, c))),
            scratch_shapes=[pltpu.VMEM((2 * h + 2, 2 * w + 2, n, c), f32)],
        ),
        compiler_params=kernel_params(),
        name="conv_one",
    )(row, *blocks, weight)


def conv_two_kernel(count, row_ref, *refs):
    blocks, raws = refs[:count], refs[count : 2 * count]
    w_ref, skip_ref, colour_ref, sum_ref, act_ref, pic_ref, pad_ref, apad_ref = refs[2 * count :]
    h2, w2, n, c = sum_ref.shape
    t = pl.program_id(0)
    dy, dx = lax.div(t, 3), lax.rem(t, 3)

    @pl.when(t == 0)
    def _():
        pad_ref[...] = jnp.zeros_like(pad_ref)
        for k in range(count):
            pad_ref[k, 1 : h2 + 1, 1 : w2 + 1] = blocks[k][...]
        skipped = sum(
            times(x_ref[x_ref.shape[0] - 1], skip_ref[owned_rows(row_ref, k, x_ref.shape[2]), :])
            for k, x_ref in enumerate(raws)
        )
        sum_ref[...] = raise_two(skipped.reshape(h2 // 2, w2 // 2, n, c))

    product = sum(
        times(
            flat(pad_ref[k, pl.ds(dy, h2), pl.ds(dx, w2)]), w_ref[0, owned_rows(row_ref, k, c), :]
        )
        for k in range(count)
    )
    sum_ref[...] += product.reshape(sum_ref.shape)

    @pl.when(t == 8)
    def _():
        active = jax.nn.silu(sum_ref[...]).astype(bf16)
        act_ref[...] = active
        apad_ref[...] = jnp.zeros_like(apad_ref)
        apad_ref[1 : h2 + 1, 1 : w2 + 1] = active
        picture = jnp.zeros(pic_ref.shape, f32)
        for tap in range(9):
            y, x = divmod(tap, 3)
            picture = picture + contract_last(
                colour_ref[tap], flat(apad_ref[y : y + h2, x : x + w2])
            )
        pic_ref[...] = picture


def conv_two(row, blocks, raws, weight, skip, colour):
    h2, w2, n, c = blocks[0].shape
    return pl.pallas_call(
        functools.partial(conv_two_kernel, len(blocks)),
        out_shape=(
            jax.ShapeDtypeStruct((h2, w2, n, c), f32),
            jax.ShapeDtypeStruct((h2, w2, n, c), bf16),
            jax.ShapeDtypeStruct((PAD, h2 * w2 * n), f32),
        ),
        grid_spec=pltpu.PrefetchScalarGridSpec(
            num_scalar_prefetch=1,
            grid=(9,),
            in_specs=[whole(b.shape) for b in blocks + raws]
            + [
                pl.BlockSpec((1,) + weight.shape[1:], lambda t, r: (t, 0, 0)),
                whole(skip.shape),
                whole(colour.shape),
            ],
            out_specs=(whole((h2, w2, n, c)), whole((h2, w2, n, c)), whole((PAD, h2 * w2 * n))),
            scratch_shapes=[
                pltpu.VMEM((len(blocks), h2 + 2, w2 + 2, n, c), bf16),
                pltpu.VMEM((h2 + 2, w2 + 2, n, c), bf16),
            ],
        ),
        compiler_params=kernel_params(28),
        name="conv_two",
    )(row, *blocks, *raws, weight, skip, colour)


def critic_kernel(
    dims, pic_ref, first_ref, second_ref, skip_ref, head_ref, count_ref, out_ref, loss_ref, small_ref, pad_ref
):
    h2, w2, n = dims
    h, w = h2 // 2, w2 // 2
    c = second_ref.shape[-1]
    taps = [divmod(tap, 3) for tap in range(9)]
    shade = jnp.tanh(jnp.transpose(pic_ref[...]))
    picture = shade.astype(bf16).reshape(h2, w2, n, PAD)
    small_ref[...] = jnp.zeros_like(small_ref)
    small_ref[1 : h2 + 1, 1 : w2 + 1] = picture
    pad_ref[...] = jnp.zeros_like(pad_ref)
    front_pre = sum(
        times(flat(small_ref[y : y + h2, x : x + w2]), first_ref[3 * y + x]) for y, x in taps
    )
    pad_ref[1 : h2 + 1, 1 : w2 + 1] = jax.nn.silu(front_pre).astype(bf16).reshape(h2, w2, n, c)
    merged = sum(times(flat(pad_ref[y : y + h2, x : x + w2]), second_ref[3 * y + x]) for y, x in taps)
    merged = 0.25 * flat(sum_two(merged.reshape(h2, w2, n, c)))
    small = 0.25 * flat(sum_two(picture.astype(f32)))
    skip = skip_ref[...].astype(f32)
    for i in range(3):
        merged = merged + small[:, i : i + 1] * skip[i : i + 1, :]
    feature = jnp.sum(jax.nn.silu(merged).reshape(h * w, n, c), axis=0)
    weights = head_ref[...] * count_ref[...]
    loss_ref[...] = jnp.broadcast_to(-jnp.sum(feature * weights, keepdims=True), loss_ref.shape)
    grad_merged = (silu_slope(merged).reshape(h * w, n, c) * -weights[None]).astype(bf16)
    grad_merged = grad_merged.reshape(h, w, n, c)
    grad_pool = raise_two(grad_merged) * jnp.bfloat16(0.25)
    pad_ref[1 : h2 + 1, 1 : w2 + 1] = grad_pool
    grad_front = sum(
        contract_last(flat(pad_ref[2 - y : 2 - y + h2, 2 - x : 2 - x + w2]), second_ref[3 * y + x])
        for y, x in taps
    )
    grad_front_pre = (grad_front * silu_slope(front_pre)).astype(bf16)
    pad_ref[1 : h2 + 1, 1 : w2 + 1] = grad_front_pre.reshape(h2, w2, n, c)
    grad_picture = sum(
        contract_last(flat(pad_ref[2 - y : 2 - y + h2, 2 - x : 2 - x + w2]), first_ref[3 * y + x])
        for y, x in taps
    )
    grad_skip = contract_last(flat(grad_merged), skip_ref[...]).reshape(h, w, n, PAD)
    grad_picture = grad_picture + 0.25 * flat(raise_two(grad_skip))
    grad_pre = (grad_picture * (1.0 - shade * shade)).astype(bf16)
    small_ref[1 : h2 + 1, 1 : w2 + 1] = grad_pre.reshape(h2, w2, n, PAD)
    out_ref[...] = jnp.concatenate(
        [flat(small_ref[2 - y : 2 - y + h2, 2 - x : 2 - x + w2]) for y, x in taps]
        + [jnp.zeros((h2 * w2 * n, 128 - 9 * PAD), bf16)],
        axis=1,
    )


def critic(picture, disc_first, disc_second, disc_skip, head, counted, dims):
    h2, w2, n = dims
    c = disc_second.shape[-1]
    return pl.pallas_call(
        functools.partial(critic_kernel, dims),
        out_shape=(
            jax.ShapeDtypeStruct((h2 * w2 * n, 128), bf16),
            jax.ShapeDtypeStruct((8, 128), f32),
        ),
        scratch_shapes=[
            pltpu.VMEM((h2 + 2, w2 + 2, n, PAD), bf16),
            pltpu.VMEM((h2 + 2, w2 + 2, n, c), bf16),
        ],
        compiler_params=kernel_params(28),
        name="critic",
    )(picture, disc_first, disc_second, disc_skip, head, counted)


def back_two_kernel(count, row_ref, g_ref, sum_ref, act_ref, colour_ref, w_ref, *refs):
    gpad_ref, gcol_ref = refs[0], refs[1]
    outs, acc_ref = refs[2:-1], refs[-1]
    h2, w2, n, c = sum_ref.shape
    t = pl.program_id(0)
    dy, dx = lax.div(t, 3), lax.rem(t, 3)

    @pl.when(t == 0)
    def _():
        grad_active = times(g_ref[...], colour_ref[...]).reshape(h2, w2, n, c)
        gpad_ref[...] = jnp.zeros_like(gpad_ref)
        gpad_ref[1 : h2 + 1, 1 : w2 + 1] = (grad_active * silu_slope(sum_ref[...])).astype(bf16)
        gcol_ref[...] = lax.dot_general(
            g_ref[...], flat(act_ref[...]), (((0,), (0,)), ((), ())), preferred_element_type=f32
        )
        acc_ref[...] = jnp.zeros_like(acc_ref)

    shifted = flat(gpad_ref[pl.ds(2 - dy, h2), pl.ds(2 - dx, w2)])
    for k in range(count):
        acc_ref[k] += contract_last(shifted, w_ref[0, owned_rows(row_ref, k, c), :])

    @pl.when(t == 8)
    def _():
        for k in range(count):
            outs[k][...] = acc_ref[k].astype(bf16)


def back_two(row, grads, summed, active, colour, weight, count):
    h2, w2, n, c = summed.shape
    rows = h2 * w2 * n
    return pl.pallas_call(
        functools.partial(back_two_kernel, count),
        out_shape=(
            jax.ShapeDtypeStruct((h2 + 2, w2 + 2, n, c), bf16),
            jax.ShapeDtypeStruct((128, c), f32),
        )
        + tuple(jax.ShapeDtypeStruct((rows, c), bf16) for _ in range(count)),
        grid_spec=pltpu.PrefetchScalarGridSpec(
            num_scalar_prefetch=1,
            grid=(9,),
            in_specs=[
                whole(grads.shape),
                whole(summed.shape),
                whole(active.shape),
                whole(colour.shape),
                pl.BlockSpec((1,) + weight.shape[1:], lambda t, r: (t, 0, 0)),
            ],
            out_specs=(whole((h2 + 2, w2 + 2, n, c)), whole((128, c)))
            + tuple(whole((rows, c)) for _ in range(count)),
            scratch_shapes=[pltpu.VMEM((count, rows, c), f32)],
        ),
        compiler_params=kernel_params(28),
        name="back_two",
    )(row, grads, summed, active, colour, weight)


def weight_two_kernel(count, row_ref, gpad_ref, *refs):
    blocks, raws, (out_ref, skip_ref) = refs[:count], refs[count : 2 * count], refs[2 * count :]
    h2, w2, n, c = (gpad_ref.shape[0] - 2, gpad_ref.shape[1] - 2) + gpad_ref.shape[2:]
    t = pl.program_id(0)
    dy, dx = lax.div(t, 3), lax.rem(t, 3)
    shifted = flat(gpad_ref[pl.ds(2 - dy, h2), pl.ds(2 - dx, w2)])
    for k in range(count):
        out_ref[0, owned_rows(row_ref, k, c), :] = times(blocks[k][...], shifted).astype(bf16)

    @pl.when(t == 8)
    def _():
        phases = gpad_ref[1 : h2 + 1, 1 : w2 + 1].reshape(h2 // 2, 2, w2 // 2, 2, n, c)
        for k in range(count):
            size = raws[k].shape[0]
            skip_ref[owned_rows(row_ref, k, size), :] = sum(
                times(raws[k][...], flat(phases[:, a, :, b])) for a in range(2) for b in range(2)
            ).astype(bf16)


def weight_two(row, gpad, blocks, raws):
    c = gpad.shape[-1]
    count = len(blocks)
    tall, wide = count * blocks[0].shape[0], count * raws[0].shape[0]
    return pl.pallas_call(
        functools.partial(weight_two_kernel, count),
        out_shape=(
            jax.ShapeDtypeStruct((9, tall, c), bf16),
            jax.ShapeDtypeStruct((wide, c), bf16),
        ),
        grid_spec=pltpu.PrefetchScalarGridSpec(
            num_scalar_prefetch=1,
            grid=(9,),
            in_specs=[whole(gpad.shape)] + [whole(b.shape) for b in blocks + raws],
            out_specs=(pl.BlockSpec((1, tall, c), lambda t, r: (t, 0, 0)), whole((wide, c))),
        ),
        compiler_params=kernel_params(28),
        name="weight_two",
    )(row, gpad, *blocks, *raws)


def back_one_kernel(count, row_ref, g_ref, w_ref, *refs):
    blocks, out_ref, outs = refs[:count], refs[count], refs[count + 1 : 2 * count + 1]
    pad_ref, acc_ref = refs[2 * count + 1 :]
    h2, w2, n, c = g_ref.shape
    size = blocks[0].shape[0]
    t = pl.program_id(0)
    dy, dx = lax.div(t, 3), lax.rem(t, 3)

    @pl.when(t == 0)
    def _():
        pad_ref[...] = jnp.zeros_like(pad_ref)
        pad_ref[1 : h2 + 1, 1 : w2 + 1] = g_ref[...]
        acc_ref[...] = jnp.zeros_like(acc_ref)

    shifted = pad_ref[pl.ds(2 - dy, h2), pl.ds(2 - dx, w2)].astype(f32)
    pooled = flat(sum_two(shifted)).astype(bf16)
    for k in range(count):
        rows = owned_rows(row_ref, k, size)
        acc_ref[k] += contract_last(pooled, w_ref[0, rows, :])
        out_ref[0, rows, :] = times(blocks[k][...], pooled).astype(bf16)

    @pl.when(t == 8)
    def _():
        for k in range(count):
            outs[k][...] = acc_ref[k].astype(bf16)


def back_one(row, grads, weight, blocks):
    h2, w2, n, c = grads.shape
    count = len(blocks)
    size, rows = blocks[0].shape
    return pl.pallas_call(
        functools.partial(back_one_kernel, count),
        out_shape=(jax.ShapeDtypeStruct((9, count * size, c), bf16),)
        + tuple(jax.ShapeDtypeStruct((rows, size), bf16) for _ in range(count)),
        grid_spec=pltpu.PrefetchScalarGridSpec(
            num_scalar_prefetch=1,
            grid=(9,),
            in_specs=[
                whole(grads.shape),
                pl.BlockSpec((1,) + weight.shape[1:], lambda t, r: (t, 0, 0)),
            ]
            + [whole(b.shape) for b in blocks],
            out_specs=(pl.BlockSpec((1, count * size, c), lambda t, r: (t, 0, 0)),)
            + tuple(whole((rows, size)) for _ in range(count)),
            scratch_shapes=[
                pltpu.VMEM((h2 + 2, w2 + 2, n, c), bf16),
                pltpu.VMEM((count, rows, size), f32),
            ],
        ),
        compiler_params=kernel_params(28),
        name="back_one",
    )(row, grads, weight, *blocks)


def in_order(pieces, axis_name):
    piled = jnp.stack(pieces, axis=0)
    r = lax.axis_index(axis_name)
    return jnp.concatenate(
        [
            lax.dynamic_index_in_dim(piled, lax.bitwise_xor(r, j), 0, keepdims=False)
            for j in range(len(pieces))
        ],
        axis=0,
    )


def gram_share(owned, pieces):
    blocks = [
        lax.dot_general(piece, owned, (((0,), (0,)), ((), ())), preferred_element_type=f32)
        for piece in pieces
    ]
    return in_order(blocks, "row")


def gram_whole(panel):
    n = lax.axis_size("dp")
    h, z = lax.axis_index("half"), lax.axis_index("dp")
    total = group_sum_wide(panel)
    pieces = row_gather(total)
    piled = jnp.stack(pieces, axis=0)
    r = lax.axis_index("row")
    return jnp.concatenate(
        [
            lax.dynamic_index_in_dim(piled, lax.bitwise_xor(r, j), 0, keepdims=False)
            for j in range(len(pieces))
        ],
        axis=1,
    )


def group_sum_wide(value):
    return group_gather(group_scatter(value))


def mul(left, right):
    return jnp.dot(left, right, precision=high, preferred_element_type=f32)


def newton_columns(gram, own):
    scale = lax.rsqrt(jnp.trace(gram) + NEWTON_EPSILON)
    current = gram * (scale * scale)
    identity = jnp.eye(gram.shape[0], dtype=f32)
    maps = []
    for iteration in range(NS_ITERS):
        square = mul(current, current)
        mapping = NS_COEF[0] * identity + NS_COEF[1] * current + NS_COEF[2] * square
        maps.append(mapping)
        if iteration < NS_ITERS - 1:
            current = mul(mapping, mul(current, mapping))
    start = lax.axis_index("row") * own
    columns = lax.dynamic_slice_in_dim(maps[-1], start, own, 1)
    for mapping in maps[-2::-1]:
        columns = mul(mapping, columns)
    return columns * scale


def muon(master, moment, gradient, groups):
    moment_new = MOMENTUM * moment + gradient
    owned = moment_new.astype(bf16)
    pieces = row_gather(owned)
    own = owned.shape[1]
    gram = gram_whole(gram_share(owned, pieces))
    columns = newton_columns(gram, own).astype(bf16)
    r = lax.axis_index("row")
    direction = sum(
        times(
            piece,
            lax.dynamic_slice_in_dim(columns, lax.bitwise_xor(r, k) * own, own, 0),
        )
        for k, piece in enumerate(pieces)
    )
    factor = 0.2 * math.sqrt(max(master.shape[0] * groups, own * len(pieces)))
    return master - MUON_RATE * (factor * direction + DECAY * master), moment_new


def transposed(values):
    return jnp.transpose(values.astype(f32)).astype(values.dtype)


def place_kernel(count, sizes, index_ref, mine_ref, other_ref, *refs):
    outs = refs[-len(sizes) :]

    def write(values):
        turned = jnp.transpose(values.astype(f32)).astype(bf16)
        start = 0
        for size, out_ref in zip(sizes, outs):
            out_ref[...] = turned[start : start + size]
            start += size

    @pl.when(pl.program_id(0) < count)
    def _():
        write(mine_ref[0])

    @pl.when(pl.program_id(0) >= count)
    def _():
        write(other_ref[0])


def place(held, index, mine, other, sizes):
    count, c, wide = mine.shape
    groups = 2 * lax.axis_size("dp")
    given = [] if held is None else list(held)
    return pl.pallas_call(
        functools.partial(place_kernel, count, sizes),
        out_shape=tuple(jax.ShapeDtypeStruct((groups * size, c), bf16) for size in sizes),
        grid_spec=pltpu.PrefetchScalarGridSpec(
            num_scalar_prefetch=1,
            grid=(2 * count,),
            in_specs=[
                pl.BlockSpec((1, c, wide), lambda t, r: (jnp.minimum(t, count - 1), 0, 0)),
                pl.BlockSpec((1, c, wide), lambda t, r: (jnp.maximum(t - count, 0), 0, 0)),
            ]
            + [pl.BlockSpec(memory_space=pl.ANY) for _ in given],
            out_specs=tuple(pl.BlockSpec((size, c), lambda t, r: (r[t], 0)) for size in sizes),
        ),
        input_output_aliases={3 + i: i for i in range(len(given))},
        compiler_params=kernel_params(),
        name="place",
    )(jnp.stack(index).astype(jnp.int32), mine, other, *given)


def place_cores(held, spots, mine, sizes):
    n = lax.axis_size("dp")
    h = lax.axis_index("half")
    index = [h * n + spot for spot in spots] + [(1 - h) * n + spot for spot in spots]
    return place(held, index, mine, axis_swap(mine, "half", 1), sizes)


def weight_one_kernel(groups, where_ref, inverse_ref, *refs):
    pieces = refs[:groups]
    all_ref, old_ref, out_ref, low_ref, pad_ref, pool_ref, grads, inputs_ref, moment_ref, sem = refs[
        groups:
    ]
    copies = [
        pltpu.make_async_copy(piece, grads.at[g], sem.at[g]) for g, piece in enumerate(pieces)
    ]
    copies.append(pltpu.make_async_copy(all_ref, inputs_ref, sem.at[groups]))
    copies.append(pltpu.make_async_copy(old_ref, moment_ref, sem.at[groups + 1]))
    for copy in copies:
        copy.start()
    h2, w2, n, c = grads.shape[1:]
    size = h2 * w2 * n // 4
    row, d = where_ref[0], where_ref[1] * (groups // 2) + where_ref[2]
    owners = []
    for side in range(2):
        for k in range(groups // 2):
            spot = lax.rem(where_ref[2] + groups // 2 - k, groups // 2)
            owners.append((where_ref[1] if side == 0 else 1 - where_ref[1]) * (groups // 2) + spot)
    pad_ref[...] = jnp.zeros_like(pad_ref)
    for g in range(groups):
        copies[g].wait()
        pad_ref[1 : h2 + 1, 1 : w2 + 1] = grads[g]
        for j in range(2):
            dy, dx = lax.div(d + j, 3), lax.rem(d + j, 3)
            shifted = pad_ref[pl.ds(2 - dy, h2), pl.ds(2 - dx, w2)].astype(f32)
            pool_ref[j, g * size : (g + 1) * size, :] = flat(sum_two(shifted)).astype(bf16)
    copies[groups].wait()
    copies[groups + 1].wait()
    inverse = inverse_ref[0, 0]
    for q in range(groups + 1):
        i = lax.rem(d + q, groups)
        j = lax.div(d + q, groups)
        start = lax.bitwise_xor(row, lax.div(i, 2)) * (2 * c) + lax.rem(i, 2) * c
        start = pl.multiple_of(start, c)
        total = sum(
            times(inputs_ref[owners[g], pl.ds(start, c), :], pool_ref[j, g * size : (g + 1) * size, :])
            for g in range(groups)
        )
        span = slice(q * c, (q + 1) * c)
        moment = MOMENTUM * moment_ref[:, span] + jnp.transpose(total) * inverse
        out_ref[:, span] = moment
        low_ref[:, span] = moment.astype(bf16)


def weight_one_moment(where, inverse, grads, inputs, moment):
    h2, w2, n, c = grads[0].shape
    groups = len(grads)
    vmem = pl.BlockSpec(memory_space=pltpu.VMEM)
    smem = pl.BlockSpec(memory_space=pltpu.SMEM)
    flops = 2 * moment.shape[1] * c * groups * h2 * w2 * n // 4
    return pl.pallas_call(
        functools.partial(weight_one_kernel, groups),
        out_shape=(
            jax.ShapeDtypeStruct(moment.shape, f32),
            jax.ShapeDtypeStruct(moment.shape, bf16),
        ),
        in_specs=[smem, smem] + [pl.BlockSpec(memory_space=pl.ANY)] * (groups + 2),
        out_specs=(vmem, vmem),
        scratch_shapes=[
            pltpu.VMEM((h2 + 2, w2 + 2, n, c), bf16),
            pltpu.VMEM((2, groups * h2 * w2 * n // 4, c), bf16),
            pltpu.VMEM((groups,) + grads[0].shape, bf16),
            pltpu.VMEM(inputs.shape, bf16),
            pltpu.VMEM(moment.shape, f32),
            pltpu.SemaphoreType.DMA((groups + 2,)),
        ],
        compiler_params=kernel_params(28),
        cost_estimate=pl.CostEstimate(flops=4 * flops, bytes_accessed=0, transcendentals=0),
        name="weight_one",
    )(where, inverse, *grads, inputs, moment)


def weight_pack_kernel(count, row_ref, gpad_ref, *refs):
    blocks, raws, (out_ref, tall_ref) = refs[:count], refs[count : 2 * count], refs[2 * count :]
    h2, w2, n, c = (gpad_ref.shape[0] - 2, gpad_ref.shape[1] - 2) + gpad_ref.shape[2:]
    groups = out_ref.shape[0]
    unit = count * c // groups
    half = unit // 2
    t = pl.program_id(0)
    dy, dx = lax.div(t, 3), lax.rem(t, 3)
    shifted = flat(gpad_ref[pl.ds(2 - dy, h2), pl.ds(2 - dx, w2)])
    for k in range(count):
        tall_ref[owned_rows(row_ref, k, c), :] = times(blocks[k][...], shifted)
    for i in range(groups):
        rows = tall_ref[i * unit : (i + 1) * unit, :]
        u = groups * t + i
        packed = jnp.concatenate([rows[:half], rows[half:]], axis=1).astype(bf16)
        spot = pl.multiple_of(lax.rem(u, groups + 1) * half, half)
        out_ref[lax.div(u, groups + 1), pl.ds(spot, half), :] = packed

    @pl.when(t == 8)
    def _():
        phases = gpad_ref[1 : h2 + 1, 1 : w2 + 1].reshape(h2 // 2, 2, w2 // 2, 2, n, c)
        size = raws[0].shape[0]
        each = count * size // groups
        for k in range(count):
            block = sum(
                times(raws[k][...], flat(phases[:, a, :, b])) for a in range(2) for b in range(2)
            )
            for m in range(size // each):
                rows = block[m * each : (m + 1) * each]
                packed = jnp.concatenate([rows[: each // 2], rows[each // 2 :]], axis=1)
                spot = lax.bitwise_xor(row_ref[0], k) * (size // each) + m
                out_ref[spot, (groups + 1) * half :, :] = packed.astype(bf16)


def weight_pack(row, gpad, blocks, raws, groups):
    c = gpad.shape[-1]
    count = len(blocks)
    tall, wide = count * blocks[0].shape[0], count * raws[0].shape[0]
    shape = (groups, (9 * tall + wide) // (2 * groups), 2 * c)
    flops = 2 * 9 * tall * c * blocks[0].shape[1]
    return pl.pallas_call(
        functools.partial(weight_pack_kernel, count),
        out_shape=jax.ShapeDtypeStruct(shape, bf16),
        grid_spec=pltpu.PrefetchScalarGridSpec(
            num_scalar_prefetch=1,
            grid=(9,),
            in_specs=[whole(gpad.shape)] + [whole(b.shape) for b in blocks + raws],
            out_specs=whole(shape),
            scratch_shapes=[pltpu.VMEM((tall, c), f32)],
        ),
        compiler_params=kernel_params(28),
        cost_estimate=pl.CostEstimate(flops=3 * flops, bytes_accessed=0, transcendentals=0),
        name="weight_two",
    )(row, gpad, *blocks, *raws)


def moments_kernel(count, inverse_ref, *refs):
    pieces = refs[:count]
    tall_ref, skip_ref, tall_out, skip_out, low_ref = refs[count:]
    c, size = tall_ref.shape
    total = pieces[0][...].astype(f32)
    for piece in pieces[1:]:
        total = total + piece[...].astype(f32)
    total = total * inverse_ref[0, 0]
    units = 9
    half = size // (2 * units)
    for q in range(units):
        rows = total[q * half : (q + 1) * half]
        rows = jnp.concatenate([rows[:, :c], rows[:, c:]], axis=0)
        span = slice(2 * q * half, 2 * (q + 1) * half)
        moment = MOMENTUM * tall_ref[:, span] + jnp.transpose(rows)
        tall_out[:, span] = moment
        low_ref[:, span] = moment.astype(bf16)
    rows = total[units * half :]
    rows = jnp.concatenate([rows[:, :c], rows[:, c:]], axis=0)
    moment = MOMENTUM * skip_ref[...] + jnp.transpose(rows)
    skip_out[...] = moment
    low_ref[:, size:] = moment.astype(bf16)


def moments_two(inverse, pieces, tall, skip):
    vmem = pl.BlockSpec(memory_space=pltpu.VMEM)
    return pl.pallas_call(
        functools.partial(moments_kernel, len(pieces)),
        out_shape=(
            jax.ShapeDtypeStruct(tall.shape, f32),
            jax.ShapeDtypeStruct(skip.shape, f32),
            jax.ShapeDtypeStruct((tall.shape[0], tall.shape[1] + skip.shape[1]), bf16),
        ),
        in_specs=[pl.BlockSpec(memory_space=pltpu.SMEM)] + [vmem] * (len(pieces) + 2),
        out_specs=(vmem, vmem, vmem),
        compiler_params=kernel_params(),
        name="moments",
    )(inverse, *pieces, tall, skip)


def gram_kernel(count, spans, row_ref, *refs):
    pieces, out_ref, hold_ref = refs[:count], refs[count], refs[count + 1]
    for m, (start, stop) in enumerate(spans):
        owned = pieces[0][:, start:stop]
        for k in range(count):
            hold_ref[k] = contract_last(owned, pieces[k][:, start:stop])
        out_ref[m] = jnp.concatenate(
            [hold_ref[lax.bitwise_xor(row_ref[0], j)] for j in range(count)], axis=1
        )


def gram_rows(row, pieces, spans):
    c = pieces[0].shape[0]
    count = len(pieces)
    vmem = pl.BlockSpec(memory_space=pltpu.VMEM)
    return pl.pallas_call(
        functools.partial(gram_kernel, count, spans),
        out_shape=jax.ShapeDtypeStruct((len(spans), c, count * c), f32),
        in_specs=[pl.BlockSpec(memory_space=pltpu.SMEM)] + [vmem] * count,
        out_specs=vmem,
        scratch_shapes=[pltpu.VMEM((count, c, c), f32)],
        compiler_params=kernel_params(),
        cost_estimate=pl.CostEstimate(
            flops=6 * count * c * c * pieces[0].shape[1], bytes_accessed=0, transcendentals=0
        ),
        name="gram",
    )(row, *pieces)


def gram_terms(halves):
    kept = near_halves(halves)
    return near_blocks(kept, kept)


def gram_total(terms):
    return placed_in_order(straight(sum(terms)))


def newton_kernel(count, sides, where_ref, *refs):
    pieces = refs[: sides * count]
    out_ref, a_ref, ah, al, maps_ref, th, tl = refs[sides * count :]
    size = a_ref.shape[0]
    own = size // count
    block = size // 3
    row, h = where_ref[0], where_ref[1]
    for q in range(count):
        for side in range(sides):
            piece = pieces[side * count + q]
            s = piece.shape[2]
            half = 0 if sides == 1 else (h if side == 0 else 1 - h)
            for p in range(piece.shape[0]):
                start = lax.bitwise_xor(row, q) * own + half * (own // 2) + p * s
                a_ref[pl.ds(pl.multiple_of(start, s), s), :] = piece[p, 0]

    def eye(shape, offset):
        rows = lax.broadcasted_iota(jnp.int32, shape, 0) + offset
        return rows == lax.broadcasted_iota(jnp.int32, shape, 1)

    whole_gram = a_ref[...]
    trace = jnp.sum(jnp.where(eye(whole_gram.shape, 0), whole_gram, 0.0), keepdims=True)
    scale = lax.rsqrt(trace + NEWTON_EPSILON)
    a_ref[...] = whole_gram * (scale * scale)

    def split(values):
        top = values.astype(bf16)
        return top, (values - top.astype(f32)).astype(bf16)

    def three(xh, xl, yh, yl):
        return times(xh, yh) + (times(xh, yl) + times(xl, yh))

    spans = [slice(i * block, (i + 1) * block) for i in range(3)]

    def symmetric(product, write):
        for i in range(3):
            for j in range(i, 3):
                write(i, j, product(spans[i], spans[j]))

    def store(high_ref, low_ref, i, j, value):
        top, low = split(value)
        high_ref[spans[i], spans[j]] = top
        low_ref[spans[i], spans[j]] = low
        if i != j:
            turned = jnp.transpose(value)
            top, low = split(turned)
            high_ref[spans[j], spans[i]] = top
            low_ref[spans[j], spans[i]] = low

    top, low = split(a_ref[...])
    ah[...] = top
    al[...] = low

    def step(k, carry):
        top = maps_ref.at[k]

        def write_map(i, j, value):
            value = NS_COEF[1] * a_ref[spans[i], spans[j]] + NS_COEF[2] * value
            if i == j:
                value = value + jnp.where(eye(value.shape, 0), NS_COEF[0], 0.0)
            top[spans[i], spans[j]] = value.astype(bf16)
            if i != j:
                top[spans[j], spans[i]] = jnp.transpose(value).astype(bf16)

        symmetric(lambda a, b: three(ah[a, :], al[a, :], ah[:, b], al[:, b]), write_map)
        symmetric(
            lambda a, b: times(ah[a, :], top[:, b]) + times(al[a, :], top[:, b]),
            functools.partial(store, th, tl),
        )

        def write_gram(i, j, value):
            a_ref[spans[i], spans[j]] = value
            store(ah, al, i, j, value)
            if i != j:
                a_ref[spans[j], spans[i]] = jnp.transpose(value)

        symmetric(lambda a, b: times(top[a, :], th[:, b]) + times(top[a, :], tl[:, b]), write_gram)
        return carry

    lax.fori_loop(0, NS_ITERS - 1, step, 0)
    mine = pl.ds(pl.multiple_of(row * own, own), own)
    last = a_ref[mine, :]
    columns = NS_COEF[1] * last + NS_COEF[2] * three(ah[mine, :], al[mine, :], ah[...], al[...])
    columns = columns + jnp.where(eye(columns.shape, row * own), NS_COEF[0], 0.0)

    def fold(k, columns):
        high_part, low_part = split(columns)
        top = maps_ref[NS_ITERS - 2 - k]
        return times(high_part, top) + times(low_part, top)

    columns = lax.fori_loop(0, NS_ITERS - 1, fold, columns) * scale
    for j in range(count):
        out_ref[0, j] = columns[:, j * own : (j + 1) * own].astype(bf16)


def newton(where, pieces, count):
    sides = len(pieces) // count
    n, m, s, size = pieces[0].shape
    own = size // count
    square = (size, size)
    maps = (NS_ITERS - 1,) + square
    return pl.pallas_call(
        functools.partial(newton_kernel, count, sides),
        out_shape=jax.ShapeDtypeStruct((m, count, own, own), bf16),
        grid_spec=pltpu.PrefetchScalarGridSpec(
            num_scalar_prefetch=1,
            grid=(m,),
            in_specs=[pl.BlockSpec((n, 1, s, size), lambda t, r: (0, t, 0, 0)) for _ in pieces],
            out_specs=pl.BlockSpec((1, count, own, own), lambda t, r: (t, 0, 0, 0)),
            scratch_shapes=[
                pltpu.VMEM(square, f32),
                pltpu.VMEM(square, bf16),
                pltpu.VMEM(square, bf16),
                pltpu.VMEM(maps, bf16),
                pltpu.VMEM(square, bf16),
                pltpu.VMEM(square, bf16),
            ],
        ),
        compiler_params=kernel_params(36),
        cost_estimate=pl.CostEstimate(
            flops=m * 50 * size**3, bytes_accessed=0, transcendentals=0
        ),
        name="newton",
    )(where, *pieces)


def update_kernel(count, spans, factors, row_ref, map_ref, *refs):
    pieces, masters, outs = refs[:count], refs[count : count + len(spans)], refs[count + len(spans) :]
    for m, (start, stop) in enumerate(spans):
        direction = sum(
            times(map_ref[m, lax.bitwise_xor(row_ref[0], k)], pieces[k][:, start:stop])
            for k in range(count)
        )
        master = masters[m][...]
        outs[m][...] = master - MUON_RATE * (factors[m] * direction + DECAY * master)


def update(row, maps, pieces, masters, spans, factors):
    count = len(pieces)
    vmem = pl.BlockSpec(memory_space=pltpu.VMEM)
    return pl.pallas_call(
        functools.partial(update_kernel, count, spans, factors),
        out_shape=tuple(jax.ShapeDtypeStruct(master.shape, f32) for master in masters),
        in_specs=[pl.BlockSpec(memory_space=pltpu.SMEM)] + [vmem] * (1 + count + len(masters)),
        out_specs=(vmem,) * len(masters),
        compiler_params=kernel_params(),
        name="update",
    )(row, maps, *pieces, *masters)


def back_in_kernel(count, row_ref, g_ref, w_ref, *refs):
    outs, (pad_ref, acc_ref) = refs[:count], refs[count:]
    h2, w2, n, c = g_ref.shape
    size = outs[0].shape[1]
    t = pl.program_id(0)
    dy, dx = lax.div(t, 3), lax.rem(t, 3)

    @pl.when(t == 0)
    def _():
        pad_ref[...] = jnp.zeros_like(pad_ref)
        pad_ref[1 : h2 + 1, 1 : w2 + 1] = g_ref[...]
        acc_ref[...] = jnp.zeros_like(acc_ref)

    shifted = pad_ref[pl.ds(2 - dy, h2), pl.ds(2 - dx, w2)].astype(f32)
    pooled = flat(sum_two(shifted)).astype(bf16)
    for k in range(count):
        acc_ref[k] += contract_last(pooled, w_ref[0, owned_rows(row_ref, k, size), :])

    @pl.when(t == 8)
    def _():
        for k in range(count):
            outs[k][...] = acc_ref[k].astype(bf16)


def back_in(row, grads, weight, count):
    h2, w2, n, c = grads.shape
    size, rows = weight.shape[1] // count, h2 * w2 * n // 4
    return pl.pallas_call(
        functools.partial(back_in_kernel, count),
        out_shape=tuple(jax.ShapeDtypeStruct((rows, size), bf16) for _ in range(count)),
        grid_spec=pltpu.PrefetchScalarGridSpec(
            num_scalar_prefetch=1,
            grid=(9,),
            in_specs=[
                whole(grads.shape),
                pl.BlockSpec((1,) + weight.shape[1:], lambda t, r: (t, 0, 0)),
            ],
            out_specs=tuple(whole((rows, size)) for _ in range(count)),
            scratch_shapes=[
                pltpu.VMEM((h2 + 2, w2 + 2, n, c), bf16),
                pltpu.VMEM((count, rows, size), f32),
            ],
        ),
        compiler_params=kernel_params(28),
        cost_estimate=pl.CostEstimate(
            flops=6 * 9 * rows * count * size * c, bytes_accessed=0, transcendentals=0
        ),
        name="back_one",
    )(row, grads, weight)


def adam_update(weight, gradient, mean_old, square_old, rate):
    mean_new = BETA_ONE * mean_old + (1.0 - BETA_ONE) * gradient
    square_new = BETA_TWO * square_old + (1.0 - BETA_TWO) * gradient * gradient
    ratio = (
        mean_new
        / (1.0 - BETA_ONE**STEP)
        / (jnp.sqrt(square_new / (1.0 - BETA_TWO**STEP)) + ADAM_EPS)
    )
    return (weight - rate * (ratio + DECAY * weight), mean_new, square_new)


def moments_of(totals, count):
    centre = totals[:MICRO] / count
    return centre, lax.rsqrt(totals[MICRO:] / count - centre * centre + BN_EPS)


def per_image(values, n):
    return jnp.repeat(values, n // MICRO, axis=0)


def per_micro(values):
    return jnp.sum(values.reshape(MICRO, -1, values.shape[-1]), axis=1)


def wide_device(
    features,
    noise,
    labels,
    counted,
    disc_first,
    disc_second,
    disc_skip,
    disc_head,
    disc_table,
    conv_first,
    conv_second,
    conv_skip,
    momentum_first,
    momentum_second,
    momentum_skip,
    class_table,
    table_mean,
    table_square,
    norm_first,
    first_mean,
    first_square,
    norm_second,
    second_mean,
    second_square,
    colour_conv,
    colour_mean,
    colour_square,
):
    groups = lax.axis_size("half") * lax.axis_size("dp")
    ranks = lax.axis_size("row")
    row = lax.axis_index("row").astype(jnp.int32).reshape(1)
    n, h, w, c_in = features.shape
    c_out = conv_first.shape[1]
    count_low = float(n // MICRO * h * w * groups)
    count_high = 4.0 * count_low

    inputs = jnp.transpose(features, (1, 2, 0, 3))
    raw = inputs.astype(f32)
    sums_low = jnp.concatenate(
        [per_micro(jnp.sum(raw, axis=(0, 1))), per_micro(jnp.sum(raw * raw, axis=(0, 1)))], axis=0
    )
    totals_low = group_sum(sums_low)
    weight_one = group_gather(conv_first.astype(bf16)).reshape(9, ranks * c_in, c_out)

    onehot = (labels[:, None] == jnp.arange(NCLS)[None, :]).astype(f32)
    conds = jnp.concatenate([jnp.dot(onehot, class_table, precision=highest), noise], axis=1)
    class_disc = jnp.dot(onehot, disc_table, precision=highest)
    mods_one = jnp.einsum("bk,kgc->bgc", conds, norm_first, precision=highest)
    mods_two = jnp.einsum("bk,kgc->bgc", conds, norm_second, precision=highest)

    centre_one, spread_one = moments_of(totals_low, count_low)
    centre_one, spread_one = per_image(centre_one, n), per_image(spread_one, n)
    gain_one, gain_two = 1.0 + mods_one[:, 0], 1.0 + mods_two[:, 0]
    normed_one = (raw - centre_one) * spread_one
    pre_one = normed_one * gain_one + mods_one[:, 1]
    acted_one = flat(jax.nn.silu(pre_one).astype(bf16))
    ones = row_gather(acted_one)
    raws = row_gather(flat(inputs))

    hidden, sums_high = conv_one(row, [one[None] for one in ones], weight_one, (h, w, n))
    held_second, held_skip, _ = lax.optimization_barrier(
        (conv_second.astype(bf16), conv_skip.astype(bf16), weight_one[0, 0, 0])
    )
    weight_skip = group_gather(held_skip)
    weight_two = group_gather(held_second).reshape(9, ranks * c_out, c_out)
    totals_high = group_sum(sums_high)
    centre_two, spread_two = moments_of(totals_high, count_high)
    centre_two, spread_two = per_image(centre_two, n), per_image(spread_two, n)
    normed_two = (hidden - centre_two) * spread_two
    pre_two = normed_two * gain_two + mods_two[:, 1]
    acted_two = jax.nn.silu(pre_two).astype(bf16)
    twos = row_gather(acted_two)

    colour = jnp.pad(
        jnp.transpose(colour_conv, (0, 2, 1)).astype(bf16), ((0, 0), (0, PAD - 3), (0, 0))
    )
    summed, active, picture = conv_two(row, twos, [one[None] for one in raws], weight_two, weight_skip, colour)
    picture = row_sum(picture)

    first_taps = jnp.pad(disc_first.reshape(9, 3, -1), ((0, 0), (0, PAD - 3), (0, 0)))
    second_taps = disc_second.reshape(9, -1, disc_second.shape[-1])
    skip_taps = jnp.pad(disc_skip, ((0, PAD - 3), (0, 0)))
    mark = counted.astype(f32)[:, None]
    grads, loss_part = critic(
        picture,
        first_taps,
        second_taps,
        skip_taps,
        disc_head[None, :] + class_disc,
        mark,
        (2 * h, 2 * w, n),
    )
    colour_rows = jnp.pad(colour.reshape(9 * PAD, c_out), ((0, 128 - 9 * PAD), (0, 0)))
    backs = back_two(row, grads, summed, active, colour_rows, weight_two, ranks)
    gpad, grad_colour, pieces = backs[0], backs[1], backs[2:]
    grad_two, grad_skip = weight_two_grads(row, gpad, twos, raws)
    grad_acted_two = row_scatter(list(pieces)).reshape(hidden.shape)

    grad_pre_two = grad_acted_two * silu_slope(pre_two)
    gains_two = jnp.sum(grad_pre_two * normed_two, axis=(0, 1))
    shifts_two = jnp.sum(grad_pre_two, axis=(0, 1))
    back_sums = group_sum(
        jnp.concatenate([per_micro(gain_two * shifts_two), per_micro(gain_two * gains_two)], axis=0)
    )
    mean_g = per_image(back_sums[:MICRO] / count_high, n)
    mean_gy = per_image(back_sums[MICRO:] / count_high, n)
    grad_hidden = (spread_two * (grad_pre_two * gain_two - mean_g - normed_two * mean_gy)).astype(
        bf16
    )
    ones_turned = [jnp.transpose(one) for one in ones]
    backs = back_one(row, grad_hidden, weight_one, ones_turned)
    grad_one, pieces = flat(backs[0]), backs[1:]
    grad_acted_one = row_scatter(list(pieces)).reshape(raw.shape)
    grad_pre_one = grad_acted_one * silu_slope(pre_one)
    gains_one = jnp.sum(grad_pre_one * normed_one, axis=(0, 1))
    shifts_one = jnp.sum(grad_pre_one, axis=(0, 1))
    grad_mods_one = jnp.stack([gains_one, shifts_one], axis=1)
    grad_mods_two = jnp.stack([gains_two, shifts_two], axis=1)

    grad_cond = jnp.einsum("bgc,kgc->bk", grad_mods_one, norm_first[:EMB], precision=highest)
    grad_cond = grad_cond + jnp.einsum(
        "bgc,kgc->bk", grad_mods_two, norm_second[:EMB], precision=highest
    )
    grad_cond = row_sum(grad_cond)

    count_part = jnp.sum(counted).astype(f32)
    small = jnp.concatenate(
        [
            grad_colour[: 9 * PAD],
            jnp.broadcast_to(loss_part[:1, :1], (1, c_out)),
            jnp.broadcast_to(count_part, (1, c_out)),
        ],
        axis=0,
    )
    small = group_sum(small)
    loss_sum, fake_count = small[9 * PAD, 0], small[9 * PAD + 1, 0]
    inverse = 1.0 / fake_count
    g_colour = jnp.transpose(small[: 9 * PAD].reshape(9, PAD, c_out)[:, :3], (0, 2, 1))

    known = group_pile(jnp.concatenate([conds, labels.astype(f32)[:, None]], axis=1))
    found = group_pile(
        jnp.concatenate(
            [grad_mods_one.reshape(n, -1), grad_mods_two.reshape(n, -1), grad_cond], axis=1
        )
    )
    conds_all, labels_all = known[:, :-1], known[:, -1].astype(jnp.int32)
    onehot_all = (labels_all[:, None] == jnp.arange(NCLS)[None, :]).astype(f32)
    cut_one, cut_two = 2 * c_in, 2 * c_in + 2 * c_out
    g_norm = lax.dot_general(
        conds_all,
        found[:, :cut_two],
        (((0,), (0,)), ((), ())),
        precision=highest,
        preferred_element_type=f32,
    )
    g_norm_one = g_norm[:, :cut_one].reshape(norm_first.shape)
    g_norm_two = g_norm[:, cut_one:].reshape(norm_second.shape)
    g_table = lax.dot_general(
        onehot_all,
        found[:, cut_two:],
        (((0,), (0,)), ((), ())),
        precision=highest,
        preferred_element_type=f32,
    )

    shares = [group_scatter(flat(g)) for g in (grad_one, grad_two, grad_skip)]
    muons = [
        muon(master, moment, share * inverse, groups)
        for master, moment, share in zip(
            (conv_first, conv_second, conv_skip),
            (momentum_first, momentum_second, momentum_skip),
            shares,
        )
    ]
    table_new = adam_update(class_table, g_table * inverse, table_mean, table_square, ADAM_RATE)
    first_new = adam_update(norm_first, g_norm_one * inverse, first_mean, first_square, ADAM_RATE)
    second_new = adam_update(
        norm_second, g_norm_two * inverse, second_mean, second_square, ADAM_RATE
    )
    colour_new = adam_update(
        colour_conv, g_colour * inverse, colour_mean, colour_square, COLOUR_RATE
    )
    return (
        (loss_sum, fake_count)
        + tuple(m[0] for m in muons)
        + tuple(m[1] for m in muons)
        + table_new
        + first_new
        + second_new
        + colour_new
    )


def near_device(
    features,
    noise,
    labels,
    counted,
    disc_first,
    disc_second,
    disc_skip,
    disc_head,
    disc_table,
    conv_first,
    conv_second,
    conv_skip,
    momentum_first,
    momentum_second,
    momentum_skip,
    class_table,
    table_mean,
    table_square,
    norm_first,
    first_mean,
    first_square,
    norm_second,
    second_mean,
    second_square,
    colour_conv,
    colour_mean,
    colour_square,
):
    groups = lax.axis_size("half") * lax.axis_size("dp")
    ranks = lax.axis_size("row")
    row = lax.axis_index("row").astype(jnp.int32).reshape(1)
    n, h, w, c_in = features.shape
    c_out = conv_first.shape[1]
    count_low = float(n // MICRO * h * w * groups)
    count_high = 4.0 * count_low

    where = jnp.stack(
        [lax.axis_index("row"), lax.axis_index("half"), lax.axis_index("dp")]
    ).astype(jnp.int32)
    n_dp, half, spot = lax.axis_size("dp"), lax.axis_index("half"), lax.axis_index("dp")
    turned = conv_first.T.astype(bf16)
    below, above = [turned, step_below(turned, 1)], [turned, step_above(turned, 1)]
    inputs = jnp.transpose(features, (1, 2, 0, 3))
    raw = inputs.astype(f32)
    sums_low = jnp.concatenate(
        [
            per_micro(jnp.sum(raw, axis=(0, 1))),
            per_micro(jnp.sum(raw * raw, axis=(0, 1))),
            jnp.broadcast_to(jnp.sum(counted).astype(f32), (1, c_in)),
        ],
        axis=0,
    )
    totals_low = near_sum(sums_low)
    below.append(step_below(below[1], 2))
    above.append(step_above(above[1], 2))
    fake_count = totals_low[2 * MICRO, 0]
    inverse = 1.0 / fake_count

    onehot = (labels[:, None] == jnp.arange(NCLS)[None, :]).astype(f32)
    conds = jnp.concatenate([jnp.dot(onehot, class_table, precision=highest), noise], axis=1)
    class_disc = jnp.dot(onehot, disc_table, precision=highest)
    mods_one = jnp.einsum("bk,kgc->bgc", conds, norm_first, precision=highest)
    mods_two = jnp.einsum("bk,kgc->bgc", conds, norm_second, precision=highest)

    centre_one, spread_one = moments_of(totals_low[: 2 * MICRO], count_low)
    centre_one, spread_one = per_image(centre_one, n), per_image(spread_one, n)
    gain_one, gain_two = 1.0 + mods_one[:, 0], 1.0 + mods_two[:, 0]
    normed_one = (raw - centre_one) * spread_one
    pre_one = normed_one * gain_one + mods_one[:, 1]
    acted_one = flat(jax.nn.silu(pre_one).astype(bf16))
    pairs = row_gather(jnp.stack([acted_one, flat(inputs)], axis=0))
    sizes = (conv_first.shape[0],)
    down, up = lax.rem(spot + 3, 4), lax.rem(spot + 1, 4)
    held = place_cores(None, [spot, down, up], jnp.stack([turned, below[1], above[1]]), sizes)
    below.append(step_below(after(below[2], *pairs), 3))
    above.append(step_above(after(above[2], *pairs), 3))
    middle = jnp.where(spot >= 2, below[2], above[2])
    held = place_cores(held, [lax.rem(spot + 2, 4)], middle[None], sizes)
    below[3], above[3] = after(below[3], *held), after(above[3], *held)
    last = jnp.where(spot == 3, below[3], jnp.where(spot == 0, above[3], turned))
    end = jnp.where(spot == 3, 0, jnp.where(spot == 0, 3, spot))
    (weight_one,) = place_cores(held, [end], last[None], sizes)
    weight_one = weight_one.reshape(9, ranks * c_in, c_out)

    hidden, sums_high = conv_one(row, pairs, weight_one, (h, w, n))
    totals_high = near_sum(sums_high)
    other = jnp.concatenate([conv_second.T, conv_skip.T], axis=1).astype(bf16)
    other = jnp.pad(other, ((0, 0), (0, -other.shape[1] % 128)))
    others = lax.all_gather(after(other, below[3], above[3]), GROUP, axis=0)
    weight_two, weight_skip = place(
        None,
        list(range(groups)),
        others[: groups // 2],
        others[groups // 2 :],
        (conv_second.shape[0], conv_skip.shape[0]),
    )
    weight_two = weight_two.reshape(9, ranks * c_out, c_out)
    centre_two, spread_two = moments_of(totals_high, count_high)
    centre_two, spread_two = per_image(centre_two, n), per_image(spread_two, n)
    normed_two = (hidden - centre_two) * spread_two
    pre_two = normed_two * gain_two + mods_two[:, 1]
    acted_two = jax.nn.silu(pre_two).astype(bf16)
    twos = row_gather(acted_two)
    colour = jnp.pad(
        jnp.transpose(colour_conv, (0, 2, 1)).astype(bf16), ((0, 0), (0, PAD - 3), (0, 0))
    )
    summed, active, picture = conv_two(row, twos, pairs, weight_two, weight_skip, colour)
    kept_pairs = [after(pair, active) for pair in pairs]
    turned = jnp.concatenate([jnp.transpose(pair[0]) for pair in kept_pairs], axis=0)
    ones_all = lax.all_gather(after(turned, others), GROUP, axis=0)

    picture = row_sum(picture)

    first_taps = jnp.pad(disc_first.reshape(9, 3, -1), ((0, 0), (0, PAD - 3), (0, 0)))
    second_taps = disc_second.reshape(9, -1, disc_second.shape[-1])
    skip_taps = jnp.pad(disc_skip, ((0, PAD - 3), (0, 0)))
    mark = counted.astype(f32)[:, None]
    grads, loss_part = critic(
        picture,
        first_taps,
        second_taps,
        skip_taps,
        disc_head[None, :] + class_disc,
        mark,
        (2 * h, 2 * w, n),
    )
    colour_rows = jnp.pad(colour.reshape(9 * PAD, c_out), ((0, 128 - 9 * PAD), (0, 0)))
    backs = back_two(row, grads, summed, active, colour_rows, weight_two, ranks)
    gpad, grad_colour = backs[0], backs[1]
    pieces = row_exchange(list(backs[2:]))
    packed = weight_pack(
        row,
        gpad,
        [jnp.transpose(flat(after(two, gpad))) for two in twos],
        [jnp.transpose(after(pair, gpad)[1]) for pair in pairs],
        groups,
    )
    kept = near_halves(packed.reshape((2, groups // 2) + packed.shape[1:]))
    pieces[-1] = after(pieces[-1], packed)
    grad_acted_two = sum(piece.astype(f32) for piece in pieces).reshape(hidden.shape)

    grad_pre_two = grad_acted_two * silu_slope(pre_two)
    gains_two = jnp.sum(grad_pre_two * normed_two, axis=(0, 1))
    shifts_two = jnp.sum(grad_pre_two, axis=(0, 1))
    back_sums = jnp.concatenate(
        [per_micro(gain_two * shifts_two), per_micro(gain_two * gains_two)], axis=0
    )
    back_sums = near_sum(back_sums)
    mean_g = per_image(back_sums[:MICRO] / count_high, n)
    mean_gy = per_image(back_sums[MICRO:] / count_high, n)
    grad_hidden = (spread_two * (grad_pre_two * gain_two - mean_g - normed_two * mean_gy)).astype(
        bf16
    )
    hidden_all = straight(grad_hidden)
    scaled = inverse.reshape(1, 1)
    hidden_all = straight(grad_hidden)
    *hidden_all, kept, wire = together(*hidden_all, kept, kept.astype(bf16))
    hidden_all = both_cores(hidden_all)
    moment_one, low_one = weight_one_moment(
        where, scaled, hidden_all, ones_all, momentum_first.T
    )
    kept, wire, grad_hidden, _ = together(kept, wire, grad_hidden, low_one)
    one_held = row_gather(low_one)
    shares = near_blocks(kept, wire)
    backs = back_in(row, grad_hidden, weight_one, ranks)
    *one_held, shares[1], shares[2], shares[3], backs = together(
        *one_held, *shares[1:], jnp.stack(backs, axis=0)
    )
    panel = gram_rows(row, one_held, [(0, conv_first.shape[0])])
    kept_one = near_halves(panel.reshape(2, 4, 1, c_out // 8, -1))
    moment_two, moment_skip, low_two = moments_two(
        scaled, [after(shares[0], panel)] + shares[1:], momentum_second.T, momentum_skip.T
    )
    kept_one = after(kept_one, low_two)
    two_held = spread(low_two, ("row",))
    total_one = gram_total(near_blocks(kept_one, kept_one))
    grams_one = row_gather(total_one)
    two_held = after(two_held, *grams_one[1:])
    two_held = [
        lax.dynamic_index_in_dim(two_held, lax.bitwise_xor(row[0], k), 0, keepdims=False)
        for k in range(ranks)
    ]
    spans = [(0, conv_second.shape[0]), (conv_second.shape[0], low_two.shape[1])]
    panels = gram_rows(row, two_held, spans)
    kept_two = near_halves(panels.reshape(2, 4, 1, c_out // 4, -1))
    backs = after(backs, *grams_one[1:])
    inward = lax.all_to_all(in_order(list(backs[:, None]), "row"), "row", 0, 0)
    grams_one = both_cores(grams_one)
    kept_two = after(kept_two, *grams_one)
    terms_two = near_blocks(kept_two, kept_two)
    terms_two[0] = after(terms_two[0], inward)
    total_two = placed_in_order(straight(sum(terms_two)))
    *grams_one, total_two = together(*grams_one, total_two)
    maps_one = newton(where, grams_one, ranks)
    factor = 0.2 * math.sqrt(max(conv_first.shape[0] * groups, c_out * ranks))
    grad_acted_one = jnp.sum(inward.astype(f32), axis=0).reshape(raw.shape)
    grad_pre_one = grad_acted_one * silu_slope(pre_one)
    gains_one = jnp.sum(grad_pre_one * normed_one, axis=(0, 1))
    shifts_one = jnp.sum(grad_pre_one, axis=(0, 1))
    grad_mods_one = jnp.stack([gains_one, shifts_one], axis=1)
    grad_mods_two = jnp.stack([gains_two, shifts_two], axis=1)

    grad_cond = jnp.einsum("bgc,kgc->bk", grad_mods_one, norm_first[:EMB], precision=highest)
    grad_cond = grad_cond + jnp.einsum(
        "bgc,kgc->bk", grad_mods_two, norm_second[:EMB], precision=highest
    )

    small = jnp.concatenate(
        [
            grad_colour[: 9 * PAD],
            jnp.broadcast_to(loss_part[:1, :1], (1, c_out)),
        ],
        axis=0,
    )

    grad_cond = jnp.sum(spread(grad_cond, ("row",)), axis=0)
    found = jnp.concatenate(
        [
            grad_mods_one.reshape(n, -1),
            grad_mods_two.reshape(n, -1),
            grad_cond,
            conds,
            labels.astype(f32)[:, None],
        ],
        axis=1,
    )
    found = jnp.pad(found, ((0, 0), (0, -found.shape[1] % 128)))
    wide = found.shape[1]
    extra = small.reshape(-1)
    extra = jnp.pad(extra, (0, -extra.shape[0] % (8 * wide))).reshape(-1, wide)
    packet = jnp.concatenate([found, extra], axis=0)
    packet = spread(after(packet, total_two), GROUP)
    found = packet[:, :n].reshape(-1, wide)
    small = jnp.sum(packet[:, n:], axis=0).reshape(-1)[: small.size].reshape(small.shape)
    loss_sum = small[9 * PAD, 0]
    g_colour = jnp.transpose(small[: 9 * PAD].reshape(9, PAD, c_out)[:, :3], (0, 2, 1))
    cut = 2 * c_in + 2 * c_out + EMB
    found, known = found[:, :cut], found[:, cut : cut + conds.shape[1] + 1]
    conds_all, labels_all = known[:, :-1], known[:, -1].astype(jnp.int32)
    onehot_all = (labels_all[:, None] == jnp.arange(NCLS)[None, :]).astype(f32)
    cut_one, cut_two = 2 * c_in, 2 * c_in + 2 * c_out
    g_norm = lax.dot_general(
        conds_all,
        found[:, :cut_two],
        (((0,), (0,)), ((), ())),
        precision=highest,
        preferred_element_type=f32,
    )
    g_norm_one = g_norm[:, :cut_one].reshape(norm_first.shape)
    g_norm_two = g_norm[:, cut_one:].reshape(norm_second.shape)
    g_table = lax.dot_general(
        onehot_all,
        found[:, cut_two:],
        (((0,), (0,)), ((), ())),
        precision=highest,
        preferred_element_type=f32,
    )

    table_new = adam_update(class_table, g_table * inverse, table_mean, table_square, ADAM_RATE)
    first_new = adam_update(norm_first, g_norm_one * inverse, first_mean, first_square, ADAM_RATE)
    second_new = adam_update(
        norm_second, g_norm_two * inverse, second_mean, second_square, ADAM_RATE
    )
    colour_new = adam_update(
        colour_conv, g_colour * inverse, colour_mean, colour_square, COLOUR_RATE
    )
    grams_two = row_gather(total_two)
    (first_out,) = update(
        row, maps_one, one_held, [conv_first.T], [(0, conv_first.shape[0])], [factor]
    )
    grams_two[0] = after(grams_two[0], first_out)
    maps_two = newton(where, grams_two, ranks)
    other_map = axis_swap(maps_two, "half", 1)
    maps_two = jnp.where(
        half == 0,
        jnp.concatenate([maps_two, other_map], axis=0),
        jnp.concatenate([other_map, maps_two], axis=0),
    )
    factors = [
        0.2 * math.sqrt(max(rows * groups, c_out * ranks))
        for rows in (conv_second.shape[0], conv_skip.shape[0])
    ]
    second_out, skip_out = update(
        row, maps_two, two_held, [conv_second.T, conv_skip.T], spans, factors
    )
    weights_new = (first_out.T, second_out.T, skip_out.T)
    moments_new = (moment_one.T, moment_two.T, moment_skip.T)
    return (
        (loss_sum, fake_count)
        + weights_new
        + moments_new
        + table_new
        + first_new
        + second_new
        + colour_new
    )


def weight_two_grads(row, gpad, twos, raws):
    turned = [jnp.transpose(flat(two)) for two in twos]
    return weight_two(row, gpad, turned, [jnp.transpose(one) for one in raws])


def solution(mesh):
    group = ("half", "dp")
    placed = (
        (P(group, None, None, "row"), P(group, None), P(group), P(group))
        + (P(),) * 5
        + (P(group, "row"),) * 6
        + (P(),) * 3
        + (P(None, None, "row"),) * 6
        + (P(None, "row", None),) * 3
    )
    near = mesh.shape["dp"] == 4 and mesh.shape["half"] == 2 and mesh.shape["row"] == 4
    return jax.shard_map(
        near_device if near else wide_device,
        mesh=mesh,
        in_specs=placed,
        out_specs=(P(), P())
        + (P(group, "row"),) * 6
        + (P(),) * 3
        + (P(None, None, "row"),) * 6
        + (P(None, "row", None),) * 3,
        check_vma=False,
    )
```

```python
import functools
import math

import jax
import jax.numpy as jnp
from jax import lax
from jax.experimental import pallas as pl
from jax.experimental.pallas import tpu as pltpu
from jax.sharding import PartitionSpec as P

EMB = 128
NCLS = 1000
MICRO = 2
NS_ITERS = 5
STEP = 10

highest = lax.Precision.HIGHEST
high = lax.Precision.HIGH
bf16 = jnp.bfloat16
f32 = jnp.float32
BN_EPS = 1e-05
NEWTON_EPSILON = 1e-07
NS_COEF = (3.4445, -4.775, 2.0315)
MOMENTUM = 0.9
MUON_RATE = 0.03
DECAY = 0.01
BETA_ONE = 0.9
BETA_TWO = 0.95
ADAM_EPS = 1e-08
ADAM_RATE = 0.05
COLOUR_RATE = 0.01
PAD = 8
MIB = 1024 * 1024


def kernel_params(size=20):
    return pltpu.CompilerParams(vmem_limit_bytes=size * MIB)


def whole(shape):
    return pl.BlockSpec(shape, lambda t, r: (0,) * len(shape))


def silu_slope(values):
    sigmoid_value = jax.nn.sigmoid(values)
    return sigmoid_value * (1.0 + values * (1.0 - sigmoid_value))


def contract_last(left, right):
    return lax.dot_general(left, right, (((1,), (1,)), ((), ())), preferred_element_type=f32)


def times(left, right):
    return jnp.dot(left, right, preferred_element_type=f32)


def axis_swap(value, axis, k):
    n = lax.axis_size(axis)
    return lax.ppermute(value, axis, [(i, i ^ k) for i in range(n)])


def axis_shift(value, axis, k):
    n = lax.axis_size(axis)
    return lax.ppermute(value, axis, [(i, (i + k) % n) for i in range(n)])


def row_gather(value):
    return [value] + [axis_swap(value, "row", k) for k in range(1, lax.axis_size("row"))]


def row_sum(value):
    return sum(row_gather(value))


def row_exchange(pieces):
    return [pieces[0]] + [axis_swap(pieces[k], "row", k) for k in range(1, len(pieces))]


def row_scatter(pieces):
    return sum(piece.astype(f32) for piece in row_exchange(pieces))


GROUP = ("half", "dp")


def group_sum(value):
    return lax.psum(value, GROUP)


def group_pile(value):
    return lax.all_gather(value, GROUP, axis=0, tiled=True)


def group_gather(value):
    return lax.all_gather(value, GROUP, axis=0, tiled=True)


def group_scatter(value):
    return lax.psum_scatter(value, GROUP, scatter_dimension=0, tiled=True).astype(f32)


def spread(value, axis):
    n = math.prod(lax.axis_size(name) for name in axis)
    return lax.all_to_all(jnp.broadcast_to(value[None], (n,) + value.shape), axis, 0, 0)


def near_sum(value):
    return jnp.sum(spread(value, GROUP), axis=0)


def together(*values):
    return lax.optimization_barrier(values)


def after(value, *others):
    return lax.optimization_barrier((value,) + others)[0]


def step_below(value, s):
    n = lax.axis_size("dp")
    return lax.ppermute(value, "dp", [(i, i + 1) for i in range(s - 1, n - 1)])


def step_above(value, s):
    n = lax.axis_size("dp")
    return lax.ppermute(value, "dp", [(i, i - 1) for i in range(1, n - s + 1)])


def straight(value):
    return [value] + [axis_shift(value, "dp", k) for k in range(1, lax.axis_size("dp"))]


def both_cores(pieces):
    return pieces + [axis_swap(piece, "half", 1) for piece in pieces]


def placed_in_order(pieces):
    n = len(pieces)
    turned = [pieces[0]] + pieces[:0:-1]
    piled = jnp.stack(turned + turned[:-1], axis=0)
    start = lax.rem(n - lax.axis_index("dp"), n)
    return lax.dynamic_slice_in_dim(piled, start, n, 0)


def near_halves(value):
    h = lax.axis_index("half")
    kept = lax.dynamic_index_in_dim(value, h, 0, keepdims=False)
    sent = lax.dynamic_index_in_dim(value, 1 - h, 0, keepdims=False)
    return kept.astype(f32) + axis_swap(sent, "half", 1).astype(f32)


def near_blocks(kept, wire):
    n = lax.axis_size("dp")
    z = lax.axis_index("dp")
    pieces = [lax.dynamic_index_in_dim(kept, z, 0, keepdims=False)]
    for k in range(1, n):
        block = lax.dynamic_index_in_dim(wire, lax.rem(z + k, n), 0, keepdims=False)
        pieces.append(axis_shift(block, "dp", k))
    return pieces


def raise_two(values):
    h, w, n, c = values.shape
    wide = jnp.stack([values, values], axis=2).reshape(h, 2 * w, n, c)
    return jnp.stack([wide, wide], axis=1).reshape(2 * h, 2 * w, n, c)


def sum_two(values):
    h, w, n, c = values.shape
    shaped = values.reshape(h // 2, 2, w // 2, 2, n, c)
    return (shaped[:, 0, :, 0] + shaped[:, 0, :, 1]) + (shaped[:, 1, :, 0] + shaped[:, 1, :, 1])


def owned_rows(row_ref, k, size):
    return pl.ds(pl.multiple_of(lax.bitwise_xor(row_ref[0], k) * size, size), size)


def flat(values):
    return values.reshape(-1, values.shape[-1])


def conv_one_kernel(row_ref, *refs):
    blocks, (w_ref, out_ref, sums_ref, acc_ref) = refs[:-4], refs[-4:]
    h2, w2, n, c = out_ref.shape
    t = pl.program_id(0)
    dy, dx = lax.div(t, 3), lax.rem(t, 3)

    @pl.when(t == 0)
    def _():
        acc_ref[...] = jnp.zeros_like(acc_ref)

    product = sum(
        times(x_ref[0], w_ref[0, owned_rows(row_ref, k, x_ref.shape[2]), :])
        for k, x_ref in enumerate(blocks)
    )
    raised = raise_two(product.reshape(h2 // 2, w2 // 2, n, c))
    acc_ref[pl.ds(2 - dy, h2), pl.ds(2 - dx, w2)] += raised

    @pl.when(t == 8)
    def _():
        hidden = acc_ref[1 : h2 + 1, 1 : w2 + 1]
        out_ref[...] = hidden
        shaped = hidden.reshape(h2 * w2, n, c)
        first, second = jnp.sum(shaped, axis=0), jnp.sum(shaped * shaped, axis=0)
        m = n // MICRO
        for i in range(MICRO):
            sums_ref[i : i + 1, :] = jnp.sum(first[i * m : (i + 1) * m], axis=0, keepdims=True)
            sums_ref[MICRO + i : MICRO + i + 1, :] = jnp.sum(
                second[i * m : (i + 1) * m], axis=0, keepdims=True
            )


def conv_one(row, blocks, weight, pixels):
    h, w, n = pixels
    c = weight.shape[-1]
    return pl.pallas_call(
        conv_one_kernel,
        out_shape=(
            jax.ShapeDtypeStruct((2 * h, 2 * w, n, c), f32),
            jax.ShapeDtypeStruct((2 * MICRO, c), f32),
        ),
        grid_spec=pltpu.PrefetchScalarGridSpec(
            num_scalar_prefetch=1,
            grid=(9,),
            in_specs=[whole(b.shape) for b in blocks]
            + [pl.BlockSpec((1,) + weight.shape[1:], lambda t, r: (t, 0, 0))],
            out_specs=(whole((2 * h, 2 * w, n, c)), whole((2 * MICRO, c))),
            scratch_shapes=[pltpu.VMEM((2 * h + 2, 2 * w + 2, n, c), f32)],
        ),
        compiler_params=kernel_params(),
        name="conv_one",
    )(row, *blocks, weight)


def conv_two_kernel(count, row_ref, *refs):
    blocks, raws = refs[:count], refs[count : 2 * count]
    w_ref, skip_ref, colour_ref, sum_ref, act_ref, pic_ref, pad_ref, apad_ref = refs[2 * count :]
    h2, w2, n, c = sum_ref.shape
    t = pl.program_id(0)
    dy, dx = lax.div(t, 3), lax.rem(t, 3)

    @pl.when(t == 0)
    def _():
        pad_ref[...] = jnp.zeros_like(pad_ref)
        for k in range(count):
            pad_ref[k, 1 : h2 + 1, 1 : w2 + 1] = blocks[k][...]
        skipped = sum(
            times(x_ref[x_ref.shape[0] - 1], skip_ref[owned_rows(row_ref, k, x_ref.shape[2]), :])
            for k, x_ref in enumerate(raws)
        )
        sum_ref[...] = raise_two(skipped.reshape(h2 // 2, w2 // 2, n, c))

    product = sum(
        times(
            flat(pad_ref[k, pl.ds(dy, h2), pl.ds(dx, w2)]), w_ref[0, owned_rows(row_ref, k, c), :]
        )
        for k in range(count)
    )
    sum_ref[...] += product.reshape(sum_ref.shape)

    @pl.when(t == 8)
    def _():
        active = jax.nn.silu(sum_ref[...]).astype(bf16)
        act_ref[...] = active
        apad_ref[...] = jnp.zeros_like(apad_ref)
        apad_ref[1 : h2 + 1, 1 : w2 + 1] = active
        picture = jnp.zeros(pic_ref.shape, f32)
        for tap in range(9):
            y, x = divmod(tap, 3)
            picture = picture + contract_last(
                colour_ref[tap], flat(apad_ref[y : y + h2, x : x + w2])
            )
        pic_ref[...] = picture


def conv_two(row, blocks, raws, weight, skip, colour):
    h2, w2, n, c = blocks[0].shape
    return pl.pallas_call(
        functools.partial(conv_two_kernel, len(blocks)),
        out_shape=(
            jax.ShapeDtypeStruct((h2, w2, n, c), f32),
            jax.ShapeDtypeStruct((h2, w2, n, c), bf16),
            jax.ShapeDtypeStruct((PAD, h2 * w2 * n), f32),
        ),
        grid_spec=pltpu.PrefetchScalarGridSpec(
            num_scalar_prefetch=1,
            grid=(9,),
            in_specs=[whole(b.shape) for b in blocks + raws]
            + [
                pl.BlockSpec((1,) + weight.shape[1:], lambda t, r: (t, 0, 0)),
                whole(skip.shape),
                whole(colour.shape),
            ],
            out_specs=(whole((h2, w2, n, c)), whole((h2, w2, n, c)), whole((PAD, h2 * w2 * n))),
            scratch_shapes=[
                pltpu.VMEM((len(blocks), h2 + 2, w2 + 2, n, c), bf16),
                pltpu.VMEM((h2 + 2, w2 + 2, n, c), bf16),
            ],
        ),
        compiler_params=kernel_params(28),
        name="conv_two",
    )(row, *blocks, *raws, weight, skip, colour)


def critic_kernel(
    dims, pic_ref, first_ref, second_ref, skip_ref, head_ref, count_ref, out_ref, loss_ref, small_ref, pad_ref
):
    h2, w2, n = dims
    h, w = h2 // 2, w2 // 2
    c = second_ref.shape[-1]
    taps = [divmod(tap, 3) for tap in range(9)]
    shade = jnp.tanh(jnp.transpose(pic_ref[...]))
    picture = shade.astype(bf16).reshape(h2, w2, n, PAD)
    small_ref[...] = jnp.zeros_like(small_ref)
    small_ref[1 : h2 + 1, 1 : w2 + 1] = picture
    pad_ref[...] = jnp.zeros_like(pad_ref)
    front_pre = sum(
        times(flat(small_ref[y : y + h2, x : x + w2]), first_ref[3 * y + x]) for y, x in taps
    )
    pad_ref[1 : h2 + 1, 1 : w2 + 1] = jax.nn.silu(front_pre).astype(bf16).reshape(h2, w2, n, c)
    merged = sum(times(flat(pad_ref[y : y + h2, x : x + w2]), second_ref[3 * y + x]) for y, x in taps)
    merged = 0.25 * flat(sum_two(merged.reshape(h2, w2, n, c)))
    small = 0.25 * flat(sum_two(picture.astype(f32)))
    skip = skip_ref[...].astype(f32)
    for i in range(3):
        merged = merged + small[:, i : i + 1] * skip[i : i + 1, :]
    feature = jnp.sum(jax.nn.silu(merged).reshape(h * w, n, c), axis=0)
    weights = head_ref[...] * count_ref[...]
    loss_ref[...] = jnp.broadcast_to(-jnp.sum(feature * weights, keepdims=True), loss_ref.shape)
    grad_merged = (silu_slope(merged).reshape(h * w, n, c) * -weights[None]).astype(bf16)
    grad_merged = grad_merged.reshape(h, w, n, c)
    grad_pool = raise_two(grad_merged) * jnp.bfloat16(0.25)
    pad_ref[1 : h2 + 1, 1 : w2 + 1] = grad_pool
    grad_front = sum(
        contract_last(flat(pad_ref[2 - y : 2 - y + h2, 2 - x : 2 - x + w2]), second_ref[3 * y + x])
        for y, x in taps
    )
    grad_front_pre = (grad_front * silu_slope(front_pre)).astype(bf16)
    pad_ref[1 : h2 + 1, 1 : w2 + 1] = grad_front_pre.reshape(h2, w2, n, c)
    grad_picture = sum(
        contract_last(flat(pad_ref[2 - y : 2 - y + h2, 2 - x : 2 - x + w2]), first_ref[3 * y + x])
        for y, x in taps
    )
    grad_skip = contract_last(flat(grad_merged), skip_ref[...]).reshape(h, w, n, PAD)
    grad_picture = grad_picture + 0.25 * flat(raise_two(grad_skip))
    grad_pre = (grad_picture * (1.0 - shade * shade)).astype(bf16)
    small_ref[1 : h2 + 1, 1 : w2 + 1] = grad_pre.reshape(h2, w2, n, PAD)
    out_ref[...] = jnp.concatenate(
        [flat(small_ref[2 - y : 2 - y + h2, 2 - x : 2 - x + w2]) for y, x in taps]
        + [jnp.zeros((h2 * w2 * n, 128 - 9 * PAD), bf16)],
        axis=1,
    )


def critic(picture, disc_first, disc_second, disc_skip, head, counted, dims):
    h2, w2, n = dims
    c = disc_second.shape[-1]
    return pl.pallas_call(
        functools.partial(critic_kernel, dims),
        out_shape=(
            jax.ShapeDtypeStruct((h2 * w2 * n, 128), bf16),
            jax.ShapeDtypeStruct((8, 128), f32),
        ),
        scratch_shapes=[
            pltpu.VMEM((h2 + 2, w2 + 2, n, PAD), bf16),
            pltpu.VMEM((h2 + 2, w2 + 2, n, c), bf16),
        ],
        compiler_params=kernel_params(28),
        name="critic",
    )(picture, disc_first, disc_second, disc_skip, head, counted)


def back_two_kernel(count, row_ref, g_ref, sum_ref, act_ref, colour_ref, w_ref, *refs):
    gpad_ref, gcol_ref = refs[0], refs[1]
    outs, acc_ref = refs[2:-1], refs[-1]
    h2, w2, n, c = sum_ref.shape
    t = pl.program_id(0)
    dy, dx = lax.div(t, 3), lax.rem(t, 3)

    @pl.when(t == 0)
    def _():
        grad_active = times(g_ref[...], colour_ref[...]).reshape(h2, w2, n, c)
        gpad_ref[...] = jnp.zeros_like(gpad_ref)
        gpad_ref[1 : h2 + 1, 1 : w2 + 1] = (grad_active * silu_slope(sum_ref[...])).astype(bf16)
        gcol_ref[...] = lax.dot_general(
            g_ref[...], flat(act_ref[...]), (((0,), (0,)), ((), ())), preferred_element_type=f32
        )
        acc_ref[...] = jnp.zeros_like(acc_ref)

    shifted = flat(gpad_ref[pl.ds(2 - dy, h2), pl.ds(2 - dx, w2)])
    for k in range(count):
        acc_ref[k] += contract_last(shifted, w_ref[0, owned_rows(row_ref, k, c), :])

    @pl.when(t == 8)
    def _():
        for k in range(count):
            outs[k][...] = acc_ref[k].astype(bf16)


def back_two(row, grads, summed, active, colour, weight, count):
    h2, w2, n, c = summed.shape
    rows = h2 * w2 * n
    return pl.pallas_call(
        functools.partial(back_two_kernel, count),
        out_shape=(
            jax.ShapeDtypeStruct((h2 + 2, w2 + 2, n, c), bf16),
            jax.ShapeDtypeStruct((128, c), f32),
        )
        + tuple(jax.ShapeDtypeStruct((rows, c), bf16) for _ in range(count)),
        grid_spec=pltpu.PrefetchScalarGridSpec(
            num_scalar_prefetch=1,
            grid=(9,),
            in_specs=[
                whole(grads.shape),
                whole(summed.shape),
                whole(active.shape),
                whole(colour.shape),
                pl.BlockSpec((1,) + weight.shape[1:], lambda t, r: (t, 0, 0)),
            ],
            out_specs=(whole((h2 + 2, w2 + 2, n, c)), whole((128, c)))
            + tuple(whole((rows, c)) for _ in range(count)),
            scratch_shapes=[pltpu.VMEM((count, rows, c), f32)],
        ),
        compiler_params=kernel_params(28),
        name="back_two",
    )(row, grads, summed, active, colour, weight)


def weight_two_kernel(count, row_ref, gpad_ref, *refs):
    blocks, raws, (out_ref, skip_ref) = refs[:count], refs[count : 2 * count], refs[2 * count :]
    h2, w2, n, c = (gpad_ref.shape[0] - 2, gpad_ref.shape[1] - 2) + gpad_ref.shape[2:]
    t = pl.program_id(0)
    dy, dx = lax.div(t, 3), lax.rem(t, 3)
    shifted = flat(gpad_ref[pl.ds(2 - dy, h2), pl.ds(2 - dx, w2)])
    for k in range(count):
        out_ref[0, owned_rows(row_ref, k, c), :] = times(blocks[k][...], shifted).astype(bf16)

    @pl.when(t == 8)
    def _():
        phases = gpad_ref[1 : h2 + 1, 1 : w2 + 1].reshape(h2 // 2, 2, w2 // 2, 2, n, c)
        for k in range(count):
            size = raws[k].shape[0]
            skip_ref[owned_rows(row_ref, k, size), :] = sum(
                times(raws[k][...], flat(phases[:, a, :, b])) for a in range(2) for b in range(2)
            ).astype(bf16)


def weight_two(row, gpad, blocks, raws):
    c = gpad.shape[-1]
    count = len(blocks)
    tall, wide = count * blocks[0].shape[0], count * raws[0].shape[0]
    return pl.pallas_call(
        functools.partial(weight_two_kernel, count),
        out_shape=(
            jax.ShapeDtypeStruct((9, tall, c), bf16),
            jax.ShapeDtypeStruct((wide, c), bf16),
        ),
        grid_spec=pltpu.PrefetchScalarGridSpec(
            num_scalar_prefetch=1,
            grid=(9,),
            in_specs=[whole(gpad.shape)] + [whole(b.shape) for b in blocks + raws],
            out_specs=(pl.BlockSpec((1, tall, c), lambda t, r: (t, 0, 0)), whole((wide, c))),
        ),
        compiler_params=kernel_params(28),
        name="weight_two",
    )(row, gpad, *blocks, *raws)


def back_one_kernel(count, row_ref, g_ref, w_ref, *refs):
    blocks, out_ref, outs = refs[:count], refs[count], refs[count + 1 : 2 * count + 1]
    pad_ref, acc_ref = refs[2 * count + 1 :]
    h2, w2, n, c = g_ref.shape
    size = blocks[0].shape[0]
    t = pl.program_id(0)
    dy, dx = lax.div(t, 3), lax.rem(t, 3)

    @pl.when(t == 0)
    def _():
        pad_ref[...] = jnp.zeros_like(pad_ref)
        pad_ref[1 : h2 + 1, 1 : w2 + 1] = g_ref[...]
        acc_ref[...] = jnp.zeros_like(acc_ref)

    shifted = pad_ref[pl.ds(2 - dy, h2), pl.ds(2 - dx, w2)].astype(f32)
    pooled = flat(sum_two(shifted)).astype(bf16)
    for k in range(count):
        rows = owned_rows(row_ref, k, size)
        acc_ref[k] += contract_last(pooled, w_ref[0, rows, :])
        out_ref[0, rows, :] = times(blocks[k][...], pooled).astype(bf16)

    @pl.when(t == 8)
    def _():
        for k in range(count):
            outs[k][...] = acc_ref[k].astype(bf16)


def back_one(row, grads, weight, blocks):
    h2, w2, n, c = grads.shape
    count = len(blocks)
    size, rows = blocks[0].shape
    return pl.pallas_call(
        functools.partial(back_one_kernel, count),
        out_shape=(jax.ShapeDtypeStruct((9, count * size, c), bf16),)
        + tuple(jax.ShapeDtypeStruct((rows, size), bf16) for _ in range(count)),
        grid_spec=pltpu.PrefetchScalarGridSpec(
            num_scalar_prefetch=1,
            grid=(9,),
            in_specs=[
                whole(grads.shape),
                pl.BlockSpec((1,) + weight.shape[1:], lambda t, r: (t, 0, 0)),
            ]
            + [whole(b.shape) for b in blocks],
            out_specs=(pl.BlockSpec((1, count * size, c), lambda t, r: (t, 0, 0)),)
            + tuple(whole((rows, size)) for _ in range(count)),
            scratch_shapes=[
                pltpu.VMEM((h2 + 2, w2 + 2, n, c), bf16),
                pltpu.VMEM((count, rows, size), f32),
            ],
        ),
        compiler_params=kernel_params(28),
        name="back_one",
    )(row, grads, weight, *blocks)


def in_order(pieces, axis_name):
    piled = jnp.stack(pieces, axis=0)
    r = lax.axis_index(axis_name)
    return jnp.concatenate(
        [
            lax.dynamic_index_in_dim(piled, lax.bitwise_xor(r, j), 0, keepdims=False)
            for j in range(len(pieces))
        ],
        axis=0,
    )


def gram_share(owned, pieces):
    blocks = [
        lax.dot_general(piece, owned, (((0,), (0,)), ((), ())), preferred_element_type=f32)
        for piece in pieces
    ]
    return in_order(blocks, "row")


def gram_whole(panel):
    n = lax.axis_size("dp")
    h, z = lax.axis_index("half"), lax.axis_index("dp")
    total = group_sum_wide(panel)
    pieces = row_gather(total)
    piled = jnp.stack(pieces, axis=0)
    r = lax.axis_index("row")
    return jnp.concatenate(
        [
            lax.dynamic_index_in_dim(piled, lax.bitwise_xor(r, j), 0, keepdims=False)
            for j in range(len(pieces))
        ],
        axis=1,
    )


def group_sum_wide(value):
    return group_gather(group_scatter(value))


def mul(left, right):
    return jnp.dot(left, right, precision=high, preferred_element_type=f32)


def newton_columns(gram, own):
    scale = lax.rsqrt(jnp.trace(gram) + NEWTON_EPSILON)
    current = gram * (scale * scale)
    identity = jnp.eye(gram.shape[0], dtype=f32)
    maps = []
    for iteration in range(NS_ITERS):
        square = mul(current, current)
        mapping = NS_COEF[0] * identity + NS_COEF[1] * current + NS_COEF[2] * square
        maps.append(mapping)
        if iteration < NS_ITERS - 1:
            current = mul(mapping, mul(current, mapping))
    start = lax.axis_index("row") * own
    columns = lax.dynamic_slice_in_dim(maps[-1], start, own, 1)
    for mapping in maps[-2::-1]:
        columns = mul(mapping, columns)
    return columns * scale


def muon(master, moment, gradient, groups):
    moment_new = MOMENTUM * moment + gradient
    owned = moment_new.astype(bf16)
    pieces = row_gather(owned)
    own = owned.shape[1]
    gram = gram_whole(gram_share(owned, pieces))
    columns = newton_columns(gram, own).astype(bf16)
    r = lax.axis_index("row")
    direction = sum(
        times(
            piece,
            lax.dynamic_slice_in_dim(columns, lax.bitwise_xor(r, k) * own, own, 0),
        )
        for k, piece in enumerate(pieces)
    )
    factor = 0.2 * math.sqrt(max(master.shape[0] * groups, own * len(pieces)))
    return master - MUON_RATE * (factor * direction + DECAY * master), moment_new


def transposed(values):
    return jnp.transpose(values.astype(f32)).astype(values.dtype)


def place_kernel(count, sizes, index_ref, mine_ref, other_ref, *refs):
    outs = refs[-len(sizes) :]

    def write(values):
        turned = jnp.transpose(values.astype(f32)).astype(bf16)
        start = 0
        for size, out_ref in zip(sizes, outs):
            out_ref[...] = turned[start : start + size]
            start += size

    @pl.when(pl.program_id(0) < count)
    def _():
        write(mine_ref[0])

    @pl.when(pl.program_id(0) >= count)
    def _():
        write(other_ref[0])


def place(held, index, mine, other, sizes):
    count, c, wide = mine.shape
    groups = 2 * lax.axis_size("dp")
    given = [] if held is None else list(held)
    return pl.pallas_call(
        functools.partial(place_kernel, count, sizes),
        out_shape=tuple(jax.ShapeDtypeStruct((groups * size, c), bf16) for size in sizes),
        grid_spec=pltpu.PrefetchScalarGridSpec(
            num_scalar_prefetch=1,
            grid=(2 * count,),
            in_specs=[
                pl.BlockSpec((1, c, wide), lambda t, r: (jnp.minimum(t, count - 1), 0, 0)),
                pl.BlockSpec((1, c, wide), lambda t, r: (jnp.maximum(t - count, 0), 0, 0)),
            ]
            + [pl.BlockSpec(memory_space=pl.ANY) for _ in given],
            out_specs=tuple(pl.BlockSpec((size, c), lambda t, r: (r[t], 0)) for size in sizes),
        ),
        input_output_aliases={3 + i: i for i in range(len(given))},
        compiler_params=kernel_params(),
        name="place",
    )(jnp.stack(index).astype(jnp.int32), mine, other, *given)


def place_cores(held, spots, mine, sizes):
    n = lax.axis_size("dp")
    h = lax.axis_index("half")
    index = [h * n + spot for spot in spots] + [(1 - h) * n + spot for spot in spots]
    return place(held, index, mine, axis_swap(mine, "half", 1), sizes)


def weight_one_kernel(groups, where_ref, inverse_ref, *refs):
    pieces = refs[:groups]
    all_ref, old_ref, out_ref, low_ref, pad_ref, pool_ref, grads, inputs_ref, moment_ref, sem = refs[
        groups:
    ]
    copies = [
        pltpu.make_async_copy(piece, grads.at[g], sem.at[g]) for g, piece in enumerate(pieces)
    ]
    copies.append(pltpu.make_async_copy(all_ref, inputs_ref, sem.at[groups]))
    copies.append(pltpu.make_async_copy(old_ref, moment_ref, sem.at[groups + 1]))
    for copy in copies:
        copy.start()
    h2, w2, n, c = grads.shape[1:]
    size = h2 * w2 * n // 4
    row, d = where_ref[0], where_ref[1] * (groups // 2) + where_ref[2]
    owners = []
    for side in range(2):
        for k in range(groups // 2):
            spot = lax.rem(where_ref[2] + groups // 2 - k, groups // 2)
            owners.append((where_ref[1] if side == 0 else 1 - where_ref[1]) * (groups // 2) + spot)
    pad_ref[...] = jnp.zeros_like(pad_ref)
    for g in range(groups):
        copies[g].wait()
        pad_ref[1 : h2 + 1, 1 : w2 + 1] = grads[g]
        for j in range(2):
            dy, dx = lax.div(d + j, 3), lax.rem(d + j, 3)
            shifted = pad_ref[pl.ds(2 - dy, h2), pl.ds(2 - dx, w2)].astype(f32)
            pool_ref[j, g * size : (g + 1) * size, :] = flat(sum_two(shifted)).astype(bf16)
    copies[groups].wait()
    copies[groups + 1].wait()
    inverse = inverse_ref[0, 0]
    for q in range(groups + 1):
        i = lax.rem(d + q, groups)
        j = lax.div(d + q, groups)
        start = lax.bitwise_xor(row, lax.div(i, 2)) * (2 * c) + lax.rem(i, 2) * c
        start = pl.multiple_of(start, c)
        total = sum(
            times(inputs_ref[owners[g], pl.ds(start, c), :], pool_ref[j, g * size : (g + 1) * size, :])
            for g in range(groups)
        )
        span = slice(q * c, (q + 1) * c)
        moment = MOMENTUM * moment_ref[:, span] + jnp.transpose(total) * inverse
        out_ref[:, span] = moment
        low_ref[:, span] = moment.astype(bf16)


def weight_one_moment(where, inverse, grads, inputs, moment):
    h2, w2, n, c = grads[0].shape
    groups = len(grads)
    vmem = pl.BlockSpec(memory_space=pltpu.VMEM)
    smem = pl.BlockSpec(memory_space=pltpu.SMEM)
    flops = 2 * moment.shape[1] * c * groups * h2 * w2 * n // 4
    return pl.pallas_call(
        functools.partial(weight_one_kernel, groups),
        out_shape=(
            jax.ShapeDtypeStruct(moment.shape, f32),
            jax.ShapeDtypeStruct(moment.shape, bf16),
        ),
        in_specs=[smem, smem] + [pl.BlockSpec(memory_space=pl.ANY)] * (groups + 2),
        out_specs=(vmem, vmem),
        scratch_shapes=[
            pltpu.VMEM((h2 + 2, w2 + 2, n, c), bf16),
            pltpu.VMEM((2, groups * h2 * w2 * n // 4, c), bf16),
            pltpu.VMEM((groups,) + grads[0].shape, bf16),
            pltpu.VMEM(inputs.shape, bf16),
            pltpu.VMEM(moment.shape, f32),
            pltpu.SemaphoreType.DMA((groups + 2,)),
        ],
        compiler_params=kernel_params(28),
        cost_estimate=pl.CostEstimate(flops=4 * flops, bytes_accessed=0, transcendentals=0),
        name="weight_one",
    )(where, inverse, *grads, inputs, moment)


def weight_pack_kernel(count, row_ref, gpad_ref, *refs):
    blocks, raws, (out_ref, tall_ref) = refs[:count], refs[count : 2 * count], refs[2 * count :]
    h2, w2, n, c = (gpad_ref.shape[0] - 2, gpad_ref.shape[1] - 2) + gpad_ref.shape[2:]
    groups = out_ref.shape[0]
    unit = count * c // groups
    half = unit // 2
    t = pl.program_id(0)
    dy, dx = lax.div(t, 3), lax.rem(t, 3)
    shifted = flat(gpad_ref[pl.ds(2 - dy, h2), pl.ds(2 - dx, w2)])
    for k in range(count):
        tall_ref[owned_rows(row_ref, k, c), :] = times(blocks[k][...], shifted)
    for i in range(groups):
        rows = tall_ref[i * unit : (i + 1) * unit, :]
        u = groups * t + i
        packed = jnp.concatenate([rows[:half], rows[half:]], axis=1).astype(bf16)
        spot = pl.multiple_of(lax.rem(u, groups + 1) * half, half)
        out_ref[lax.div(u, groups + 1), pl.ds(spot, half), :] = packed

    @pl.when(t == 8)
    def _():
        phases = gpad_ref[1 : h2 + 1, 1 : w2 + 1].reshape(h2 // 2, 2, w2 // 2, 2, n, c)
        size = raws[0].shape[0]
        each = count * size // groups
        for k in range(count):
            block = sum(
                times(raws[k][...], flat(phases[:, a, :, b])) for a in range(2) for b in range(2)
            )
            for m in range(size // each):
                rows = block[m * each : (m + 1) * each]
                packed = jnp.concatenate([rows[: each // 2], rows[each // 2 :]], axis=1)
                spot = lax.bitwise_xor(row_ref[0], k) * (size // each) + m
                out_ref[spot, (groups + 1) * half :, :] = packed.astype(bf16)


def weight_pack(row, gpad, blocks, raws, groups):
    c = gpad.shape[-1]
    count = len(blocks)
    tall, wide = count * blocks[0].shape[0], count * raws[0].shape[0]
    shape = (groups, (9 * tall + wide) // (2 * groups), 2 * c)
    flops = 2 * 9 * tall * c * blocks[0].shape[1]
    return pl.pallas_call(
        functools.partial(weight_pack_kernel, count),
        out_shape=jax.ShapeDtypeStruct(shape, bf16),
        grid_spec=pltpu.PrefetchScalarGridSpec(
            num_scalar_prefetch=1,
            grid=(9,),
            in_specs=[whole(gpad.shape)] + [whole(b.shape) for b in blocks + raws],
            out_specs=whole(shape),
            scratch_shapes=[pltpu.VMEM((tall, c), f32)],
        ),
        compiler_params=kernel_params(28),
        cost_estimate=pl.CostEstimate(flops=3 * flops, bytes_accessed=0, transcendentals=0),
        name="weight_two",
    )(row, gpad, *blocks, *raws)


def moments_kernel(count, inverse_ref, *refs):
    pieces = refs[:count]
    tall_ref, skip_ref, tall_out, skip_out, low_ref = refs[count:]
    c, size = tall_ref.shape
    total = pieces[0][...].astype(f32)
    for piece in pieces[1:]:
        total = total + piece[...].astype(f32)
    total = total * inverse_ref[0, 0]
    units = 9
    half = size // (2 * units)
    for q in range(units):
        rows = total[q * half : (q + 1) * half]
        rows = jnp.concatenate([rows[:, :c], rows[:, c:]], axis=0)
        span = slice(2 * q * half, 2 * (q + 1) * half)
        moment = MOMENTUM * tall_ref[:, span] + jnp.transpose(rows)
        tall_out[:, span] = moment
        low_ref[:, span] = moment.astype(bf16)
    rows = total[units * half :]
    rows = jnp.concatenate([rows[:, :c], rows[:, c:]], axis=0)
    moment = MOMENTUM * skip_ref[...] + jnp.transpose(rows)
    skip_out[...] = moment
    low_ref[:, size:] = moment.astype(bf16)


def moments_two(inverse, pieces, tall, skip):
    vmem = pl.BlockSpec(memory_space=pltpu.VMEM)
    return pl.pallas_call(
        functools.partial(moments_kernel, len(pieces)),
        out_shape=(
            jax.ShapeDtypeStruct(tall.shape, f32),
            jax.ShapeDtypeStruct(skip.shape, f32),
            jax.ShapeDtypeStruct((tall.shape[0], tall.shape[1] + skip.shape[1]), bf16),
        ),
        in_specs=[pl.BlockSpec(memory_space=pltpu.SMEM)] + [vmem] * (len(pieces) + 2),
        out_specs=(vmem, vmem, vmem),
        compiler_params=kernel_params(),
        name="moments",
    )(inverse, *pieces, tall, skip)


def gram_kernel(count, spans, row_ref, *refs):
    pieces, out_ref, hold_ref = refs[:count], refs[count], refs[count + 1]
    for m, (start, stop) in enumerate(spans):
        owned = pieces[0][:, start:stop]
        for k in range(count):
            hold_ref[k] = contract_last(owned, pieces[k][:, start:stop])
        out_ref[m] = jnp.concatenate(
            [hold_ref[lax.bitwise_xor(row_ref[0], j)] for j in range(count)], axis=1
        )


def gram_rows(row, pieces, spans):
    c = pieces[0].shape[0]
    count = len(pieces)
    vmem = pl.BlockSpec(memory_space=pltpu.VMEM)
    return pl.pallas_call(
        functools.partial(gram_kernel, count, spans),
        out_shape=jax.ShapeDtypeStruct((len(spans), c, count * c), f32),
        in_specs=[pl.BlockSpec(memory_space=pltpu.SMEM)] + [vmem] * count,
        out_specs=vmem,
        scratch_shapes=[pltpu.VMEM((count, c, c), f32)],
        compiler_params=kernel_params(),
        cost_estimate=pl.CostEstimate(
            flops=6 * count * c * c * pieces[0].shape[1], bytes_accessed=0, transcendentals=0
        ),
        name="gram",
    )(row, *pieces)


def gram_terms(halves):
    kept = near_halves(halves)
    return near_blocks(kept, kept)


def gram_total(terms):
    return placed_in_order(straight(sum(terms)))


def newton_kernel(count, sides, where_ref, *refs):
    pieces = refs[: sides * count]
    out_ref, a_ref, ah, al, maps_ref, th, tl = refs[sides * count :]
    size = a_ref.shape[0]
    own = size // count
    block = size // 3
    row, h = where_ref[0], where_ref[1]
    for q in range(count):
        for side in range(sides):
            piece = pieces[side * count + q]
            s = piece.shape[2]
            half = 0 if sides == 1 else (h if side == 0 else 1 - h)
            for p in range(piece.shape[0]):
                start = lax.bitwise_xor(row, q) * own + half * (own // 2) + p * s
                a_ref[pl.ds(pl.multiple_of(start, s), s), :] = piece[p, 0]

    def eye(shape, offset):
        rows = lax.broadcasted_iota(jnp.int32, shape, 0) + offset
        return rows == lax.broadcasted_iota(jnp.int32, shape, 1)

    whole_gram = a_ref[...]
    trace = jnp.sum(jnp.where(eye(whole_gram.shape, 0), whole_gram, 0.0), keepdims=True)
    scale = lax.rsqrt(trace + NEWTON_EPSILON)
    a_ref[...] = whole_gram * (scale * scale)

    def split(values):
        top = values.astype(bf16)
        return top, (values - top.astype(f32)).astype(bf16)

    def three(xh, xl, yh, yl):
        return times(xh, yh) + (times(xh, yl) + times(xl, yh))

    spans = [slice(i * block, (i + 1) * block) for i in range(3)]

    def symmetric(product, write):
        for i in range(3):
            for j in range(i, 3):
                write(i, j, product(spans[i], spans[j]))

    def store(high_ref, low_ref, i, j, value):
        top, low = split(value)
        high_ref[spans[i], spans[j]] = top
        low_ref[spans[i], spans[j]] = low
        if i != j:
            turned = jnp.transpose(value)
            top, low = split(turned)
            high_ref[spans[j], spans[i]] = top
            low_ref[spans[j], spans[i]] = low

    top, low = split(a_ref[...])
    ah[...] = top
    al[...] = low

    def step(k, carry):
        top = maps_ref.at[k]

        def write_map(i, j, value):
            value = NS_COEF[1] * a_ref[spans[i], spans[j]] + NS_COEF[2] * value
            if i == j:
                value = value + jnp.where(eye(value.shape, 0), NS_COEF[0], 0.0)
            top[spans[i], spans[j]] = value.astype(bf16)
            if i != j:
                top[spans[j], spans[i]] = jnp.transpose(value).astype(bf16)

        def square(a, b):
            if a == b:
                cross = times(ah[a, :], al[:, a])
                return times(ah[a, :], ah[:, a]) + (cross + jnp.transpose(cross))
            return three(ah[a, :], al[a, :], ah[:, b], al[:, b])

        symmetric(square, write_map)
        symmetric(
            lambda a, b: times(ah[a, :], top[:, b]) + times(al[a, :], top[:, b]),
            functools.partial(store, th, tl),
        )

        def write_gram(i, j, value):
            a_ref[spans[i], spans[j]] = value
            store(ah, al, i, j, value)
            if i != j:
                a_ref[spans[j], spans[i]] = jnp.transpose(value)

        symmetric(lambda a, b: times(top[a, :], th[:, b]) + times(top[a, :], tl[:, b]), write_gram)
        return carry

    lax.fori_loop(0, NS_ITERS - 1, step, 0)
    mine = pl.ds(pl.multiple_of(row * own, own), own)
    last = a_ref[mine, :]
    columns = NS_COEF[1] * last + NS_COEF[2] * three(ah[mine, :], al[mine, :], ah[...], al[...])
    columns = columns + jnp.where(eye(columns.shape, row * own), NS_COEF[0], 0.0)

    def fold(k, columns):
        high_part, low_part = split(columns)
        top = maps_ref[NS_ITERS - 2 - k]
        return times(high_part, top) + times(low_part, top)

    columns = lax.fori_loop(0, NS_ITERS - 1, fold, columns) * scale
    for j in range(count):
        out_ref[0, j] = columns[:, j * own : (j + 1) * own].astype(bf16)


def newton(where, pieces, count):
    sides = len(pieces) // count
    n, m, s, size = pieces[0].shape
    own = size // count
    square = (size, size)
    maps = (NS_ITERS - 1,) + square
    return pl.pallas_call(
        functools.partial(newton_kernel, count, sides),
        out_shape=jax.ShapeDtypeStruct((m, count, own, own), bf16),
        grid_spec=pltpu.PrefetchScalarGridSpec(
            num_scalar_prefetch=1,
            grid=(m,),
            in_specs=[pl.BlockSpec((n, 1, s, size), lambda t, r: (0, t, 0, 0)) for _ in pieces],
            out_specs=pl.BlockSpec((1, count, own, own), lambda t, r: (t, 0, 0, 0)),
            scratch_shapes=[
                pltpu.VMEM(square, f32),
                pltpu.VMEM(square, bf16),
                pltpu.VMEM(square, bf16),
                pltpu.VMEM(maps, bf16),
                pltpu.VMEM(square, bf16),
                pltpu.VMEM(square, bf16),
            ],
        ),
        compiler_params=kernel_params(36),
        cost_estimate=pl.CostEstimate(
            flops=m * 50 * size**3, bytes_accessed=0, transcendentals=0
        ),
        name="newton",
    )(where, *pieces)


def update_kernel(count, spans, factors, row_ref, map_ref, *refs):
    pieces, masters, outs = refs[:count], refs[count : count + len(spans)], refs[count + len(spans) :]
    for m, (start, stop) in enumerate(spans):
        direction = sum(
            times(map_ref[m, lax.bitwise_xor(row_ref[0], k)], pieces[k][:, start:stop])
            for k in range(count)
        )
        master = masters[m][...]
        outs[m][...] = master - MUON_RATE * (factors[m] * direction + DECAY * master)


def update(row, maps, pieces, masters, spans, factors):
    count = len(pieces)
    vmem = pl.BlockSpec(memory_space=pltpu.VMEM)
    return pl.pallas_call(
        functools.partial(update_kernel, count, spans, factors),
        out_shape=tuple(jax.ShapeDtypeStruct(master.shape, f32) for master in masters),
        in_specs=[pl.BlockSpec(memory_space=pltpu.SMEM)] + [vmem] * (1 + count + len(masters)),
        out_specs=(vmem,) * len(masters),
        compiler_params=kernel_params(),
        name="update",
    )(row, maps, *pieces, *masters)


def back_in_kernel(count, row_ref, g_ref, w_ref, *refs):
    outs, (pad_ref, acc_ref) = refs[:count], refs[count:]
    h2, w2, n, c = g_ref.shape
    size = outs[0].shape[1]
    t = pl.program_id(0)
    dy, dx = lax.div(t, 3), lax.rem(t, 3)

    @pl.when(t == 0)
    def _():
        pad_ref[...] = jnp.zeros_like(pad_ref)
        pad_ref[1 : h2 + 1, 1 : w2 + 1] = g_ref[...]
        acc_ref[...] = jnp.zeros_like(acc_ref)

    shifted = pad_ref[pl.ds(2 - dy, h2), pl.ds(2 - dx, w2)].astype(f32)
    pooled = flat(sum_two(shifted)).astype(bf16)
    for k in range(count):
        acc_ref[k] += contract_last(pooled, w_ref[0, owned_rows(row_ref, k, size), :])

    @pl.when(t == 8)
    def _():
        for k in range(count):
            outs[k][...] = acc_ref[k].astype(bf16)


def back_in(row, grads, weight, count):
    h2, w2, n, c = grads.shape
    size, rows = weight.shape[1] // count, h2 * w2 * n // 4
    return pl.pallas_call(
        functools.partial(back_in_kernel, count),
        out_shape=tuple(jax.ShapeDtypeStruct((rows, size), bf16) for _ in range(count)),
        grid_spec=pltpu.PrefetchScalarGridSpec(
            num_scalar_prefetch=1,
            grid=(9,),
            in_specs=[
                whole(grads.shape),
                pl.BlockSpec((1,) + weight.shape[1:], lambda t, r: (t, 0, 0)),
            ],
            out_specs=tuple(whole((rows, size)) for _ in range(count)),
            scratch_shapes=[
                pltpu.VMEM((h2 + 2, w2 + 2, n, c), bf16),
                pltpu.VMEM((count, rows, size), f32),
            ],
        ),
        compiler_params=kernel_params(28),
        cost_estimate=pl.CostEstimate(
            flops=6 * 9 * rows * count * size * c, bytes_accessed=0, transcendentals=0
        ),
        name="back_one",
    )(row, grads, weight)


def adam_update(weight, gradient, mean_old, square_old, rate):
    mean_new = BETA_ONE * mean_old + (1.0 - BETA_ONE) * gradient
    square_new = BETA_TWO * square_old + (1.0 - BETA_TWO) * gradient * gradient
    ratio = (
        mean_new
        / (1.0 - BETA_ONE**STEP)
        / (jnp.sqrt(square_new / (1.0 - BETA_TWO**STEP)) + ADAM_EPS)
    )
    return (weight - rate * (ratio + DECAY * weight), mean_new, square_new)


def moments_of(totals, count):
    centre = totals[:MICRO] / count
    return centre, lax.rsqrt(totals[MICRO:] / count - centre * centre + BN_EPS)


def per_image(values, n):
    return jnp.repeat(values, n // MICRO, axis=0)


def per_micro(values):
    return jnp.sum(values.reshape(MICRO, -1, values.shape[-1]), axis=1)


def wide_device(
    features,
    noise,
    labels,
    counted,
    disc_first,
    disc_second,
    disc_skip,
    disc_head,
    disc_table,
    conv_first,
    conv_second,
    conv_skip,
    momentum_first,
    momentum_second,
    momentum_skip,
    class_table,
    table_mean,
    table_square,
    norm_first,
    first_mean,
    first_square,
    norm_second,
    second_mean,
    second_square,
    colour_conv,
    colour_mean,
    colour_square,
):
    groups = lax.axis_size("half") * lax.axis_size("dp")
    ranks = lax.axis_size("row")
    row = lax.axis_index("row").astype(jnp.int32).reshape(1)
    n, h, w, c_in = features.shape
    c_out = conv_first.shape[1]
    count_low = float(n // MICRO * h * w * groups)
    count_high = 4.0 * count_low

    inputs = jnp.transpose(features, (1, 2, 0, 3))
    raw = inputs.astype(f32)
    sums_low = jnp.concatenate(
        [per_micro(jnp.sum(raw, axis=(0, 1))), per_micro(jnp.sum(raw * raw, axis=(0, 1)))], axis=0
    )
    totals_low = group_sum(sums_low)
    weight_one = group_gather(conv_first.astype(bf16)).reshape(9, ranks * c_in, c_out)

    onehot = (labels[:, None] == jnp.arange(NCLS)[None, :]).astype(f32)
    conds = jnp.concatenate([jnp.dot(onehot, class_table, precision=highest), noise], axis=1)
    class_disc = jnp.dot(onehot, disc_table, precision=highest)
    mods_one = jnp.einsum("bk,kgc->bgc", conds, norm_first, precision=highest)
    mods_two = jnp.einsum("bk,kgc->bgc", conds, norm_second, precision=highest)

    centre_one, spread_one = moments_of(totals_low, count_low)
    centre_one, spread_one = per_image(centre_one, n), per_image(spread_one, n)
    gain_one, gain_two = 1.0 + mods_one[:, 0], 1.0 + mods_two[:, 0]
    normed_one = (raw - centre_one) * spread_one
    pre_one = normed_one * gain_one + mods_one[:, 1]
    acted_one = flat(jax.nn.silu(pre_one).astype(bf16))
    ones = row_gather(acted_one)
    raws = row_gather(flat(inputs))

    hidden, sums_high = conv_one(row, [one[None] for one in ones], weight_one, (h, w, n))
    held_second, held_skip, _ = lax.optimization_barrier(
        (conv_second.astype(bf16), conv_skip.astype(bf16), weight_one[0, 0, 0])
    )
    weight_skip = group_gather(held_skip)
    weight_two = group_gather(held_second).reshape(9, ranks * c_out, c_out)
    totals_high = group_sum(sums_high)
    centre_two, spread_two = moments_of(totals_high, count_high)
    centre_two, spread_two = per_image(centre_two, n), per_image(spread_two, n)
    normed_two = (hidden - centre_two) * spread_two
    pre_two = normed_two * gain_two + mods_two[:, 1]
    acted_two = jax.nn.silu(pre_two).astype(bf16)
    twos = row_gather(acted_two)

    colour = jnp.pad(
        jnp.transpose(colour_conv, (0, 2, 1)).astype(bf16), ((0, 0), (0, PAD - 3), (0, 0))
    )
    summed, active, picture = conv_two(row, twos, [one[None] for one in raws], weight_two, weight_skip, colour)
    picture = row_sum(picture)

    first_taps = jnp.pad(disc_first.reshape(9, 3, -1), ((0, 0), (0, PAD - 3), (0, 0)))
    second_taps = disc_second.reshape(9, -1, disc_second.shape[-1])
    skip_taps = jnp.pad(disc_skip, ((0, PAD - 3), (0, 0)))
    mark = counted.astype(f32)[:, None]
    grads, loss_part = critic(
        picture,
        first_taps,
        second_taps,
        skip_taps,
        disc_head[None, :] + class_disc,
        mark,
        (2 * h, 2 * w, n),
    )
    colour_rows = jnp.pad(colour.reshape(9 * PAD, c_out), ((0, 128 - 9 * PAD), (0, 0)))
    backs = back_two(row, grads, summed, active, colour_rows, weight_two, ranks)
    gpad, grad_colour, pieces = backs[0], backs[1], backs[2:]
    grad_two, grad_skip = weight_two_grads(row, gpad, twos, raws)
    grad_acted_two = row_scatter(list(pieces)).reshape(hidden.shape)

    grad_pre_two = grad_acted_two * silu_slope(pre_two)
    gains_two = jnp.sum(grad_pre_two * normed_two, axis=(0, 1))
    shifts_two = jnp.sum(grad_pre_two, axis=(0, 1))
    back_sums = group_sum(
        jnp.concatenate([per_micro(gain_two * shifts_two), per_micro(gain_two * gains_two)], axis=0)
    )
    mean_g = per_image(back_sums[:MICRO] / count_high, n)
    mean_gy = per_image(back_sums[MICRO:] / count_high, n)
    grad_hidden = (spread_two * (grad_pre_two * gain_two - mean_g - normed_two * mean_gy)).astype(
        bf16
    )
    ones_turned = [jnp.transpose(one) for one in ones]
    backs = back_one(row, grad_hidden, weight_one, ones_turned)
    grad_one, pieces = flat(backs[0]), backs[1:]
    grad_acted_one = row_scatter(list(pieces)).reshape(raw.shape)
    grad_pre_one = grad_acted_one * silu_slope(pre_one)
    gains_one = jnp.sum(grad_pre_one * normed_one, axis=(0, 1))
    shifts_one = jnp.sum(grad_pre_one, axis=(0, 1))
    grad_mods_one = jnp.stack([gains_one, shifts_one], axis=1)
    grad_mods_two = jnp.stack([gains_two, shifts_two], axis=1)

    grad_cond = jnp.einsum("bgc,kgc->bk", grad_mods_one, norm_first[:EMB], precision=highest)
    grad_cond = grad_cond + jnp.einsum(
        "bgc,kgc->bk", grad_mods_two, norm_second[:EMB], precision=highest
    )
    grad_cond = row_sum(grad_cond)

    count_part = jnp.sum(counted).astype(f32)
    small = jnp.concatenate(
        [
            grad_colour[: 9 * PAD],
            jnp.broadcast_to(loss_part[:1, :1], (1, c_out)),
            jnp.broadcast_to(count_part, (1, c_out)),
        ],
        axis=0,
    )
    small = group_sum(small)
    loss_sum, fake_count = small[9 * PAD, 0], small[9 * PAD + 1, 0]
    inverse = 1.0 / fake_count
    g_colour = jnp.transpose(small[: 9 * PAD].reshape(9, PAD, c_out)[:, :3], (0, 2, 1))

    known = group_pile(jnp.concatenate([conds, labels.astype(f32)[:, None]], axis=1))
    found = group_pile(
        jnp.concatenate(
            [grad_mods_one.reshape(n, -1), grad_mods_two.reshape(n, -1), grad_cond], axis=1
        )
    )
    conds_all, labels_all = known[:, :-1], known[:, -1].astype(jnp.int32)
    onehot_all = (labels_all[:, None] == jnp.arange(NCLS)[None, :]).astype(f32)
    cut_one, cut_two = 2 * c_in, 2 * c_in + 2 * c_out
    g_norm = lax.dot_general(
        conds_all,
        found[:, :cut_two],
        (((0,), (0,)), ((), ())),
        precision=highest,
        preferred_element_type=f32,
    )
    g_norm_one = g_norm[:, :cut_one].reshape(norm_first.shape)
    g_norm_two = g_norm[:, cut_one:].reshape(norm_second.shape)
    g_table = lax.dot_general(
        onehot_all,
        found[:, cut_two:],
        (((0,), (0,)), ((), ())),
        precision=highest,
        preferred_element_type=f32,
    )

    shares = [group_scatter(flat(g)) for g in (grad_one, grad_two, grad_skip)]
    muons = [
        muon(master, moment, share * inverse, groups)
        for master, moment, share in zip(
            (conv_first, conv_second, conv_skip),
            (momentum_first, momentum_second, momentum_skip),
            shares,
        )
    ]
    table_new = adam_update(class_table, g_table * inverse, table_mean, table_square, ADAM_RATE)
    first_new = adam_update(norm_first, g_norm_one * inverse, first_mean, first_square, ADAM_RATE)
    second_new = adam_update(
        norm_second, g_norm_two * inverse, second_mean, second_square, ADAM_RATE
    )
    colour_new = adam_update(
        colour_conv, g_colour * inverse, colour_mean, colour_square, COLOUR_RATE
    )
    return (
        (loss_sum, fake_count)
        + tuple(m[0] for m in muons)
        + tuple(m[1] for m in muons)
        + table_new
        + first_new
        + second_new
        + colour_new
    )


def near_device(
    features,
    noise,
    labels,
    counted,
    disc_first,
    disc_second,
    disc_skip,
    disc_head,
    disc_table,
    conv_first,
    conv_second,
    conv_skip,
    momentum_first,
    momentum_second,
    momentum_skip,
    class_table,
    table_mean,
    table_square,
    norm_first,
    first_mean,
    first_square,
    norm_second,
    second_mean,
    second_square,
    colour_conv,
    colour_mean,
    colour_square,
):
    groups = lax.axis_size("half") * lax.axis_size("dp")
    ranks = lax.axis_size("row")
    row = lax.axis_index("row").astype(jnp.int32).reshape(1)
    n, h, w, c_in = features.shape
    c_out = conv_first.shape[1]
    count_low = float(n // MICRO * h * w * groups)
    count_high = 4.0 * count_low

    where = jnp.stack(
        [lax.axis_index("row"), lax.axis_index("half"), lax.axis_index("dp")]
    ).astype(jnp.int32)
    n_dp, half, spot = lax.axis_size("dp"), lax.axis_index("half"), lax.axis_index("dp")
    turned = conv_first.T.astype(bf16)
    below, above = [turned, step_below(turned, 1)], [turned, step_above(turned, 1)]
    inputs = jnp.transpose(features, (1, 2, 0, 3))
    raw = inputs.astype(f32)
    sums_low = jnp.concatenate(
        [
            per_micro(jnp.sum(raw, axis=(0, 1))),
            per_micro(jnp.sum(raw * raw, axis=(0, 1))),
            jnp.broadcast_to(jnp.sum(counted).astype(f32), (1, c_in)),
        ],
        axis=0,
    )
    totals_low = near_sum(sums_low)
    below.append(step_below(below[1], 2))
    above.append(step_above(above[1], 2))
    fake_count = totals_low[2 * MICRO, 0]
    inverse = 1.0 / fake_count

    onehot = (labels[:, None] == jnp.arange(NCLS)[None, :]).astype(f32)
    conds = jnp.concatenate([jnp.dot(onehot, class_table, precision=highest), noise], axis=1)
    class_disc = jnp.dot(onehot, disc_table, precision=highest)
    mods_one = jnp.einsum("bk,kgc->bgc", conds, norm_first, precision=highest)
    mods_two = jnp.einsum("bk,kgc->bgc", conds, norm_second, precision=highest)

    centre_one, spread_one = moments_of(totals_low[: 2 * MICRO], count_low)
    centre_one, spread_one = per_image(centre_one, n), per_image(spread_one, n)
    gain_one, gain_two = 1.0 + mods_one[:, 0], 1.0 + mods_two[:, 0]
    normed_one = (raw - centre_one) * spread_one
    pre_one = normed_one * gain_one + mods_one[:, 1]
    acted_one = flat(jax.nn.silu(pre_one).astype(bf16))
    pairs = row_gather(jnp.stack([acted_one, flat(inputs)], axis=0))
    sizes = (conv_first.shape[0],)
    down, up = lax.rem(spot + 3, 4), lax.rem(spot + 1, 4)
    held = place_cores(None, [spot, down, up], jnp.stack([turned, below[1], above[1]]), sizes)
    below.append(step_below(after(below[2], *pairs), 3))
    above.append(step_above(after(above[2], *pairs), 3))
    middle = jnp.where(spot >= 2, below[2], above[2])
    held = place_cores(held, [lax.rem(spot + 2, 4)], middle[None], sizes)
    below[3], above[3] = after(below[3], *held), after(above[3], *held)
    last = jnp.where(spot == 3, below[3], jnp.where(spot == 0, above[3], turned))
    end = jnp.where(spot == 3, 0, jnp.where(spot == 0, 3, spot))
    (weight_one,) = place_cores(held, [end], last[None], sizes)
    weight_one = weight_one.reshape(9, ranks * c_in, c_out)

    hidden, sums_high = conv_one(row, pairs, weight_one, (h, w, n))
    totals_high = near_sum(sums_high)
    other = jnp.concatenate([conv_second.T, conv_skip.T], axis=1).astype(bf16)
    other = jnp.pad(other, ((0, 0), (0, -other.shape[1] % 128)))
    others = lax.all_gather(after(other, below[3], above[3]), GROUP, axis=0)
    weight_two, weight_skip = place(
        None,
        list(range(groups)),
        others[: groups // 2],
        others[groups // 2 :],
        (conv_second.shape[0], conv_skip.shape[0]),
    )
    weight_two = weight_two.reshape(9, ranks * c_out, c_out)
    centre_two, spread_two = moments_of(totals_high, count_high)
    centre_two, spread_two = per_image(centre_two, n), per_image(spread_two, n)
    normed_two = (hidden - centre_two) * spread_two
    pre_two = normed_two * gain_two + mods_two[:, 1]
    acted_two = jax.nn.silu(pre_two).astype(bf16)
    twos = row_gather(acted_two)
    colour = jnp.pad(
        jnp.transpose(colour_conv, (0, 2, 1)).astype(bf16), ((0, 0), (0, PAD - 3), (0, 0))
    )
    summed, active, picture = conv_two(row, twos, pairs, weight_two, weight_skip, colour)
    kept_pairs = [after(pair, weight_two) for pair in pairs]
    turned = jnp.concatenate([jnp.transpose(pair[0]) for pair in kept_pairs], axis=0)
    ones_all = lax.all_gather(after(turned, others), GROUP, axis=0)

    picture = row_sum(picture)

    first_taps = jnp.pad(disc_first.reshape(9, 3, -1), ((0, 0), (0, PAD - 3), (0, 0)))
    second_taps = disc_second.reshape(9, -1, disc_second.shape[-1])
    skip_taps = jnp.pad(disc_skip, ((0, PAD - 3), (0, 0)))
    mark = counted.astype(f32)[:, None]
    grads, loss_part = critic(
        picture,
        first_taps,
        second_taps,
        skip_taps,
        disc_head[None, :] + class_disc,
        mark,
        (2 * h, 2 * w, n),
    )
    colour_rows = jnp.pad(colour.reshape(9 * PAD, c_out), ((0, 128 - 9 * PAD), (0, 0)))
    backs = back_two(row, grads, summed, active, colour_rows, weight_two, ranks)
    gpad, grad_colour = backs[0], backs[1]
    pieces = row_exchange(list(backs[2:]))
    packed = weight_pack(
        row,
        gpad,
        [jnp.transpose(flat(after(two, gpad))) for two in twos],
        [jnp.transpose(after(pair, gpad)[1]) for pair in pairs],
        groups,
    )
    kept = near_halves(packed.reshape((2, groups // 2) + packed.shape[1:]))
    pieces[-1] = after(pieces[-1], packed)
    grad_acted_two = sum(piece.astype(f32) for piece in pieces).reshape(hidden.shape)

    grad_pre_two = grad_acted_two * silu_slope(pre_two)
    gains_two = jnp.sum(grad_pre_two * normed_two, axis=(0, 1))
    shifts_two = jnp.sum(grad_pre_two, axis=(0, 1))
    back_sums = jnp.concatenate(
        [per_micro(gain_two * shifts_two), per_micro(gain_two * gains_two)], axis=0
    )
    back_sums = near_sum(back_sums)
    mean_g = per_image(back_sums[:MICRO] / count_high, n)
    mean_gy = per_image(back_sums[MICRO:] / count_high, n)
    grad_hidden = (spread_two * (grad_pre_two * gain_two - mean_g - normed_two * mean_gy)).astype(
        bf16
    )
    hidden_all = straight(grad_hidden)
    scaled = inverse.reshape(1, 1)
    hidden_all = straight(grad_hidden)
    small = jnp.concatenate(
        [
            grad_colour[: 9 * PAD],
            jnp.broadcast_to(loss_part[:1, :1], (1, c_out)),
        ],
        axis=0,
    )

    wide = 2 * c_in + 2 * c_out + EMB + conds.shape[1] + 1
    wide = wide + -wide % 128
    extra = small.reshape(-1)
    extra = jnp.pad(extra, (0, -extra.shape[0] % (8 * wide))).reshape(-1, wide)
    *hidden_all, kept, wire, extra = together(*hidden_all, kept, kept.astype(bf16), extra)
    hidden_all = both_cores(hidden_all)
    moment_one, low_one = weight_one_moment(
        where, scaled, hidden_all, ones_all, momentum_first.T
    )
    kept, wire, grad_hidden, _ = together(kept, wire, grad_hidden, low_one)
    one_held = row_gather(low_one)
    shares = near_blocks(kept, wire)
    backs = back_in(row, grad_hidden, weight_one, ranks)
    *one_held, shares[1], shares[2], shares[3], backs = together(
        *one_held, *shares[1:], jnp.stack(backs, axis=0)
    )
    panel = gram_rows(row, one_held, [(0, conv_first.shape[0])])
    kept_one = near_halves(panel.reshape(2, 4, 1, c_out // 8, -1))
    moment_two, moment_skip, low_two = moments_two(
        scaled, [after(shares[0], panel)] + shares[1:], momentum_second.T, momentum_skip.T
    )
    kept_one = after(kept_one, low_two)
    two_held = spread(low_two, ("row",))
    total_one = gram_total(near_blocks(kept_one, kept_one))
    grams_one = row_gather(total_one)
    two_held = after(two_held, *grams_one[1:])
    two_held = [
        lax.dynamic_index_in_dim(two_held, lax.bitwise_xor(row[0], k), 0, keepdims=False)
        for k in range(ranks)
    ]
    spans = [(0, conv_second.shape[0]), (conv_second.shape[0], low_two.shape[1])]
    panels = gram_rows(row, two_held, spans)
    kept_two = near_halves(panels.reshape(2, 4, 1, c_out // 4, -1))
    backs = after(backs, *grams_one[1:])
    inward = lax.all_to_all(in_order(list(backs[:, None]), "row"), "row", 0, 0)
    grams_one = both_cores(grams_one)
    kept_two = after(kept_two, *grams_one)
    terms_two = near_blocks(kept_two, kept_two)
    terms_two[0] = after(terms_two[0], inward)
    total_two = placed_in_order(straight(sum(terms_two)))
    *grams_one, total_two = together(*grams_one, total_two)
    maps_one = newton(where, grams_one, ranks)
    factor = 0.2 * math.sqrt(max(conv_first.shape[0] * groups, c_out * ranks))
    grad_acted_one = jnp.sum(inward.astype(f32), axis=0).reshape(raw.shape)
    grad_pre_one = grad_acted_one * silu_slope(pre_one)
    gains_one = jnp.sum(grad_pre_one * normed_one, axis=(0, 1))
    shifts_one = jnp.sum(grad_pre_one, axis=(0, 1))
    grad_mods_one = jnp.stack([gains_one, shifts_one], axis=1)
    grad_mods_two = jnp.stack([gains_two, shifts_two], axis=1)

    grad_cond = jnp.einsum("bgc,kgc->bk", grad_mods_one, norm_first[:EMB], precision=highest)
    grad_cond = grad_cond + jnp.einsum(
        "bgc,kgc->bk", grad_mods_two, norm_second[:EMB], precision=highest
    )

    grad_cond = jnp.sum(spread(grad_cond, ("row",)), axis=0)
    found = jnp.concatenate(
        [
            grad_mods_one.reshape(n, -1),
            grad_mods_two.reshape(n, -1),
            grad_cond,
            conds,
            labels.astype(f32)[:, None],
        ],
        axis=1,
    )
    found = jnp.pad(found, ((0, 0), (0, -found.shape[1] % 128)))
    packet = jnp.concatenate([found, extra], axis=0)
    packet = spread(after(packet, total_two), GROUP)
    found = packet[:, :n].reshape(-1, wide)
    small = jnp.sum(packet[:, n:], axis=0).reshape(-1)[: small.size].reshape(small.shape)
    loss_sum = small[9 * PAD, 0]
    g_colour = jnp.transpose(small[: 9 * PAD].reshape(9, PAD, c_out)[:, :3], (0, 2, 1))
    cut = 2 * c_in + 2 * c_out + EMB
    found, known = found[:, :cut], found[:, cut : cut + conds.shape[1] + 1]
    conds_all, labels_all = known[:, :-1], known[:, -1].astype(jnp.int32)
    onehot_all = (labels_all[:, None] == jnp.arange(NCLS)[None, :]).astype(f32)
    cut_one, cut_two = 2 * c_in, 2 * c_in + 2 * c_out
    g_norm = lax.dot_general(
        conds_all,
        found[:, :cut_two],
        (((0,), (0,)), ((), ())),
        precision=highest,
        preferred_element_type=f32,
    )
    g_norm_one = g_norm[:, :cut_one].reshape(norm_first.shape)
    g_norm_two = g_norm[:, cut_one:].reshape(norm_second.shape)
    g_table = lax.dot_general(
        onehot_all,
        found[:, cut_two:],
        (((0,), (0,)), ((), ())),
        precision=highest,
        preferred_element_type=f32,
    )

    table_new = adam_update(class_table, g_table * inverse, table_mean, table_square, ADAM_RATE)
    first_new = adam_update(norm_first, g_norm_one * inverse, first_mean, first_square, ADAM_RATE)
    second_new = adam_update(
        norm_second, g_norm_two * inverse, second_mean, second_square, ADAM_RATE
    )
    colour_new = adam_update(
        colour_conv, g_colour * inverse, colour_mean, colour_square, COLOUR_RATE
    )
    grams_two = row_gather(total_two)
    (first_out,) = update(
        row, maps_one, one_held, [conv_first.T], [(0, conv_first.shape[0])], [factor]
    )
    grams_two[0] = after(grams_two[0], first_out)
    maps_two = newton(where, grams_two, ranks)
    other_map = axis_swap(maps_two, "half", 1)
    maps_two = jnp.where(
        half == 0,
        jnp.concatenate([maps_two, other_map], axis=0),
        jnp.concatenate([other_map, maps_two], axis=0),
    )
    factors = [
        0.2 * math.sqrt(max(rows * groups, c_out * ranks))
        for rows in (conv_second.shape[0], conv_skip.shape[0])
    ]
    second_out, skip_out = update(
        row, maps_two, two_held, [conv_second.T, conv_skip.T], spans, factors
    )
    weights_new = (first_out.T, second_out.T, skip_out.T)
    moments_new = (moment_one.T, moment_two.T, moment_skip.T)
    return (
        (loss_sum, fake_count)
        + weights_new
        + moments_new
        + table_new
        + first_new
        + second_new
        + colour_new
    )


def weight_two_grads(row, gpad, twos, raws):
    turned = [jnp.transpose(flat(two)) for two in twos]
    return weight_two(row, gpad, turned, [jnp.transpose(one) for one in raws])


def solution(mesh):
    group = ("half", "dp")
    placed = (
        (P(group, None, None, "row"), P(group, None), P(group), P(group))
        + (P(),) * 5
        + (P(group, "row"),) * 6
        + (P(),) * 3
        + (P(None, None, "row"),) * 6
        + (P(None, "row", None),) * 3
    )
    near = mesh.shape["dp"] == 4 and mesh.shape["half"] == 2 and mesh.shape["row"] == 4
    return jax.shard_map(
        near_device if near else wide_device,
        mesh=mesh,
        in_specs=placed,
        out_specs=(P(), P())
        + (P(group, "row"),) * 6
        + (P(),) * 3
        + (P(None, None, "row"),) * 6
        + (P(None, "row", None),) * 3,
        check_vma=False,
    )
```
